32 devices in a mesh: rep: 2 (over x), dp: 16 (over z, y, core).
Axes of the slice: x: 2, y: 2, z: 4, core: 2. Of those that a mesh axis runs over, the one named last changes fastest.
Arguments:
- tokens: bfloat16 [32, 256, 2048], P(('rep', 'dp')), may hold values from -6 to 6
- cotangent: bfloat16 [32, 256, 2048], P(('rep', 'dp')), may hold values from -6 to 6
- branch: int32 [32, 2], P(('rep', 'dp')), may hold values from 32 to 128, as said below
- att_master: float32 [2048, 8192], P('dp')
- att_first: float32 [2, 2048, 8192], P('rep', 'dp')
- att_second: float32 [2, 2048, 8192], P('rep', 'dp')
- att_outer: float32 [2048, 8192], P('dp'), may hold values from -0.3125 to 0.3125
- mlp_master: float32 [2048, 24576], P('dp')
- mlp_first: float32 [2, 2048, 24576], P('rep', 'dp')
- mlp_second: float32 [2, 2048, 24576], P('rep', 'dp')
- mlp_outer: float32 [2048, 24576], P('dp'), may hold values from -0.3125 to 0.3125
Outputs:
- out_tokens: bfloat16 [32, 256, 2048], P(('rep', 'dp'))
- grad_tokens: float32 [32, 256, 2048], P(('rep', 'dp'))
- att_new: float32 [2048, 8192], P('dp')
- att_first_new: float32 [2, 2048, 8192], P('rep', 'dp')
- att_second_new: float32 [2, 2048, 8192], P('rep', 'dp')
- att_mean_diff: float32 [2048, 8192], P('dp')
- att_outer_new: float32 [2048, 8192], P('dp')
- mlp_new: float32 [2048, 24576], P('dp')
- mlp_first_new: float32 [2, 2048, 24576], P('rep', 'dp')
- mlp_second_new: float32 [2, 2048, 24576], P('rep', 'dp')
- mlp_mean_diff: float32 [2048, 24576], P('dp')
- mlp_outer_new: float32 [2048, 24576], P('dp')
The draws below stay inside these ranges and needn't reach their ends.
Inputs may be any that keep to these rules, and one draw needn't show every extreme that they name: Continuation c of a unit follows the first branch[unit, c] prompt tokens; the value 128 occurs in every draw.
All inputs are finite; a program needn't handle non-finite values.
Results may differ from the reference program's by a relative error of at most 0.015.
Values may be sent and summed in bfloat16 or wider, within the bound.
A program may use at most 960 MiB of HBM per device.

```python
import math
import jax
import jax.numpy as jnp
from jax import lax

D = 2048
FF = 8192
HEADS = 16
HEAD_DIM = 128
PROMPT = 128
CLEN = 64
CONT = 2
STEP = 10
TOK_UNIT = 256
UNITS = 32
REPS = 2
GROUP_TOKENS = 4096
N_REP = 2


def column_scales(first_cols, first_scale, last_cols, last_scale):
    return jnp.concatenate([jnp.full((first_cols,), first_scale, jnp.float32), jnp.full((last_cols,), last_scale, jnp.float32)])


def first_moment(key, shape, scales):
    return jax.random.normal(key, shape, jnp.float32) * (0.1111 * scales)


def second_moment(key, shape, scales):
    spread = jax.random.uniform(key, shape, jnp.float32, 1.0, 4.0)
    return spread * (0.05263 * scales * scales)


def draw_branch(key, part):
    key = jax.random.fold_in(key, 7)
    keys = jax.random.split(key, 2)
    picked = jax.random.randint(keys[0], (UNITS * CONT,), PROMPT // 4, PROMPT + 1)
    spots = jax.random.permutation(keys[1], UNITS * CONT)
    picked = picked.at[spots[0]].set(PROMPT).at[spots[1]].set(PROMPT // 4)
    return picked.reshape(UNITS, CONT).astype(jnp.int32)


def draw_att_master(key, part):
    key = jax.random.fold_in(key, 1)
    scales = column_scales(3 * D, D ** (-0.5), D, 4.0 * D ** (-0.5))
    return jax.random.normal(key, (D, 4 * D), jnp.float32) * scales


def draw_mlp_master(key, part):
    key = jax.random.fold_in(key, 2)
    scales = column_scales(2 * FF, D ** (-0.5), FF, FF ** (-0.5))
    return jax.random.normal(key, (D, 3 * FF), jnp.float32) * scales


def draw_att_first(key, part):
    key = jax.random.fold_in(key, 3)
    root = GROUP_TOKENS ** 0.5
    scales = column_scales(3 * D, 0.4 * root, D, 0.2 * root)
    return first_moment(key, (REPS, D, 4 * D), scales)


def draw_att_second(key, part):
    key = jax.random.fold_in(key, 4)
    root = GROUP_TOKENS ** 0.5
    scales = column_scales(3 * D, 0.4 * root, D, 0.2 * root)
    return second_moment(key, (REPS, D, 4 * D), scales)


def draw_mlp_first(key, part):
    key = jax.random.fold_in(key, 5)
    root = GROUP_TOKENS ** 0.5
    scales = column_scales(2 * FF, 0.3 * root, FF, 0.6 * root)
    return first_moment(key, (REPS, D, 3 * FF), scales)


def draw_mlp_second(key, part):
    key = jax.random.fold_in(key, 6)
    root = GROUP_TOKENS ** 0.5
    scales = column_scales(2 * FF, 0.3 * root, FF, 0.6 * root)
    return second_moment(key, (REPS, D, 3 * FF), scales)


def block_scale(key, shape, shards, low, high):
    level, own = 1.0, jax.random.fold_in(key, 6)
    for axis_at, parts in shards:
        steps = jnp.exp(jax.random.uniform(jax.random.fold_in(own, axis_at), (parts,), jnp.float32, low / len(shards), high / len(shards)))
        level = level * jnp.repeat(steps, shape[axis_at] // parts).reshape([-1 if axis == axis_at else 1 for axis in range(len(shape))])
    return level


def gaussian(rng, dims, deviation, bound, cuts=(), kind=jnp.bfloat16):
    values = jax.random.normal(rng, dims, jnp.float32) * deviation
    if len(cuts) > 0:
        values = block_scale(rng, dims, cuts, -0.22, 0.18) * values
    return jnp.clip(values, min=-bound, max=bound).astype(kind)


def setup_inputs(seed: int = 0) -> dict:
    streams_of = jax.random.split(jax.random.key(seed), 12)
    return {
        "tokens": gaussian(streams_of[0], (UNITS, TOK_UNIT, D), 1.0, 6.0, ((0, 32),)),
        "cotangent": gaussian(streams_of[1], (UNITS, TOK_UNIT, D), 1.0, 6.0, ((0, 32),)),
        "branch": draw_branch(jax.random.fold_in(streams_of[11], 71), 0),
        "att_master": draw_att_master(jax.random.fold_in(streams_of[11], 71), 0),
        "att_first": draw_att_first(jax.random.fold_in(streams_of[11], 71), 0),
        "att_second": draw_att_second(jax.random.fold_in(streams_of[11], 71), 0),
        "att_outer": gaussian(streams_of[6], (D, 4 * D), 0.02, 0.3125, ((0, 16),), jnp.float32),
        "mlp_master": draw_mlp_master(jax.random.fold_in(streams_of[11], 71), 0),
        "mlp_first": draw_mlp_first(jax.random.fold_in(streams_of[11], 71), 0),
        "mlp_second": draw_mlp_second(jax.random.fold_in(streams_of[11], 71), 0),
        "mlp_outer": gaussian(streams_of[10], (D, 3 * FF), 0.02, 0.3125, ((0, 16),), jnp.float32),
    }


@jax.custom_vjp
def low(v):
    return lax.optimization_barrier(v.astype(jnp.bfloat16)).astype(jnp.float32)

@jax.custom_vjp
def low_back(v):
    return v

def low_keep(v):
    return (low(v), None)

def low_pass(kept, grad):
    return (grad,)

def back_keep(v):
    return (v, None)

def back_low(kept, grad):
    return (low(grad),)
low.defvjp(low_keep, low_pass)
low_back.defvjp(back_keep, back_low)
LN_EPS = 1e-05
BETA_ONE = 0.9
BETA_TWO = 0.95
ADAM_EPS = 1e-08
DECAY = 0.1
RATE = 0.05
OUTER_RATE = 0.7
OUTER_MOMENTUM = 0.9
HIGH = lax.Precision.HIGHEST

def rounded_both(values):
    return low(low_back(values))

def layer_norm(values):
    centre = values - lax.optimization_barrier(jnp.mean(values, axis=-1, keepdims=True))
    return centre * lax.rsqrt(lax.optimization_barrier(jnp.mean(centre * centre, axis=-1, keepdims=True)) + LN_EPS)

def token_layout(seen, length):
    places = jnp.arange(length, dtype=jnp.int32)
    segment = jnp.where(places < PROMPT, -1, (places - PROMPT) // CLEN)
    within = jnp.where(places < PROMPT, places, (places - PROMPT) % CLEN)
    lookup = jnp.arange(CONT, dtype=jnp.int32)
    reach = lax.optimization_barrier(jnp.sum(jnp.where(segment[:, None] == lookup[None, :], seen[None, :], 0), axis=1))
    position = jnp.where(segment < 0, places, reach + within)
    allowed = (segment[:, None] == segment[None, :]) & (within[None, :] <= within[:, None]) | (segment[None, :] < 0) & (segment[:, None] >= 0) & (places[None, :] < reach[:, None])
    return (position, allowed)

def rotate(values, position):
    depth = values.shape[-1]
    half_depth = depth // 2
    freqs = jnp.exp(jnp.arange(half_depth, dtype=jnp.float32) * (-2.0 * math.log(10000.0) / depth))
    angle = position.astype(jnp.float32)[:, None] * freqs[None, :]
    cosine = jnp.cos(angle)[:, None, :]
    sine = jnp.sin(angle)[:, None, :]
    first = values[..., :half_depth]
    second = values[..., half_depth:]
    return jnp.concatenate([first * cosine - second * sine, second * cosine + first * sine], axis=-1)

def attend_unit(inputs):
    query_raw, key_raw, value_raw, seen = inputs
    length = query_raw.shape[0]
    position, allowed = token_layout(seen, length)
    query = low(rotate(query_raw, position))
    keys = low(rotate(key_raw, position))
    values = low(value_raw)
    scores = jnp.einsum('qhd,khd->hqk', query, keys, precision=HIGH) * HEAD_DIM ** (-0.5)
    scores = low_back(jnp.where(allowed[None], scores, -1e+30))
    weights = low(jax.nn.softmax(scores, axis=-1))
    mixed = jnp.einsum('hqk,khd->qhd', weights, values, precision=HIGH)
    return rounded_both(mixed).reshape(length, D)

def forward(tokens_f, att_master, mlp_master, branch):
    units, length, width = tokens_f.shape
    flat = tokens_f.reshape(units * length, width)
    att_low = low(att_master)
    mlp_low = low(mlp_master)
    normed_one = low(layer_norm(flat))
    projected = low_back(jnp.dot(normed_one, att_low[:, :3 * width], precision=HIGH))
    projected = projected.reshape(units, length, 3, HEADS, HEAD_DIM)
    mixed = lax.map(jax.checkpoint(attend_unit), (projected[:, :, 0], projected[:, :, 1], projected[:, :, 2], branch))
    mixed = mixed.reshape(units * length, width)
    attended = low_back(jnp.dot(mixed, att_low[:, 3 * width:].T, precision=HIGH))
    resid = flat + attended
    normed_two = low(layer_norm(resid))
    gate_up = low_back(jnp.dot(normed_two, mlp_low[:, :2 * FF], precision=HIGH))
    hidden = low(jax.nn.silu(gate_up[:, :FF]) * gate_up[:, FF:])
    fed = low_back(jnp.dot(hidden, mlp_low[:, 2 * FF:].T, precision=HIGH))
    return (resid + fed).reshape(units, length, width)

def adam_step(master, gradient, first, second):
    first_new = BETA_ONE * first + (1.0 - BETA_ONE) * gradient
    second_new = BETA_TWO * second + (1.0 - BETA_TWO) * gradient * gradient
    ratio = first_new / (1.0 - BETA_ONE ** STEP) / (jnp.sqrt(second_new / (1.0 - BETA_TWO ** STEP)) + ADAM_EPS)
    return (master - RATE * (ratio + DECAY * master), first_new, second_new)

def outer_step(master, mean_diff, momentum):
    momentum_new = OUTER_MOMENTUM * momentum + mean_diff
    return (master - OUTER_RATE * (mean_diff + OUTER_MOMENTUM * momentum_new), momentum_new)

def reference(tokens, cotangent, branch, att_master, att_first, att_second, att_outer, mlp_master, mlp_first, mlp_second, mlp_outer):
    per_group = tokens.shape[0] // N_REP
    outputs = []
    input_grads = []
    att_firsts = []
    att_seconds = []
    mlp_firsts = []
    mlp_seconds = []
    att_diff = jnp.zeros_like(att_master)
    mlp_diff = jnp.zeros_like(mlp_master)
    for group_index in range(N_REP):
        lower = group_index * per_group
        upper = lower + per_group
        group_branch = branch[lower:upper]

        def group_forward(tokens_f, att_weights, mlp_weights):
            return forward(tokens_f, att_weights, mlp_weights, group_branch)
        result, pullback = jax.vjp(group_forward, tokens[lower:upper].astype(jnp.float32), att_master, mlp_master)
        grad_input, att_grad, mlp_grad = pullback(cotangent[lower:upper].astype(jnp.float32))
        outputs.append(result.astype(jnp.bfloat16))
        input_grads.append(grad_input)
        att_inner, att_one, att_two = adam_step(att_master, att_grad, att_first[group_index], att_second[group_index])
        mlp_inner, mlp_one, mlp_two = adam_step(mlp_master, mlp_grad, mlp_first[group_index], mlp_second[group_index])
        att_firsts.append(att_one)
        att_seconds.append(att_two)
        mlp_firsts.append(mlp_one)
        mlp_seconds.append(mlp_two)
        att_diff = att_diff + (att_master - att_inner)
        mlp_diff = mlp_diff + (mlp_master - mlp_inner)
    att_mean = att_diff / N_REP
    mlp_mean = mlp_diff / N_REP
    att_new, att_momentum = outer_step(att_master, att_mean, att_outer)
    mlp_new, mlp_momentum = outer_step(mlp_master, mlp_mean, mlp_outer)
    return (jnp.concatenate(outputs, axis=0), jnp.concatenate(input_grads, axis=0), att_new, jnp.stack(att_firsts), jnp.stack(att_seconds), att_mean, att_momentum, mlp_new, jnp.stack(mlp_firsts), jnp.stack(mlp_seconds), mlp_mean, mlp_momentum)
```

```python
import math

import jax
import jax.numpy as jnp
from jax import lax
from jax.sharding import PartitionSpec as P

HEAD_DIM = 128
PROMPT = 128
CLEN = 64
CONT = 2
STEP = 10
TEAM = 8


LN_EPS = 1e-05
BETA_ONE = 0.9
BETA_TWO = 0.95
ADAM_EPS = 1e-08
DECAY = 0.1
RATE = 0.05
OUTER_RATE = 0.7
OUTER_MOMENTUM = 0.9
CONTRACT_LAST = (((1,), (1,)), ((), ()))
CONTRACT_FIRST = (((0,), (0,)), ((), ()))
LOW = jnp.bfloat16
FULL = jnp.float32


def normalize(values):
    centre = values - jnp.mean(values, axis=-1, keepdims=True)
    factor = lax.rsqrt(jnp.mean(centre * centre, axis=-1, keepdims=True) + LN_EPS)
    return (centre * factor, factor)


def normalize_back(values, gradient):
    normed, factor = normalize(values)
    projection = jnp.mean(gradient * normed, axis=-1, keepdims=True)
    return factor * (gradient - jnp.mean(gradient, axis=-1, keepdims=True) - normed * projection)


def token_layout(seen, length):
    places = jnp.arange(length, dtype=jnp.int32)
    segment = jnp.where(places < PROMPT, -1, (places - PROMPT) // CLEN)
    within = jnp.where(places < PROMPT, places, (places - PROMPT) % CLEN)
    lookup = jnp.arange(CONT, dtype=jnp.int32)
    reach = jnp.sum(jnp.where(segment[:, None] == lookup[None, :], seen[None, :], 0), axis=1)
    position = jnp.where(segment < 0, places, reach + within)
    allowed = (segment[:, None] == segment[None, :]) & (within[None, :] <= within[:, None]) | (
        segment[None, :] < 0
    ) & (segment[:, None] >= 0) & (places[None, :] < reach[:, None])
    return (position, allowed)


def rotary_tables(position, depth):
    half_depth = depth // 2
    freqs = jnp.exp(jnp.arange(half_depth, dtype=jnp.float32) * (-2.0 * math.log(10000.0) / depth))
    angle = position.astype(jnp.float32)[:, None] * freqs[None, :]
    return (jnp.cos(angle)[:, None, :], jnp.sin(angle)[:, None, :])


def rotate(values, cosine, sine):
    half_depth = values.shape[-1] // 2
    first = values[..., :half_depth]
    second = values[..., half_depth:]
    return jnp.concatenate(
        [first * cosine - second * sine, second * cosine + first * sine], axis=-1
    )


def rotate_back(gradient, cosine, sine):
    half_depth = gradient.shape[-1] // 2
    first = gradient[..., :half_depth]
    second = gradient[..., half_depth:]
    return jnp.concatenate(
        [first * cosine + second * sine, second * cosine - first * sine], axis=-1
    )


def adam_step(master, gradient, first, second):
    first_new = BETA_ONE * first + (1.0 - BETA_ONE) * gradient
    second_new = BETA_TWO * second + (1.0 - BETA_TWO) * gradient * gradient
    ratio = (
        first_new
        / (1.0 - BETA_ONE**STEP)
        / (jnp.sqrt(second_new / (1.0 - BETA_TWO**STEP)) + ADAM_EPS)
    )
    return (master - RATE * (ratio + DECAY * master), first_new, second_new)


def outer_step(master, mean_diff, momentum):
    momentum_new = OUTER_MOMENTUM * momentum + mean_diff
    return (master - OUTER_RATE * (mean_diff + OUTER_MOMENTUM * momentum_new), momentum_new)


def dot(left, right, dims=(((1,), (0,)), ((), ()))):
    return lax.dot_general(left, right, dims, preferred_element_type=FULL)


def on_device(
    reps,
    ranks,
    tokens,
    cotangent,
    branch,
    att_master,
    att_first,
    att_second,
    att_outer,
    mlp_master,
    mlp_first,
    mlp_second,
    mlp_outer,
):
    units, length, width = tokens.shape
    hidden_width = mlp_master.shape[1] // 3
    depth = HEAD_DIM
    count = units * length
    rows = att_master.shape[0]
    team = TEAM
    att_share = width // team
    hid_share = hidden_width // team
    me = lax.axis_index("dp")
    rep = lax.axis_index("rep")
    mate = me % team

    def hop(values, other):
        pairs = [(r * ranks + i, r * ranks + (i ^ other)) for r in range(reps) for i in range(ranks)]
        return lax.ppermute(values, ("rep", "dp"), pairs)

    def swap(values):
        pairs = [(r * ranks + i, (1 - r) * ranks + i) for r in range(reps) for i in range(ranks)]
        return lax.ppermute(values, ("rep", "dp"), pairs)

    def team_gather(block):
        half = block.shape[0] // 2
        core = hop(block, 1)
        second = hop(block, 2)
        third = hop(block, 4)
        both = jnp.concatenate([hop(third[:half], 2), hop(second[half:], 4)])
        return jnp.stack(
            [block, core, second, hop(second, 1), third, hop(third, 1), both, hop(both, 1)]
        )

    def team_sum(parts):
        half = parts.shape[1] // 2
        sent = hop(parts[1::2], 1)
        pair = parts[0::2].astype(FULL) + sent.astype(FULL)
        over_second = hop(pair[3, :half].astype(LOW), 2)
        over_third = hop(pair[3, half:].astype(LOW), 4)
        for_third = jnp.concatenate([pair[2, :half] + over_second, pair[2, half:]]).astype(LOW)
        for_second = jnp.concatenate([pair[1, :half], pair[1, half:] + over_third]).astype(LOW)
        return pair[0] + hop(for_second, 2).astype(FULL) + hop(for_third, 4).astype(FULL)

    def share_out(master, bases, share):
        low = master.astype(LOW)
        return jnp.concatenate(
            [
                low[:, base : base + team * share].reshape(rows, team, share).transpose(1, 0, 2)
                for base in bases
            ],
            axis=2,
        )

    def weight_gather(shares):
        total = shares.shape[2]
        result = jnp.zeros((ranks * rows, total), LOW)
        for other in range(ranks):
            block = lax.dynamic_index_in_dim(shares, (me ^ other) % team, 0, keepdims=False)
            start = (me ^ other) * rows
            if other < team or reps != 2:
                part = hop(block, other) if other else block
                result = lax.dynamic_update_slice(result, part, (start, 0))
            else:
                half = rows // 2
                part = hop(lax.dynamic_slice(block, (rep * half, 0), (half, total)), other)
                result = lax.dynamic_update_slice(result, part, (start + rep * half, 0))
                part = swap(part)
                result = lax.dynamic_update_slice(result, part, (start + (1 - rep) * half, 0))
        return result

    def grad_scatter(grad):
        sums = []
        for low_bits in range(team):
            total = None
            for high_bits in range(ranks // team):
                other = high_bits * team + low_bits
                block = lax.dynamic_slice(grad, ((me ^ other) * rows, 0), (rows, grad.shape[1]))
                block = (hop(block, other) if other else block).astype(FULL)
                total = block if total is None else total + block
            sums.append(total)
        return jnp.take(jnp.stack(sums), jnp.arange(team) ^ mate, axis=0)

    def spread(sums, pieces):
        share = sums.shape[2] // pieces
        return [
            sums[:, :, p * share : (p + 1) * share].transpose(1, 0, 2).reshape(rows, team * share)
            for p in range(pieces)
        ]

    flat = tokens.reshape(count, width).astype(FULL)
    grad_fed_own = cotangent.reshape(count, width)
    seen_all = jnp.stack([branch if k == 0 else hop(branch, k) for k in range(team)])
    seen_all = seen_all.reshape(team * units, CONT)
    normed_one = team_gather(normalize(flat)[0].astype(LOW)).reshape(team * count, width)
    att_low = weight_gather(
        share_out(att_master, [0, width, 2 * width, 3 * width], att_share)
    )
    qkv_low, out_low = att_low[:, : 3 * att_share], att_low[:, 3 * att_share :]
    gate_low = weight_gather(share_out(mlp_master, [0, hidden_width], hid_share))
    down_low = weight_gather(share_out(mlp_master, [2 * hidden_width], hid_share))
    grad_fed = team_gather(grad_fed_own).reshape(team * count, width)

    heads = att_share // depth
    position, allowed = jax.vmap(lambda seen: token_layout(seen, length))(seen_all)
    cosine, sine = jax.vmap(lambda places: rotary_tables(places, depth))(position)
    projected = dot(normed_one, qkv_low).reshape(team * units, length, 3, heads, depth)
    query = rotate(projected[:, :, 0], cosine, sine).astype(LOW)
    keys = rotate(projected[:, :, 1], cosine, sine).astype(LOW)
    values = projected[:, :, 2].astype(LOW)
    scale = depth ** (-0.5)

    def ein(spec, left, right):
        return jnp.einsum(spec, left, right, preferred_element_type=FULL)

    scores = jnp.where(allowed[:, None], ein("uqhd,ukhd->uhqk", query, keys) * scale, -1e30)
    highest = jnp.max(scores, axis=-1, keepdims=True)
    powers = jnp.exp(scores - highest)
    prob = powers / jnp.sum(powers, axis=-1, keepdims=True)
    prob_low = prob.astype(LOW)
    mixed = ein("uhqk,ukhd->uqhd", prob_low, values).astype(LOW).reshape(team * count, att_share)
    attended = dot(mixed, out_low, CONTRACT_LAST).astype(LOW).reshape(team, count, width)
    resid = flat + team_sum(attended)
    normed_two = team_gather(normalize(resid)[0].astype(LOW)).reshape(team * count, width)
    gate_up = dot(normed_two, gate_low)
    gate_value = gate_up[:, :hid_share]
    up_value = gate_up[:, hid_share:]
    sigmoid_gate = jax.nn.sigmoid(gate_value)
    silu_gate = gate_value * sigmoid_gate
    hidden = (silu_gate * up_value).astype(LOW)
    down_grad = grad_scatter(dot(grad_fed, hidden, CONTRACT_FIRST).astype(LOW))
    grad_hidden = dot(grad_fed, down_low)
    grad_gate = grad_hidden * up_value * sigmoid_gate * (1.0 + gate_value * (1.0 - sigmoid_gate))
    grad_up = grad_hidden * silu_gate
    grad_gate_up = jnp.concatenate([grad_gate, grad_up], axis=1).astype(LOW)
    gate_grad = grad_scatter(dot(normed_two, grad_gate_up, CONTRACT_FIRST).astype(LOW))
    grad_normed_two = dot(grad_gate_up, gate_low, CONTRACT_LAST).astype(LOW)
    grad_normed_two = team_sum(grad_normed_two.reshape(team, count, width))
    grad_resid = grad_fed_own.astype(FULL) + normalize_back(resid, grad_normed_two)
    grad_attended = team_gather(grad_resid.astype(LOW)).reshape(team * count, width)
    grad_mixed = dot(grad_attended, out_low).astype(LOW)
    out_grad = dot(grad_attended, mixed, CONTRACT_FIRST)
    grad_mixed = grad_mixed.reshape(team * units, length, heads, depth)
    grad_prob = ein("uqhd,ukhd->uhqk", grad_mixed, values)
    grad_values = ein("uhqk,uqhd->ukhd", prob_low, grad_mixed)
    grad_scores = prob * (grad_prob - jnp.sum(grad_prob * prob, axis=-1, keepdims=True))
    grad_scores = grad_scores.astype(LOW)
    grad_query = rotate_back(ein("uhqk,ukhd->uqhd", grad_scores, keys) * scale, cosine, sine)
    grad_keys = rotate_back(ein("uhqk,uqhd->ukhd", grad_scores, query) * scale, cosine, sine)
    grad_projected = jnp.stack([grad_query, grad_keys, grad_values], axis=2).astype(LOW)
    grad_projected = grad_projected.reshape(team * count, 3 * att_share)
    qkv_grad = dot(normed_one, grad_projected, CONTRACT_FIRST)
    att_grad = grad_scatter(jnp.concatenate([qkv_grad, out_grad], axis=1).astype(LOW))
    grad_normed_one = dot(grad_projected, qkv_low, CONTRACT_LAST).astype(LOW)
    grad_normed_one = team_sum(grad_normed_one.reshape(team, count, width))
    grad_tokens = (grad_resid + normalize_back(flat, grad_normed_one)).reshape(units, length, width)
    fed = dot(hidden, down_low, CONTRACT_LAST).astype(LOW)
    fed = team_sum(fed.reshape(team, count, width))
    out_tokens = (resid + fed).astype(LOW).reshape(units, length, width)

    att_full_grad = jnp.concatenate(spread(att_grad, 4), axis=1)
    mlp_full_grad = jnp.concatenate(spread(gate_grad, 2) + spread(down_grad, 1), axis=1)

    def update(master, grad, first, second, outer):
        inner, one, two = adam_step(master, grad, first[0], second[0])
        diff = (master - inner).astype(LOW)
        total = diff.astype(FULL) + swap(diff).astype(FULL)
        mean = total / reps
        new, momentum = outer_step(master, mean, outer)
        return (new, one[None], two[None], mean, momentum)

    return (
        out_tokens,
        grad_tokens,
        *update(att_master, att_full_grad, att_first, att_second, att_outer),
        *update(mlp_master, mlp_full_grad, mlp_first, mlp_second, mlp_outer),
    )


def solution(mesh):
    in_specs = (
        P(("rep", "dp"), None, None),
        P(("rep", "dp"), None, None),
        P(("rep", "dp"), None),
        P("dp", None),
        P("rep", "dp", None),
        P("rep", "dp", None),
        P("dp", None),
        P("dp", None),
        P("rep", "dp", None),
        P("rep", "dp", None),
        P("dp", None),
    )
    out_specs = (
        P(("rep", "dp"), None, None),
        P(("rep", "dp"), None, None),
        P("dp", None),
        P("rep", "dp", None),
        P("rep", "dp", None),
        P("dp", None),
        P("dp", None),
        P("dp", None),
        P("rep", "dp", None),
        P("rep", "dp", None),
        P("dp", None),
        P("dp", None),
    )

    def body(*args):
        return on_device(mesh.shape["rep"], mesh.shape["dp"], *args)

    return jax.shard_map(
        body, mesh=mesh, in_specs=in_specs, out_specs=out_specs, check_vma=False
    )
```

```python
import functools
import math

import jax
import jax.numpy as jnp
from jax import lax
from jax.experimental import pallas as pl
from jax.experimental.pallas import tpu as pltpu
from jax.sharding import PartitionSpec as P

HEAD_DIM = 128
PROMPT = 128
CLEN = 64
CONT = 2
STEP = 10
TEAM = 8


LN_EPS = 1e-05
BETA_ONE = 0.9
BETA_TWO = 0.95
ADAM_EPS = 1e-08
DECAY = 0.1
RATE = 0.05
OUTER_RATE = 0.7
OUTER_MOMENTUM = 0.9
CONTRACT_LAST = (((1,), (1,)), ((), ()))
CONTRACT_FIRST = (((0,), (0,)), ((), ()))
LOW = jnp.bfloat16
FULL = jnp.float32


def normalize(values):
    centre = values - jnp.mean(values, axis=-1, keepdims=True)
    factor = lax.rsqrt(jnp.mean(centre * centre, axis=-1, keepdims=True) + LN_EPS)
    return (centre * factor, factor)


def normalize_back(values, gradient):
    normed, factor = normalize(values)
    projection = jnp.mean(gradient * normed, axis=-1, keepdims=True)
    return factor * (gradient - jnp.mean(gradient, axis=-1, keepdims=True) - normed * projection)


def token_layout(seen, length):
    places = jnp.arange(length, dtype=jnp.int32)
    segment = jnp.where(places < PROMPT, -1, (places - PROMPT) // CLEN)
    within = jnp.where(places < PROMPT, places, (places - PROMPT) % CLEN)
    lookup = jnp.arange(CONT, dtype=jnp.int32)
    reach = jnp.sum(jnp.where(segment[:, None] == lookup[None, :], seen[None, :], 0), axis=1)
    position = jnp.where(segment < 0, places, reach + within)
    allowed = (segment[:, None] == segment[None, :]) & (within[None, :] <= within[:, None]) | (
        segment[None, :] < 0
    ) & (segment[:, None] >= 0) & (places[None, :] < reach[:, None])
    return (position, allowed)


def rotary_tables(position, depth):
    half_depth = depth // 2
    freqs = jnp.exp(jnp.arange(half_depth, dtype=jnp.float32) * (-2.0 * math.log(10000.0) / depth))
    angle = position.astype(jnp.float32)[:, None] * freqs[None, :]
    return (jnp.cos(angle)[:, None, :], jnp.sin(angle)[:, None, :])


def rotate(values, cosine, sine):
    half_depth = values.shape[-1] // 2
    first = values[..., :half_depth]
    second = values[..., half_depth:]
    return jnp.concatenate(
        [first * cosine - second * sine, second * cosine + first * sine], axis=-1
    )


def rotate_back(gradient, cosine, sine):
    half_depth = gradient.shape[-1] // 2
    first = gradient[..., :half_depth]
    second = gradient[..., half_depth:]
    return jnp.concatenate(
        [first * cosine + second * sine, second * cosine - first * sine], axis=-1
    )


def adam_step(master, gradient, first, second):
    first_new = BETA_ONE * first + (1.0 - BETA_ONE) * gradient
    second_new = BETA_TWO * second + (1.0 - BETA_TWO) * gradient * gradient
    ratio = (
        first_new
        / (1.0 - BETA_ONE**STEP)
        / (jnp.sqrt(second_new / (1.0 - BETA_TWO**STEP)) + ADAM_EPS)
    )
    return (master - RATE * (ratio + DECAY * master), first_new, second_new)


def outer_step(master, mean_diff, momentum):
    momentum_new = OUTER_MOMENTUM * momentum + mean_diff
    return (master - OUTER_RATE * (mean_diff + OUTER_MOMENTUM * momentum_new), momentum_new)


def dot(left, right, dims=(((1,), (0,)), ((), ()))):
    return lax.dot_general(left, right, dims, preferred_element_type=FULL)


MESH = pl.DeviceIdType.MESH
ANYWHERE = pl.BlockSpec(memory_space=pl.ANY)
BITS = (1, 2, 4)
PIECES = 4
STRIP = 16
GATHER_COPIES = 6 * PIECES + 1
VMEM_BYTES = 56 * 1024 * 1024


def flip(me, bit):
    return me + bit - 2 * bit * ((me // bit) % 2)


def across(me, other):
    bit = 1
    while bit <= other:
        if other & bit:
            me = flip(me, bit)
        bit *= 2
    return me


def greet(me, others, with_rep):
    barrier = pltpu.get_barrier_semaphore()
    for other in others:
        pl.semaphore_signal(
            barrier, inc=1, device_id={"dp": across(me, other)}, device_id_type=MESH
        )
    if with_rep:
        rep = lax.axis_index("rep")
        pl.semaphore_signal(barrier, inc=1, device_id={"rep": 1 - rep}, device_id_type=MESH)
    pl.semaphore_wait(barrier, len(others) + (1 if with_rep else 0))


class Sender:
    def __init__(self, sent, came):
        self.sent, self.came, self.index = sent, came, 0

    def __call__(self, source, target, where):
        copy = pltpu.make_async_remote_copy(
            src_ref=source,
            dst_ref=target,
            send_sem=self.sent.at[self.index],
            recv_sem=self.came.at[self.index],
            device_id=where,
            device_id_type=MESH,
        )
        copy.start()
        self.index += 1
        return copy


class TeamGather:
    def __init__(self, me, own, out, send):
        self.out, self.send = out, send
        self.piece = own.shape[0] // PIECES
        self.core, self.second, self.third = ({"dp": flip(me, bit)} for bit in BITS)
        self.late = list(range(PIECES // 2, PIECES)) + list(range(PIECES // 2))
        self.early = list(range(PIECES))
        self.own = own
        self.over_second, self.over_third, self.rest = {}, {}, []

    def cut(self, ref, p):
        return ref.at[pl.ds(p * self.piece, self.piece)]

    def begin(self):
        own, out, cut = self.own, self.out, self.cut
        for a, b in zip(self.late, self.early):
            self.over_second[a] = self.send(cut(own, a), cut(out.at[2], a), self.second)
            self.over_third[b] = self.send(cut(own, b), cut(out.at[4], b), self.third)
        self.rest.append(self.send(own, out.at[1], self.core))

    def finish(self):
        out, cut, send = self.out, self.cut, self.send
        half = PIECES // 2
        corner = {}
        for a, b in zip(self.late, self.early):
            self.over_second[a].wait_recv()
            if a >= half:
                corner[a] = send(cut(out.at[2], a), cut(out.at[6], a), self.third)
            self.rest.append(send(cut(out.at[2], a), cut(out.at[3], a), self.core))
            self.over_third[b].wait_recv()
            if b < half:
                corner[b] = send(cut(out.at[4], b), cut(out.at[6], b), self.second)
            self.rest.append(send(cut(out.at[4], b), cut(out.at[5], b), self.core))
        for p in range(half):
            for q in (p, p + half):
                corner[q].wait_recv()
                self.rest.append(send(cut(out.at[6], q), cut(out.at[7], q), self.core))
        for group in (self.over_second, self.over_third, corner):
            for copy in group.values():
                copy.wait_send()
        for copy in self.rest:
            copy.wait()


SUM_COPIES = 8 + 6


def sum_scratch(count, width):
    return [
        pltpu.VMEM((4, count, width), LOW),
        pltpu.VMEM((4, count, width), LOW),
        pltpu.VMEM((4, count, width), LOW),
        pltpu.SemaphoreType.DMA((SUM_COPIES,)),
        pltpu.SemaphoreType.DMA((SUM_COPIES,)),
        pltpu.SemaphoreType.DMA((4,)),
    ]


def team_sum(me, parts, own, got, edge, sent, came, loads, total):
    count = own.shape[1]
    half = count // 2
    send = Sender(sent, came)
    core, second, third = ({"dp": flip(me, bit)} for bit in BITS)

    def cut(ref, h):
        return ref.at[pl.ds(h * half, half)]

    order = [(3, 0), (3, 1), (2, 1), (1, 0), (2, 0), (1, 1), (0, 0), (0, 1)]
    loading = {}
    for j in (3, 2, 1, 0):
        loading[j] = pltpu.make_async_copy(parts.at[2 * j], own.at[j], loads.at[j])
        loading[j].start()
    first = {
        (j, h): send(cut(parts.at[2 * j + 1], h), cut(got.at[j], h), core) for j, h in order
    }
    loaded = set()

    def ready(j, h):
        if j not in loaded:
            loading[j].wait()
            loaded.add(j)
        first[j, h].wait_recv()

    def add(j, h, extra=None):
        @pl.loop(0, half // STRIP)
        def _(step):
            at = pl.ds(h * half + step * STRIP, STRIP)
            value = own[j, at].astype(FULL) + got[j, at].astype(FULL)
            if extra is not None:
                value = value + extra[at].astype(FULL)
            own[j, at] = value.astype(LOW)

    later = []
    ready(3, 0)
    add(3, 0)
    corner_second = send(cut(own.at[3], 0), cut(edge.at[0], 0), second)
    ready(3, 1)
    add(3, 1)
    corner_third = send(cut(own.at[3], 1), cut(edge.at[1], 1), third)
    ready(2, 1)
    add(2, 1)
    third_late = send(cut(own.at[2], 1), cut(edge.at[3], 1), third)
    ready(1, 0)
    add(1, 0)
    second_early = send(cut(own.at[1], 0), cut(edge.at[2], 0), second)
    ready(2, 0)
    corner_second.wait_recv()
    add(2, 0, edge.at[0])
    third_early = send(cut(own.at[2], 0), cut(edge.at[3], 0), third)
    ready(1, 1)
    corner_third.wait_recv()
    add(1, 1, edge.at[1])
    second_late = send(cut(own.at[1], 1), cut(edge.at[2], 1), second)
    for h, waits in ((0, (second_early, third_early)), (1, (third_late, second_late))):
        ready(0, h)
        for copy in waits:
            copy.wait_recv()

        @pl.loop(0, half // STRIP)
        def _(step, h=h):
            start = h * half + step * STRIP
            at = pl.ds(start, STRIP)
            value = own[0, at].astype(FULL) + got[0, at].astype(FULL)
            total(start, value + edge[2, at].astype(FULL) + edge[3, at].astype(FULL))

    for copy in (
        corner_second, corner_third, third_late, second_early, third_early, second_late
    ):
        copy.wait_send()
    for copy in first.values():
        copy.wait_send()


def params(collective_id):
    return pltpu.CompilerParams(
        collective_id=collective_id, has_side_effects=True, vmem_limit_bytes=VMEM_BYTES
    )


def open_kernel(ranks, normed, cot, pack, normed_all, cot_all, weights, *scratch):
    sent, came, sent_two, came_two, sent_w, came_w, sent_x, came_x, local = scratch
    me = lax.axis_index("dp")
    rep = lax.axis_index("rep")
    rows = pack.shape[1]
    half = rows // 2
    greet(me, range(1, ranks), True)
    token_gather = TeamGather(me, normed, normed_all, Sender(sent, came))
    token_gather.begin()
    send_w = Sender(sent_w, came_w)
    order = list(range(TEAM, ranks)) + list(range(1, TEAM))
    mine = pl.ds(me * rows + rep * half, half)
    own = [
        pltpu.make_async_copy(normed, normed_all.at[0], local.at[0]),
        pltpu.make_async_copy(cot, cot_all.at[0], local.at[1]),
        pltpu.make_async_copy(
            pack.at[me % TEAM], weights.at[pl.ds(me * rows, rows)], local.at[2]
        ),
    ]
    for copy in own:
        copy.start()
    ways = []
    for other in order:
        where = across(me, other)
        source = pack.at[where % TEAM, pl.ds(rep * half, half)]
        ways.append(send_w(source, weights.at[mine], {"dp": where}))
    cot_gather = TeamGather(me, cot, cot_all, Sender(sent_two, came_two))
    cot_gather.begin()
    token_gather.finish()
    send_x = Sender(sent_x, came_x)
    swaps = []
    for other, copy in zip(order, ways):
        copy.wait_recv()
        at = weights.at[pl.ds(across(me, other) * rows + rep * half, half)]
        swaps.append(send_x(at, at, {"rep": 1 - rep}))
    cot_gather.finish()
    for copy in ways:
        copy.wait_send()
    for copy in swaps:
        copy.wait()
    for copy in own:
        copy.wait()


def open_layer(ranks, normed, cot, pack):
    count, width = normed.shape
    pairs = [(GATHER_COPIES,)] * 4 + [(ranks - 1,)] * 4
    gathered = jax.ShapeDtypeStruct((TEAM, count, width), LOW)
    return pl.pallas_call(
        functools.partial(open_kernel, ranks),
        out_shape=[
            gathered,
            gathered,
            jax.ShapeDtypeStruct((ranks * pack.shape[1], pack.shape[2]), LOW),
        ],
        in_specs=[ANYWHERE] * 3,
        out_specs=[ANYWHERE] * 3,
        scratch_shapes=[pltpu.SemaphoreType.DMA(shape) for shape in pairs + [(3,)]],
        compiler_params=params(0),
        name="open_layer",
    )(normed, cot, pack)


def strip_normalize(value):
    width = value.shape[1]
    centre = value - jnp.sum(value, axis=1, keepdims=True) * (1.0 / width)
    factor = lax.rsqrt(jnp.sum(centre * centre, axis=1, keepdims=True) * (1.0 / width) + LN_EPS)
    return (centre * factor, factor)


def middle_kernel(ranks, parts, flat, *refs):
    packs, refs = refs[:2], refs[2:]
    crossed, refs = refs[:2], refs[2:]
    resid, normed_all = refs[:2]
    weights, refs = refs[2:4], refs[4:]
    normed, *refs = refs
    sum_refs, refs = refs[:6], refs[6:]
    sent, came, sent_w, came_w, sent_x, came_x, local = refs
    me = lax.axis_index("dp")
    rep = lax.axis_index("rep")
    rows = packs[0].shape[1]
    half = rows // 2
    tops = ranks // TEAM
    greet(me, range(1, TEAM), True)
    send_w = Sender(sent_w, came_w)
    send_x = Sender(sent_x, came_x)
    own = []
    for pack, weight in zip(packs, weights):
        at = weight.at[pl.ds(me * rows, rows)]
        own.append(pltpu.make_async_copy(pack.at[me % TEAM], at, local.at[len(own)]))
        own[-1].start()

    def total(start, value):
        at = pl.ds(start, STRIP)
        value = value + flat[at].astype(FULL)
        resid[at] = value
        normed[at] = strip_normalize(value)[0].astype(LOW)

    team_sum(me, parts, *sum_refs, total)
    gather = TeamGather(me, normed, normed_all, Sender(sent, came))
    gather.begin()
    swaps, ways = [], []
    for which in range(2):
        weight = weights[which]
        for top in range(tops):
            from_rows = across(me, top * TEAM)
            at = pl.ds(from_rows * rows + rep * half, half)
            for other in range(TEAM):
                where = across(me, other)
                if top == 0:
                    source = packs[which].at[where % TEAM, pl.ds(rep * half, half)]
                else:
                    source = crossed[which].at[top - 1, where % TEAM]
                if other:
                    ways.append((which, top, other, send_w(source, weight.at[at], {"dp": where})))
                elif top:
                    own.append(pltpu.make_async_copy(source, weight.at[at], local.at[len(own)]))
                    own[-1].start()
                    swaps.append(send_x(source, weight.at[at], {"rep": 1 - rep}))
    keep = pltpu.make_async_copy(normed, normed_all.at[0], local.at[len(own)])
    keep.start()
    gather.finish()
    for which, top, other, copy in ways:
        copy.wait_recv()
        place = across(across(me, top * TEAM), other) * rows + rep * half
        at = weights[which].at[pl.ds(place, half)]
        swaps.append(send_x(at, at, {"rep": 1 - rep}))
    for _, _, _, copy in ways:
        copy.wait_send()
    for copy in swaps + own + [keep]:
        copy.wait()


def middle_layer(ranks, parts, flat, packs, crossed):
    team, count, width = parts.shape
    tops = ranks // TEAM
    ways = 2 * tops * (TEAM - 1)
    swaps = ways + 2 * (tops - 1)
    pairs = [(GATHER_COPIES,)] * 2 + [(ways,)] * 2 + [(swaps,)] * 2 + [(2 * tops + 1,)]
    vmem = pl.BlockSpec(memory_space=pltpu.VMEM)
    return pl.pallas_call(
        functools.partial(middle_kernel, ranks),
        out_shape=[
            jax.ShapeDtypeStruct((count, width), FULL),
            jax.ShapeDtypeStruct((TEAM, count, width), LOW),
        ]
        + [
            jax.ShapeDtypeStruct((ranks * pack.shape[1], pack.shape[2]), LOW) for pack in packs
        ],
        in_specs=[ANYWHERE, vmem] + [ANYWHERE] * 4,
        out_specs=[vmem] + [ANYWHERE] * 3,
        scratch_shapes=[pltpu.VMEM((count, width), LOW)]
        + sum_scratch(count, width)
        + [pltpu.SemaphoreType.DMA(shape) for shape in pairs],
        compiler_params=params(1),
        name="middle_layer",
    )(parts, flat, *packs, *crossed)


def back_kernel(parts, resid, cot, grad_resid, grad_all, grad_low, *refs):
    sum_refs, (sent, came, local) = refs[:6], refs[6:]
    me = lax.axis_index("dp")
    greet(me, BITS, False)

    def total(start, value):
        at = pl.ds(start, STRIP)
        width = value.shape[1]
        normed, factor = strip_normalize(resid[at])
        along = jnp.sum(value * normed, axis=1, keepdims=True) * (1.0 / width)
        middle = jnp.sum(value, axis=1, keepdims=True) * (1.0 / width)
        value = cot[at].astype(FULL) + factor * (value - middle - normed * along)
        grad_resid[at] = value
        grad_low[at] = value.astype(LOW)

    team_sum(me, parts, *sum_refs, total)
    gather = TeamGather(me, grad_low, grad_all, Sender(sent, came))
    gather.begin()
    keep = pltpu.make_async_copy(grad_low, grad_all.at[0], local)
    keep.start()
    gather.finish()
    keep.wait()


def back_layer(parts, resid, cot):
    team, count, width = parts.shape
    vmem = pl.BlockSpec(memory_space=pltpu.VMEM)
    return pl.pallas_call(
        back_kernel,
        out_shape=[
            jax.ShapeDtypeStruct((count, width), FULL),
            jax.ShapeDtypeStruct((team, count, width), LOW),
        ],
        in_specs=[ANYWHERE, vmem, vmem],
        out_specs=[vmem, ANYWHERE],
        scratch_shapes=[pltpu.VMEM((count, width), LOW)]
        + sum_scratch(count, width)
        + [pltpu.SemaphoreType.DMA((GATHER_COPIES,))] * 2
        + [pltpu.SemaphoreType.DMA],
        compiler_params=params(2),
        name="back_layer",
    )(parts, resid, cot)


def sum_kernel(parts, out, *refs):
    me = lax.axis_index("dp")
    greet(me, BITS, False)

    def total(start, value):
        out[pl.ds(start, STRIP)] = value

    team_sum(me, parts, *refs, total)


def sum_layer(parts, collective_id):
    team, count, width = parts.shape
    return pl.pallas_call(
        sum_kernel,
        out_shape=jax.ShapeDtypeStruct((count, width), FULL),
        in_specs=[ANYWHERE],
        out_specs=pl.BlockSpec(memory_space=pltpu.VMEM),
        scratch_shapes=sum_scratch(count, width),
        compiler_params=params(collective_id),
        name="sum_layer",
    )(parts)


def trade_kernel(blocks, out, sent, came, local):
    me = lax.axis_index("dp")
    greet(me, range(1, TEAM), False)
    send = Sender(sent, came)
    keep = pltpu.make_async_copy(blocks.at[me % TEAM], out.at[me % TEAM], local)
    keep.start()
    copies = []
    for other in (7, 6, 5, 4, 3, 2, 1):
        where = across(me, other)
        copies.append(send(blocks.at[where % TEAM], out.at[me % TEAM], {"dp": where}))
    for copy in copies:
        copy.wait()
    keep.wait()


def trade(blocks, collective_id):
    return pl.pallas_call(
        trade_kernel,
        out_shape=jax.ShapeDtypeStruct(blocks.shape, blocks.dtype),
        in_specs=[ANYWHERE],
        out_specs=ANYWHERE,
        scratch_shapes=[pltpu.SemaphoreType.DMA((TEAM - 1,))] * 2 + [pltpu.SemaphoreType.DMA],
        compiler_params=params(collective_id),
        name="trade",
    )(blocks)


def pack_kernel(*refs):
    share = refs[0].shape[1]
    for p, ref in enumerate(refs[:-1]):
        refs[-1][0, :, p * share : (p + 1) * share] = ref[...].astype(LOW)


def pack_shares(master, bases, share):
    rows = master.shape[0]
    return pl.pallas_call(
        pack_kernel,
        grid=(TEAM,),
        out_shape=jax.ShapeDtypeStruct((TEAM, rows, len(bases) * share), LOW),
        in_specs=[
            pl.BlockSpec((rows, share), lambda i, base=base: (0, base + i)) for base in bases
        ],
        out_specs=pl.BlockSpec((1, rows, len(bases) * share), lambda i: (i, 0, 0)),
        name="pack_shares",
    )(*[master] * len(bases))


def adam_kernel(grad, master, first, second, *refs):
    first_new, second_new, diff = refs[-3:]
    gradient = grad[0].astype(FULL)
    inner, first_new[0], second_new[0] = adam_step(master[...], gradient, first[0], second[0])
    diff[...] = (master[...] - inner).astype(LOW)


def adam_chunk(grads, master, first, second, bases, share, written):
    rows = master.shape[0]
    parts = len(bases)

    def column(t, p):
        place = bases[0]
        for q in range(1, parts):
            place = place + jnp.where(p >= q, bases[q] - bases[q - 1], 0)
        return place + t

    wide = pl.BlockSpec((1, rows, share), lambda t, p: (0, 0, column(t, p)))
    flat = pl.BlockSpec((rows, share), lambda t, p: (0, column(t, p)))
    state = jax.ShapeDtypeStruct(first.shape, FULL)
    extra = [] if written is None else list(written)
    return pl.pallas_call(
        adam_kernel,
        grid=(TEAM, parts),
        out_shape=[state, state, jax.ShapeDtypeStruct((rows, TEAM * parts * share), LOW)],
        in_specs=[pl.BlockSpec((1, rows, share), lambda t, p: (t, 0, p)), flat, wide, wide]
        + [ANYWHERE] * len(extra),
        out_specs=[wide, wide, pl.BlockSpec((rows, share), lambda t, p: (0, p * TEAM + t))],
        input_output_aliases={4 + i: i for i in range(len(extra))},
        name="adam_chunk",
    )(grads, master, first, second, *extra)


def outer_kernel(reps, diff, other, master, momentum, *refs):
    mean_out, new, momentum_new = refs[-3:]
    mean = (diff[...].astype(FULL) + other[...].astype(FULL)) / reps
    mean_out[...] = mean
    new[...], momentum_new[...] = outer_step(master[...], mean, momentum[...])


def outer_chunk(reps, diff, other, master, momentum, bases, share, written):
    rows = master.shape[0]
    parts = len(bases)

    def column(t, p):
        place = bases[0]
        for q in range(1, parts):
            place = place + jnp.where(p >= q, bases[q] - bases[q - 1], 0)
        return place + t

    flat = pl.BlockSpec((rows, share), lambda t, p: (0, column(t, p)))
    packed = pl.BlockSpec((rows, share), lambda t, p: (0, p * TEAM + t))
    extra = [] if written is None else list(written)
    return pl.pallas_call(
        functools.partial(outer_kernel, reps),
        grid=(TEAM, parts),
        out_shape=[jax.ShapeDtypeStruct(master.shape, FULL)] * 3,
        in_specs=[packed, packed, flat, flat] + [ANYWHERE] * len(extra),
        out_specs=[flat] * 3,
        input_output_aliases={4 + i: i for i in range(len(extra))},
        name="outer_chunk",
    )(diff, other, master, momentum, *extra)


def on_device(
    reps,
    ranks,
    tokens,
    cotangent,
    branch,
    att_master,
    att_first,
    att_second,
    att_outer,
    mlp_master,
    mlp_first,
    mlp_second,
    mlp_outer,
):
    units, length, width = tokens.shape
    hidden_width = mlp_master.shape[1] // 3
    depth = HEAD_DIM
    count = units * length
    rows = att_master.shape[0]
    team = TEAM
    tops = ranks // team
    all_tokens = team * count
    att_share = width // team
    hid_share = hidden_width // team
    me = lax.axis_index("dp")
    rep = lax.axis_index("rep")
    top = me // team

    def hop(values, other):
        pairs = [(r * ranks + i, r * ranks + (i ^ other)) for r in range(reps) for i in range(ranks)]
        return lax.ppermute(values, ("rep", "dp"), pairs)

    def swap(values):
        pairs = [(r * ranks + i, (1 - r) * ranks + i) for r in range(reps) for i in range(ranks)]
        return lax.ppermute(values, ("rep", "dp"), pairs)

    def cross(pack):
        half = rows // 2
        mine = lax.dynamic_slice_in_dim(pack, rep * half, half, 1)
        return jnp.stack([hop(mine, other * team) for other in range(1, tops)])

    def combine(grad):
        span = team * rows
        kept = lax.dynamic_slice_in_dim(grad, top * span, span, 0)
        if tops > 1:
            kept = kept.astype(FULL)
        for other in range(1, tops):
            sent = lax.dynamic_slice_in_dim(grad, (top ^ other) * span, span, 0)
            kept = kept + hop(sent, other * team).astype(FULL)
        return kept.astype(LOW).reshape(team, rows, grad.shape[1])

    flat_low = tokens.reshape(count, width)
    flat = flat_low.astype(FULL)
    cot = cotangent.reshape(count, width)
    seen_all = jnp.stack([branch if k == 0 else hop(branch, k) for k in range(team)])
    seen_all = seen_all.reshape(team * units, CONT)
    att_pack = pack_shares(att_master, [0, team, 2 * team, 3 * team], att_share)
    normed_one, grad_fed, att_low = open_layer(ranks, normalize(flat)[0].astype(LOW), cot, att_pack)
    normed_one = normed_one.reshape(all_tokens, width)
    grad_fed = grad_fed.reshape(all_tokens, width)
    packs = [
        pack_shares(mlp_master, [0, team], hid_share),
        pack_shares(mlp_master, [2 * team], hid_share),
    ]
    packs_later, att_low = lax.optimization_barrier((packs, att_low))
    crossed = [cross(pack) for pack in packs_later]
    qkv_low, out_low = att_low[:, : 3 * att_share], att_low[:, 3 * att_share :]

    heads = att_share // depth
    position, allowed = jax.vmap(lambda seen: token_layout(seen, length))(seen_all)
    cosine, sine = jax.vmap(lambda places: rotary_tables(places, depth))(position)
    projected = dot(normed_one, qkv_low).reshape(team * units, length, 3, heads, depth)
    query = rotate(projected[:, :, 0], cosine, sine).astype(LOW)
    keys = rotate(projected[:, :, 1], cosine, sine).astype(LOW)
    values = projected[:, :, 2].astype(LOW)
    scale = depth ** (-0.5)

    def ein(spec, left, right):
        return jnp.einsum(spec, left, right, preferred_element_type=FULL)

    scores = jnp.where(allowed[:, None], ein("uqhd,ukhd->uhqk", query, keys) * scale, -1e30)
    highest = jnp.max(scores, axis=-1, keepdims=True)
    powers = jnp.exp(scores - highest)
    prob = powers / jnp.sum(powers, axis=-1, keepdims=True)
    prob_low = prob.astype(LOW)
    mixed = ein("uhqk,ukhd->uqhd", prob_low, values).astype(LOW).reshape(all_tokens, att_share)
    attended = dot(mixed, out_low, CONTRACT_LAST).astype(LOW).reshape(team, count, width)
    resid, normed_two, gate_low, down_low = middle_layer(ranks, attended, flat_low, packs, crossed)
    normed_two = normed_two.reshape(all_tokens, width)
    gate_up = dot(normed_two, gate_low)
    gate_value = gate_up[:, :hid_share]
    up_value = gate_up[:, hid_share:]
    sigmoid_gate = jax.nn.sigmoid(gate_value)
    silu_gate = gate_value * sigmoid_gate
    hidden = (silu_gate * up_value).astype(LOW)
    down_grad = combine(dot(grad_fed, hidden, CONTRACT_FIRST).astype(LOW))
    grad_hidden = dot(grad_fed, down_low)
    grad_gate = grad_hidden * up_value * sigmoid_gate * (1.0 + gate_value * (1.0 - sigmoid_gate))
    grad_up = grad_hidden * silu_gate
    grad_gate_up = jnp.concatenate([grad_gate, grad_up], axis=1).astype(LOW)
    gate_grad = combine(dot(normed_two, grad_gate_up, CONTRACT_FIRST).astype(LOW))
    grad_normed_two = dot(grad_gate_up, gate_low, CONTRACT_LAST).astype(LOW)
    grad_resid, grad_attended = back_layer(
        grad_normed_two.reshape(team, count, width), resid, cot
    )
    grad_attended = grad_attended.reshape(all_tokens, width)
    grad_mixed = dot(grad_attended, out_low).astype(LOW)
    out_grad = dot(grad_attended, mixed, CONTRACT_FIRST)
    grad_mixed = grad_mixed.reshape(team * units, length, heads, depth)
    grad_prob = ein("uqhd,ukhd->uhqk", grad_mixed, values)
    grad_values = ein("uhqk,uqhd->ukhd", prob_low, grad_mixed)
    grad_scores = prob * (grad_prob - jnp.sum(grad_prob * prob, axis=-1, keepdims=True))
    grad_scores = grad_scores.astype(LOW)
    grad_query = rotate_back(ein("uhqk,ukhd->uqhd", grad_scores, keys) * scale, cosine, sine)
    grad_keys = rotate_back(ein("uhqk,uqhd->ukhd", grad_scores, query) * scale, cosine, sine)
    grad_projected = jnp.stack([grad_query, grad_keys, grad_values], axis=2).astype(LOW)
    grad_projected = grad_projected.reshape(all_tokens, 3 * att_share)
    qkv_grad = dot(normed_one, grad_projected, CONTRACT_FIRST)
    att_grad = combine(jnp.concatenate([qkv_grad, out_grad], axis=1).astype(LOW))
    grad_normed_one = dot(grad_projected, qkv_low, CONTRACT_LAST).astype(LOW)
    grad_normed_one = sum_layer(grad_normed_one.reshape(team, count, width), 3)
    grad_tokens = (grad_resid + normalize_back(flat, grad_normed_one)).reshape(units, length, width)
    fed = dot(hidden, down_low, CONTRACT_LAST).astype(LOW)
    fed = sum_layer(fed.reshape(team, count, width), 3)
    out_tokens = (resid + fed).astype(LOW).reshape(units, length, width)

    mlp_state, mlp_out = None, None
    for grads, bases in ((down_grad, [2 * team]), (gate_grad, [0, team])):
        *mlp_state, diff = adam_chunk(
            trade(grads, 4 if len(bases) == 1 else 5),
            mlp_master, mlp_first, mlp_second, bases, hid_share, mlp_state,
        )
        mlp_out = outer_chunk(
            reps, diff, swap(diff), mlp_master, mlp_outer, bases, hid_share, mlp_out
        )
    bases = [0, team, 2 * team, 3 * team]
    *att_state, diff = adam_chunk(
        trade(att_grad, 4), att_master, att_first, att_second, bases, att_share, None
    )
    att_out = outer_chunk(reps, diff, swap(diff), att_master, att_outer, bases, att_share, None)
    return (
        out_tokens,
        grad_tokens,
        *(att_out[1], *att_state, att_out[0], att_out[2]),
        *(mlp_out[1], *mlp_state, mlp_out[0], mlp_out[2]),
    )


def solution(mesh):
    in_specs = (
        P(("rep", "dp"), None, None),
        P(("rep", "dp"), None, None),
        P(("rep", "dp"), None),
        P("dp", None),
        P("rep", "dp", None),
        P("rep", "dp", None),
        P("dp", None),
        P("dp", None),
        P("rep", "dp", None),
        P("rep", "dp", None),
        P("dp", None),
    )
    out_specs = (
        P(("rep", "dp"), None, None),
        P(("rep", "dp"), None, None),
        P("dp", None),
        P("rep", "dp", None),
        P("rep", "dp", None),
        P("dp", None),
        P("dp", None),
        P("dp", None),
        P("rep", "dp", None),
        P("rep", "dp", None),
        P("dp", None),
        P("dp", None),
    )

    def body(*args):
        return on_device(mesh.shape["rep"], mesh.shape["dp"], *args)

    return jax.shard_map(
        body, mesh=mesh, in_specs=in_specs, out_specs=out_specs, check_vma=False
    )
```

```python
import functools
import math

import jax
import jax.numpy as jnp
from jax import lax
from jax.experimental import pallas as pl
from jax.experimental.pallas import tpu as pltpu
from jax.sharding import PartitionSpec as P

HEAD_DIM = 128
PROMPT = 128
CLEN = 64
CONT = 2
STEP = 10
TEAM = 8


LN_EPS = 1e-05
BETA_ONE = 0.9
BETA_TWO = 0.95
ADAM_EPS = 1e-08
DECAY = 0.1
RATE = 0.05
OUTER_RATE = 0.7
OUTER_MOMENTUM = 0.9
CONTRACT_LAST = (((1,), (1,)), ((), ()))
CONTRACT_FIRST = (((0,), (0,)), ((), ()))
LOW = jnp.bfloat16
FULL = jnp.float32


def normalize(values):
    centre = values - jnp.mean(values, axis=-1, keepdims=True)
    factor = lax.rsqrt(jnp.mean(centre * centre, axis=-1, keepdims=True) + LN_EPS)
    return (centre * factor, factor)


def normalize_back(values, gradient):
    normed, factor = normalize(values)
    projection = jnp.mean(gradient * normed, axis=-1, keepdims=True)
    return factor * (gradient - jnp.mean(gradient, axis=-1, keepdims=True) - normed * projection)


def token_layout(seen, length):
    places = jnp.arange(length, dtype=jnp.int32)
    segment = jnp.where(places < PROMPT, -1, (places - PROMPT) // CLEN)
    within = jnp.where(places < PROMPT, places, (places - PROMPT) % CLEN)
    lookup = jnp.arange(CONT, dtype=jnp.int32)
    reach = jnp.sum(jnp.where(segment[:, None] == lookup[None, :], seen[None, :], 0), axis=1)
    position = jnp.where(segment < 0, places, reach + within)
    allowed = (segment[:, None] == segment[None, :]) & (within[None, :] <= within[:, None]) | (
        segment[None, :] < 0
    ) & (segment[:, None] >= 0) & (places[None, :] < reach[:, None])
    return (position, allowed)


def rotary_tables(position, depth):
    half_depth = depth // 2
    freqs = jnp.exp(jnp.arange(half_depth, dtype=jnp.float32) * (-2.0 * math.log(10000.0) / depth))
    angle = position.astype(jnp.float32)[:, None] * freqs[None, :]
    return (jnp.cos(angle)[:, None, :], jnp.sin(angle)[:, None, :])


def rotate(values, cosine, sine):
    half_depth = values.shape[-1] // 2
    first = values[..., :half_depth]
    second = values[..., half_depth:]
    return jnp.concatenate(
        [first * cosine - second * sine, second * cosine + first * sine], axis=-1
    )


def rotate_back(gradient, cosine, sine):
    half_depth = gradient.shape[-1] // 2
    first = gradient[..., :half_depth]
    second = gradient[..., half_depth:]
    return jnp.concatenate(
        [first * cosine + second * sine, second * cosine - first * sine], axis=-1
    )


def adam_step(master, gradient, first, second):
    first_new = BETA_ONE * first + (1.0 - BETA_ONE) * gradient
    second_new = BETA_TWO * second + (1.0 - BETA_TWO) * gradient * gradient
    ratio = (
        first_new
        / (1.0 - BETA_ONE**STEP)
        / (jnp.sqrt(second_new / (1.0 - BETA_TWO**STEP)) + ADAM_EPS)
    )
    return (master - RATE * (ratio + DECAY * master), first_new, second_new)


def outer_step(master, mean_diff, momentum):
    momentum_new = OUTER_MOMENTUM * momentum + mean_diff
    return (master - OUTER_RATE * (mean_diff + OUTER_MOMENTUM * momentum_new), momentum_new)


def dot(left, right, dims=(((1,), (0,)), ((), ()))):
    return lax.dot_general(left, right, dims, preferred_element_type=FULL)


MESH = pl.DeviceIdType.MESH
ANYWHERE = pl.BlockSpec(memory_space=pl.ANY)
BITS = (1, 2, 4)
PIECES = 4
STRIP = 16
GATHER_COPIES = 6 * PIECES + 1
VMEM_BYTES = 56 * 1024 * 1024


def flip(me, bit):
    return me + bit - 2 * bit * ((me // bit) % 2)


def across(me, other):
    bit = 1
    while bit <= other:
        if other & bit:
            me = flip(me, bit)
        bit *= 2
    return me


def greet(me, others, with_rep):
    barrier = pltpu.get_barrier_semaphore()
    for other in others:
        pl.semaphore_signal(
            barrier, inc=1, device_id={"dp": across(me, other)}, device_id_type=MESH
        )
    if with_rep:
        rep = lax.axis_index("rep")
        pl.semaphore_signal(barrier, inc=1, device_id={"rep": 1 - rep}, device_id_type=MESH)
    pl.semaphore_wait(barrier, len(others) + (1 if with_rep else 0))


class Sender:
    def __init__(self, sent, came):
        self.sent, self.came, self.index = sent, came, 0

    def __call__(self, source, target, where):
        copy = pltpu.make_async_remote_copy(
            src_ref=source,
            dst_ref=target,
            send_sem=self.sent.at[self.index],
            recv_sem=self.came.at[self.index],
            device_id=where,
            device_id_type=MESH,
        )
        copy.start()
        self.index += 1
        return copy


class TeamGather:
    def __init__(self, me, own, out, send):
        self.out, self.send = out, send
        self.piece = own.shape[0] // PIECES
        self.core, self.second, self.third = ({"dp": flip(me, bit)} for bit in BITS)
        self.late = list(range(PIECES // 2, PIECES)) + list(range(PIECES // 2))
        self.early = list(range(PIECES))
        self.own = own
        self.over_second, self.over_third, self.rest = {}, {}, []

    def cut(self, ref, p):
        return ref.at[pl.ds(p * self.piece, self.piece)]

    def begin(self):
        own, out, cut = self.own, self.out, self.cut
        for a, b in zip(self.late, self.early):
            self.over_second[a] = self.send(cut(own, a), cut(out.at[2], a), self.second)
            self.over_third[b] = self.send(cut(own, b), cut(out.at[4], b), self.third)
        self.rest.append(self.send(own, out.at[1], self.core))

    def finish(self):
        out, cut, send = self.out, self.cut, self.send
        half = PIECES // 2
        corner = {}
        for a, b in zip(self.late, self.early):
            self.over_second[a].wait_recv()
            if a >= half:
                corner[a] = send(cut(out.at[2], a), cut(out.at[6], a), self.third)
            self.rest.append(send(cut(out.at[2], a), cut(out.at[3], a), self.core))
            self.over_third[b].wait_recv()
            if b < half:
                corner[b] = send(cut(out.at[4], b), cut(out.at[6], b), self.second)
            self.rest.append(send(cut(out.at[4], b), cut(out.at[5], b), self.core))
        for p in range(half):
            for q in (p, p + half):
                corner[q].wait_recv()
                self.rest.append(send(cut(out.at[6], q), cut(out.at[7], q), self.core))
        for group in (self.over_second, self.over_third, corner):
            for copy in group.values():
                copy.wait_send()
        for copy in self.rest:
            copy.wait()


SUM_COPIES = 6


def sum_scratch(count, width):
    return [
        pltpu.VMEM((4, count, width), LOW),
        pltpu.VMEM((4, count, width), LOW),
        pltpu.VMEM((3, count, width), LOW),
        pltpu.SemaphoreType.DMA((SUM_COPIES + 4,)),
        pltpu.SemaphoreType.DMA((SUM_COPIES + 4,)),
        pltpu.SemaphoreType.DMA((4,)),
    ]


def team_sum(me, parts, own, got, edge, sent, came, loads, total):
    send = Sender(sent, came)
    core = {"dp": flip(me, 1)}
    loading = [pltpu.make_async_copy(parts.at[2 * j], own.at[j], loads.at[j]) for j in range(4)]
    first = {}
    for j in (3, 2, 1, 0):
        loading[j].start()
        first[j] = send(parts.at[2 * j + 1], got.at[j], core)
    for copy in loading:
        copy.wait()
    sum_steps(me, own, got, edge, first, send, total, lambda: None)


def sum_steps(me, own, got, edge, first, send, total, between):
    count = own.shape[1]
    half = count // 2
    _, second, third = ({"dp": flip(me, bit)} for bit in BITS)

    def cut(ref, h):
        return ref.at[pl.ds(h * half, half)]

    def add(j, h, extra=None):
        @pl.loop(0, half // STRIP)
        def _(step):
            at = pl.ds(h * half + step * STRIP, STRIP)
            value = own[j, at].astype(FULL) + got[j, at].astype(FULL)
            if extra is not None:
                value = value + extra[at].astype(FULL)
            own[j, at] = value.astype(LOW)

    first[3].wait_recv()
    add(3, 0)
    corner_second = send(cut(own.at[3], 0), cut(edge.at[0], 0), second)
    add(3, 1)
    corner_third = send(cut(own.at[3], 1), cut(edge.at[0], 1), third)
    first[2].wait_recv()
    add(2, 1)
    third_late = send(cut(own.at[2], 1), cut(edge.at[2], 1), third)
    first[1].wait_recv()
    add(1, 0)
    second_early = send(cut(own.at[1], 0), cut(edge.at[1], 0), second)
    between()
    corner_second.wait_recv()
    add(2, 0, edge.at[0])
    third_early = send(cut(own.at[2], 0), cut(edge.at[2], 0), third)
    corner_third.wait_recv()
    add(1, 1, edge.at[0])
    second_late = send(cut(own.at[1], 1), cut(edge.at[1], 1), second)
    first[0].wait_recv()
    for h, waits in ((0, (second_early, third_early)), (1, (third_late, second_late))):
        for copy in waits:
            copy.wait_recv()

        @pl.loop(0, half // STRIP)
        def _(step, h=h):
            start = h * half + step * STRIP
            at = pl.ds(start, STRIP)
            value = own[0, at].astype(FULL) + got[0, at].astype(FULL)
            total(start, value + edge[1, at].astype(FULL) + edge[2, at].astype(FULL))

    for copy in (
        corner_second, corner_third, third_late, second_early, third_early, second_late
    ):
        copy.wait_send()
    for j in range(4):
        first[j].wait_send()


def params(collective_id):
    return pltpu.CompilerParams(
        collective_id=collective_id, has_side_effects=True, vmem_limit_bytes=VMEM_BYTES
    )


def strip_normalize(value):
    width = value.shape[1]
    centre = value - jnp.sum(value, axis=1, keepdims=True) * (1.0 / width)
    factor = lax.rsqrt(jnp.sum(centre * centre, axis=1, keepdims=True) * (1.0 / width) + LN_EPS)
    return (centre * factor, factor)


class RowGather:
    def __init__(self, ranks, me, rep, weights, send, send_x, local):
        self.me, self.rep, self.weights, self.local = me, rep, weights, local
        self.send, self.send_x = send, send_x
        self.rows = weights.shape[0] // ranks
        self.half = self.rows // 2
        self.order = list(range(TEAM, ranks)) + list(range(1, TEAM))

    def place(self, device):
        return self.weights.at[pl.ds(device * self.rows + self.rep * self.half, self.half)]

    def begin(self, pack):
        me, rep = self.me, self.rep
        at = self.weights.at[pl.ds(me * self.rows, self.rows)]
        self.own = pltpu.make_async_copy(pack.at[me % TEAM], at, self.local)
        self.own.start()
        self.ways = []
        for other in self.order:
            where = across(me, other)
            source = pack.at[where % TEAM, pl.ds(rep * self.half, self.half)]
            self.ways.append(self.send(source, self.place(me), {"dp": where}))

    def forward(self):
        self.swaps = []
        for other, copy in zip(self.order, self.ways):
            copy.wait_recv()
            at = self.place(across(self.me, other))
            self.swaps.append(self.send_x(at, at, {"rep": 1 - self.rep}))

    def finish(self):
        for copy in self.ways:
            copy.wait_send()
        for copy in self.swaps + [self.own]:
            copy.wait()


def attend_unit(values, cosine, sine, bias, share):
    depth = HEAD_DIM
    parts = []
    for p in range(2):
        turned = []
        for at in range(p * share, (p + 1) * share, depth):
            head = values[:, at : at + depth]
            turned.append((head * cosine + pltpu.roll(head, depth // 2, 1) * sine).astype(LOW))
        parts.append(turned)
    query, keys = parts
    value = [
        values[:, at : at + depth].astype(LOW) for at in range(2 * share, 3 * share, depth)
    ]
    mixed = []
    for one, two, three in zip(query, keys, value):
        scores = dot(one, two, CONTRACT_LAST) * depth ** (-0.5) + bias
        powers = jnp.exp(scores - jnp.max(scores, axis=1, keepdims=True))
        prob = powers / jnp.sum(powers, axis=1, keepdims=True)
        mixed.append(dot(prob.astype(LOW), three).astype(LOW))
    return jnp.concatenate(query + keys + value, axis=1), jnp.concatenate(mixed, axis=1)


def forward_kernel(
    ranks,
    flat,
    normed_own,
    cot,
    att_pack,
    mlp_master,
    cosine,
    sine,
    bias,
    normed_all,
    cot_all,
    att_weights,
    gate_weights,
    down_weights,
    gate_pack,
    down_pack,
    projected_all,
    mixed_all,
    resid,
    normed_two_all,
    gate_all,
    up_all,
    hidden_all,
    att,
    gate,
    block,
    odd,
    own,
    got,
    edge,
    normed,
    *sems,
):
    sent_team, came_team, sent_rows, came_rows, sent_x, came_x, first_sent, first_came, local = sems
    me = lax.axis_index("dp")
    rep = lax.axis_index("rep")
    rows, share = att_pack.shape[1], att_pack.shape[2] // 4
    hid = gate_pack.shape[2] // 2
    core = {"dp": flip(me, 1)}
    greet(me, range(1, ranks), True)
    send = Sender(sent_team, came_team)
    send_rows = Sender(sent_rows, came_rows)
    send_x = Sender(sent_x, came_x)
    tokens = TeamGather(me, normed_own, normed_all, send)
    tokens.begin()
    gathers = [
        RowGather(ranks, me, rep, weights, send_rows, send_x, local.at[i])
        for i, weights in enumerate((att_weights, gate_weights, down_weights))
    ]
    gathers[0].begin(att_pack)
    keep = [pltpu.make_async_copy(normed_own, normed_all.at[0], local.at[3])]
    keep.append(pltpu.make_async_copy(cot, cot_all.at[0], local.at[4]))
    for copy in keep:
        copy.start()

    def pack(wide, low):
        def loads(t, slot):
            return [
                pltpu.make_async_copy(
                    mlp_master.at[:, pl.ds((p * TEAM + t) * hid, hid)],
                    wide.at[slot, p],
                    local.at[5 + 3 * slot + p],
                )
                for p in range(3)
            ]

        for copy in loads(0, 0):
            copy.start()

        @pl.loop(0, TEAM)
        def _(t):
            slot = t % 2

            @pl.when(t + 1 < TEAM)
            def _():
                for copy in loads(t + 1, 1 - slot):
                    copy.start()

            for copy in loads(t, slot):
                copy.wait()
            low[:, : 2 * hid] = jnp.concatenate(
                [wide[slot, 0].astype(LOW), wide[slot, 1].astype(LOW)], axis=1
            )
            low[:, 2 * hid :] = wide[slot, 2].astype(LOW)
            out_copies = [
                pltpu.make_async_copy(low.at[:, pl.ds(0, 2 * hid)], gate_pack.at[t], local.at[11]),
                pltpu.make_async_copy(low.at[:, pl.ds(2 * hid, hid)], down_pack.at[t], local.at[12]),
            ]
            for copy in out_copies:
                copy.start()
            for copy in out_copies:
                copy.wait()

    pl.run_scoped(
        pack, pltpu.VMEM((2, 3, rows, hid), FULL), pltpu.VMEM((rows, 3 * hid), LOW)
    )
    tokens.finish()
    gathers[1].begin(gate_pack)
    gathers[0].forward()
    gathers[0].finish()
    for copy in keep:
        copy.wait()
    load = pltpu.make_async_copy(att_weights, att, local.at[0])
    load.start()
    load.wait()

    def unit_of(step):
        return 2 * (TEAM // 2 - 1 - step % (TEAM // 2)) + jnp.where(step < TEAM // 2, 1, 0)

    def fetch(step, slot):
        return pltpu.make_async_copy(
            normed_all.at[unit_of(step)], block.at[slot], local.at[5 + slot]
        )

    fetch(0, 0).start()

    @pl.loop(0, TEAM)
    def _(step):
        slot = step % 2
        unit = unit_of(step)

        @pl.when(step + 1 < TEAM)
        def _():
            fetch(step + 1, 1 - slot).start()

        fetch(step, slot).wait()
        values = dot(block[slot], att[:, : 3 * share])
        projected, mixed = attend_unit(values, cosine[unit], sine[unit], bias[unit], share)
        projected_all[unit] = projected
        mixed_all[unit] = mixed
        term = dot(mixed, att[:, 3 * share :], CONTRACT_LAST).astype(LOW)
        j = unit // 2

        @pl.when(step < TEAM // 2)
        def _():
            odd[j] = term
            pltpu.make_async_remote_copy(
                src_ref=odd.at[j],
                dst_ref=got.at[j],
                send_sem=first_sent.at[j],
                recv_sem=first_came.at[j],
                device_id=core,
                device_id_type=MESH,
            ).start()

        @pl.when(step >= TEAM // 2)
        def _():
            own[j] = term

    first = [
        pltpu.make_async_remote_copy(
            src_ref=odd.at[j],
            dst_ref=got.at[j],
            send_sem=first_sent.at[j],
            recv_sem=first_came.at[j],
            device_id=core,
            device_id_type=MESH,
        )
        for j in range(TEAM // 2)
    ]

    def total(start, value):
        at = pl.ds(start, STRIP)
        value = value + flat[at].astype(FULL)
        resid[at] = value
        normed[at] = strip_normalize(value)[0].astype(LOW)

    sum_steps(me, own, got, edge, first, send, total, gathers[1].forward)
    tokens = TeamGather(me, normed, normed_two_all, send)
    tokens.begin()
    keep = pltpu.make_async_copy(normed, normed_two_all.at[0], local.at[3])
    keep.start()
    tokens.finish()
    cots = TeamGather(me, cot, cot_all, send)
    cots.begin()
    gathers[2].begin(down_pack)
    keep.wait()
    gathers[1].finish()
    load = pltpu.make_async_copy(gate_weights, gate, local.at[1])
    load.start()
    load.wait()

    def feed(low):
        def fetch(unit, slot):
            return pltpu.make_async_copy(
                normed_two_all.at[unit], block.at[slot], local.at[5 + slot]
            )

        def stores(unit, slot):
            return [
                pltpu.make_async_copy(low.at[slot, i], out.at[unit], local.at[7 + 3 * slot + i])
                for i, out in enumerate((gate_all, up_all, hidden_all))
            ]

        fetch(0, 0).start()

        @pl.loop(0, TEAM)
        def _(unit):
            slot = unit % 2

            @pl.when(unit + 1 < TEAM)
            def _():
                fetch(unit + 1, 1 - slot).start()

            fetch(unit, slot).wait()

            @pl.when(unit >= 2)
            def _():
                for copy in stores(unit - 2, slot):
                    copy.wait()

            tile = 256

            @pl.loop(0, hid // tile)
            def _(column):
                at = pl.ds(pl.multiple_of(column * tile, tile), tile)
                later = pl.ds(pl.multiple_of(hid + column * tile, tile), tile)
                gate_value = dot(block[slot], gate[:, at])
                up_value = dot(block[slot], gate[:, later])
                low[slot, 0, :, at] = gate_value.astype(LOW)
                low[slot, 1, :, at] = up_value.astype(LOW)
                hidden = gate_value * jax.nn.sigmoid(gate_value) * up_value
                low[slot, 2, :, at] = hidden.astype(LOW)

            for copy in stores(unit, slot):
                copy.start()

        for unit in (TEAM - 2, TEAM - 1):
            for copy in stores(unit, unit % 2):
                copy.wait()

    pl.run_scoped(feed, pltpu.VMEM((2, 3, normed.shape[0], hid), LOW))
    cots.finish()
    gathers[2].forward()
    gathers[2].finish()


def forward_layer(ranks, flat, normed, cot, att_pack, mlp_master, cosine, sine, bias):
    count, width = normed.shape
    rows, share = att_pack.shape[1], att_pack.shape[2] // 4
    hid = mlp_master.shape[1] // (3 * TEAM)
    gathered = jax.ShapeDtypeStruct((TEAM, count, width), LOW)
    hidden = jax.ShapeDtypeStruct((TEAM, count, hid), LOW)
    vmem = pl.BlockSpec(memory_space=pltpu.VMEM)

    def weights(columns):
        return jax.ShapeDtypeStruct((ranks * rows, columns), LOW)

    def packs(columns):
        return jax.ShapeDtypeStruct((TEAM, rows, columns), LOW)

    out = [
        (gathered, ANYWHERE),
        (gathered, ANYWHERE),
        (weights(4 * share), ANYWHERE),
        (weights(2 * hid), ANYWHERE),
        (weights(hid), ANYWHERE),
        (packs(2 * hid), ANYWHERE),
        (packs(hid), ANYWHERE),
        (jax.ShapeDtypeStruct((TEAM, count, 3 * share), LOW), vmem),
        (jax.ShapeDtypeStruct((TEAM, count, share), LOW), vmem),
        (jax.ShapeDtypeStruct((count, width), FULL), vmem),
        (gathered, ANYWHERE),
        (hidden, ANYWHERE),
        (hidden, ANYWHERE),
        (hidden, ANYWHERE),
    ]
    team_copies = 3 * GATHER_COPIES + SUM_COPIES
    pairs = [team_copies] * 2 + [3 * (ranks - 1)] * 4 + [TEAM // 2] * 2 + [13]
    return pl.pallas_call(
        functools.partial(forward_kernel, ranks),
        out_shape=[shape for shape, _ in out],
        in_specs=[vmem] + [ANYWHERE] * 4 + [vmem] * 3,
        out_specs=[spec for _, spec in out],
        scratch_shapes=[
            pltpu.VMEM((ranks * rows, 4 * share), LOW),
            pltpu.VMEM((ranks * rows, 2 * hid), LOW),
            pltpu.VMEM((2, count, width), LOW),
            pltpu.VMEM((TEAM // 2, count, width), LOW),
            pltpu.VMEM((TEAM // 2, count, width), LOW),
            pltpu.VMEM((TEAM // 2, count, width), LOW),
            pltpu.VMEM((3, count, width), LOW),
            pltpu.VMEM((count, width), LOW),
        ]
        + [pltpu.SemaphoreType.DMA((number,)) for number in pairs],
        compiler_params=params(0),
        name="forward_layer",
    )(flat, normed, cot, att_pack, mlp_master, cosine, sine, bias)


def back_kernel(parts, resid, cot, grad_resid, grad_all, grad_low, *refs):
    sum_refs, (sent, came, local) = refs[:6], refs[6:]
    me = lax.axis_index("dp")
    greet(me, BITS, False)

    def total(start, value):
        at = pl.ds(start, STRIP)
        width = value.shape[1]
        normed, factor = strip_normalize(resid[at])
        along = jnp.sum(value * normed, axis=1, keepdims=True) * (1.0 / width)
        middle = jnp.sum(value, axis=1, keepdims=True) * (1.0 / width)
        value = cot[at].astype(FULL) + factor * (value - middle - normed * along)
        grad_resid[at] = value
        grad_low[at] = value.astype(LOW)

    team_sum(me, parts, *sum_refs, total)
    gather = TeamGather(me, grad_low, grad_all, Sender(sent, came))
    gather.begin()
    keep = pltpu.make_async_copy(grad_low, grad_all.at[0], local)
    keep.start()
    gather.finish()
    keep.wait()


def back_layer(parts, resid, cot):
    team, count, width = parts.shape
    vmem = pl.BlockSpec(memory_space=pltpu.VMEM)
    return pl.pallas_call(
        back_kernel,
        out_shape=[
            jax.ShapeDtypeStruct((count, width), FULL),
            jax.ShapeDtypeStruct((team, count, width), LOW),
        ],
        in_specs=[ANYWHERE, vmem, vmem],
        out_specs=[vmem, ANYWHERE],
        scratch_shapes=[pltpu.VMEM((count, width), LOW)]
        + sum_scratch(count, width)
        + [pltpu.SemaphoreType.DMA((GATHER_COPIES,))] * 2
        + [pltpu.SemaphoreType.DMA],
        compiler_params=params(2),
        name="back_layer",
    )(parts, resid, cot)


def sum_kernel(parts, out, *refs):
    me = lax.axis_index("dp")
    greet(me, BITS, False)

    def total(start, value):
        out[pl.ds(start, STRIP)] = value

    team_sum(me, parts, *refs, total)


def sum_layer(parts, collective_id):
    team, count, width = parts.shape
    return pl.pallas_call(
        sum_kernel,
        out_shape=jax.ShapeDtypeStruct((count, width), FULL),
        in_specs=[ANYWHERE],
        out_specs=pl.BlockSpec(memory_space=pltpu.VMEM),
        scratch_shapes=sum_scratch(count, width),
        compiler_params=params(collective_id),
        name="sum_layer",
    )(parts)


def trade_kernel(blocks, out, sent, came, local):
    me = lax.axis_index("dp")
    greet(me, range(1, TEAM), False)
    send = Sender(sent, came)
    keep = pltpu.make_async_copy(blocks.at[me % TEAM], out.at[me % TEAM], local)
    keep.start()
    copies = []
    for other in (7, 6, 5, 4, 3, 2, 1):
        where = across(me, other)
        copies.append(send(blocks.at[where % TEAM], out.at[me % TEAM], {"dp": where}))
    for copy in copies:
        copy.wait()
    keep.wait()


def trade(blocks, collective_id):
    return pl.pallas_call(
        trade_kernel,
        out_shape=jax.ShapeDtypeStruct(blocks.shape, blocks.dtype),
        in_specs=[ANYWHERE],
        out_specs=ANYWHERE,
        scratch_shapes=[pltpu.SemaphoreType.DMA((TEAM - 1,))] * 2 + [pltpu.SemaphoreType.DMA],
        compiler_params=params(collective_id),
        name="trade",
    )(blocks)


def pack_kernel(*refs):
    share = refs[0].shape[1]
    for p, ref in enumerate(refs[:-1]):
        refs[-1][0, :, p * share : (p + 1) * share] = ref[...].astype(LOW)


def pack_shares(master, bases, share):
    rows = master.shape[0]
    return pl.pallas_call(
        pack_kernel,
        grid=(TEAM,),
        out_shape=jax.ShapeDtypeStruct((TEAM, rows, len(bases) * share), LOW),
        in_specs=[
            pl.BlockSpec((rows, share), lambda i, base=base: (0, base + i)) for base in bases
        ],
        out_specs=pl.BlockSpec((1, rows, len(bases) * share), lambda i: (i, 0, 0)),
        name="pack_shares",
    )(*[master] * len(bases))


def adam_kernel(grad, master, first, second, *refs):
    first_new, second_new, diff = refs[-3:]
    gradient = grad[0].astype(FULL)
    inner, first_new[0], second_new[0] = adam_step(master[...], gradient, first[0], second[0])
    diff[...] = (master[...] - inner).astype(LOW)


def adam_chunk(grads, master, first, second, bases, share, written):
    rows = master.shape[0]
    parts = len(bases)

    def column(t, p):
        place = bases[0]
        for q in range(1, parts):
            place = place + jnp.where(p >= q, bases[q] - bases[q - 1], 0)
        return place + t

    wide = pl.BlockSpec((1, rows, share), lambda t, p: (0, 0, column(t, p)))
    flat = pl.BlockSpec((rows, share), lambda t, p: (0, column(t, p)))
    state = jax.ShapeDtypeStruct(first.shape, FULL)
    extra = [] if written is None else list(written)
    return pl.pallas_call(
        adam_kernel,
        grid=(TEAM, parts),
        out_shape=[state, state, jax.ShapeDtypeStruct((rows, TEAM * parts * share), LOW)],
        in_specs=[pl.BlockSpec((1, rows, share), lambda t, p: (t, 0, p)), flat, wide, wide]
        + [ANYWHERE] * len(extra),
        out_specs=[wide, wide, pl.BlockSpec((rows, share), lambda t, p: (0, p * TEAM + t))],
        input_output_aliases={4 + i: i for i in range(len(extra))},
        name="adam_chunk",
    )(grads, master, first, second, *extra)


def outer_kernel(reps, diff, other, master, momentum, *refs):
    mean_out, new, momentum_new = refs[-3:]
    mean = (diff[...].astype(FULL) + other[...].astype(FULL)) / reps
    mean_out[...] = mean
    new[...], momentum_new[...] = outer_step(master[...], mean, momentum[...])


def outer_chunk(reps, diff, other, master, momentum, bases, share, written):
    rows = master.shape[0]
    parts = len(bases)

    def column(t, p):
        place = bases[0]
        for q in range(1, parts):
            place = place + jnp.where(p >= q, bases[q] - bases[q - 1], 0)
        return place + t

    flat = pl.BlockSpec((rows, share), lambda t, p: (0, column(t, p)))
    packed = pl.BlockSpec((rows, share), lambda t, p: (0, p * TEAM + t))
    extra = [] if written is None else list(written)
    return pl.pallas_call(
        functools.partial(outer_kernel, reps),
        grid=(TEAM, parts),
        out_shape=[jax.ShapeDtypeStruct(master.shape, FULL)] * 3,
        in_specs=[packed, packed, flat, flat] + [ANYWHERE] * len(extra),
        out_specs=[flat] * 3,
        input_output_aliases={4 + i: i for i in range(len(extra))},
        name="outer_chunk",
    )(diff, other, master, momentum, *extra)


def on_device(
    reps,
    ranks,
    tokens,
    cotangent,
    branch,
    att_master,
    att_first,
    att_second,
    att_outer,
    mlp_master,
    mlp_first,
    mlp_second,
    mlp_outer,
):
    units, length, width = tokens.shape
    hidden_width = mlp_master.shape[1] // 3
    depth = HEAD_DIM
    count = units * length
    rows = att_master.shape[0]
    team = TEAM
    tops = ranks // team
    all_tokens = team * count
    att_share = width // team
    hid_share = hidden_width // team
    me = lax.axis_index("dp")
    rep = lax.axis_index("rep")
    top = me // team

    def hop(values, other):
        pairs = [(r * ranks + i, r * ranks + (i ^ other)) for r in range(reps) for i in range(ranks)]
        return lax.ppermute(values, ("rep", "dp"), pairs)

    def swap(values):
        pairs = [(r * ranks + i, (1 - r) * ranks + i) for r in range(reps) for i in range(ranks)]
        return lax.ppermute(values, ("rep", "dp"), pairs)

    def combine(grad):
        span = team * rows
        kept = lax.dynamic_slice_in_dim(grad, top * span, span, 0)
        if tops > 1:
            kept = kept.astype(FULL)
        for other in range(1, tops):
            sent = lax.dynamic_slice_in_dim(grad, (top ^ other) * span, span, 0)
            kept = kept + hop(sent, other * team).astype(FULL)
        return kept.astype(LOW).reshape(team, rows, grad.shape[1])

    flat_low = tokens.reshape(count, width)
    flat = flat_low.astype(FULL)
    cot = cotangent.reshape(count, width)
    seen_all = jnp.stack([branch if k == 0 else hop(branch, k) for k in range(team)])
    seen_all = seen_all.reshape(team * units, CONT)
    heads = att_share // depth
    position, allowed = jax.vmap(lambda seen: token_layout(seen, length))(seen_all)
    cosine, sine = jax.vmap(lambda places: rotary_tables(places, depth))(position)
    scale = depth ** (-0.5)
    bias = jnp.where(allowed, 0.0, -1e30).astype(FULL)
    wide_cosine = jnp.concatenate([cosine, cosine], axis=-1).reshape(team, count, depth)
    wide_sine = jnp.concatenate([-sine, sine], axis=-1).reshape(team, count, depth)
    att_pack = pack_shares(att_master, [0, team, 2 * team, 3 * team], att_share)
    (
        normed_one,
        grad_fed,
        att_low,
        gate_low,
        down_low,
        _,
        _,
        projected,
        mixed,
        resid,
        normed_two,
        gate_value,
        up_value,
        hidden,
    ) = forward_layer(
        ranks,
        flat_low,
        normalize(flat)[0].astype(LOW),
        cot,
        att_pack,
        mlp_master,
        wide_cosine,
        wide_sine,
        bias,
    )
    normed_one = normed_one.reshape(all_tokens, width)
    grad_fed = grad_fed.reshape(all_tokens, width)
    mixed = mixed.reshape(all_tokens, att_share)
    normed_two = normed_two.reshape(all_tokens, width)
    gate_value = gate_value.reshape(all_tokens, hid_share).astype(FULL)
    up_value = up_value.reshape(all_tokens, hid_share).astype(FULL)
    hidden = hidden.reshape(all_tokens, hid_share)
    qkv_low, out_low = att_low[:, : 3 * att_share], att_low[:, 3 * att_share :]
    projected = projected.reshape(team * units, length, 3, heads, depth)
    query, keys, values = projected[:, :, 0], projected[:, :, 1], projected[:, :, 2]

    def ein(spec, left, right):
        return jnp.einsum(spec, left, right, preferred_element_type=FULL)

    scores = ein("uqhd,ukhd->uhqk", query, keys) * scale + bias[:, None]
    powers = jnp.exp(scores - jnp.max(scores, axis=-1, keepdims=True))
    prob = powers / jnp.sum(powers, axis=-1, keepdims=True)
    prob_low = prob.astype(LOW)
    sigmoid_gate = jax.nn.sigmoid(gate_value)
    silu_gate = gate_value * sigmoid_gate
    down_grad = combine(dot(grad_fed, hidden, CONTRACT_FIRST).astype(LOW))
    grad_hidden = dot(grad_fed, down_low)
    grad_gate = grad_hidden * up_value * sigmoid_gate * (1.0 + gate_value * (1.0 - sigmoid_gate))
    grad_up = grad_hidden * silu_gate
    grad_gate_up = jnp.concatenate([grad_gate, grad_up], axis=1).astype(LOW)
    gate_grad = combine(dot(normed_two, grad_gate_up, CONTRACT_FIRST).astype(LOW))
    grad_normed_two = dot(grad_gate_up, gate_low, CONTRACT_LAST).astype(LOW)
    grad_resid, grad_attended = back_layer(
        grad_normed_two.reshape(team, count, width), resid, cot
    )
    grad_attended = grad_attended.reshape(all_tokens, width)
    grad_mixed = dot(grad_attended, out_low).astype(LOW)
    out_grad = dot(grad_attended, mixed, CONTRACT_FIRST)
    grad_mixed = grad_mixed.reshape(team * units, length, heads, depth)
    grad_prob = ein("uqhd,ukhd->uhqk", grad_mixed, values)
    grad_values = ein("uhqk,uqhd->ukhd", prob_low, grad_mixed)
    grad_scores = prob * (grad_prob - jnp.sum(grad_prob * prob, axis=-1, keepdims=True))
    grad_scores = grad_scores.astype(LOW)
    grad_query = rotate_back(ein("uhqk,ukhd->uqhd", grad_scores, keys) * scale, cosine, sine)
    grad_keys = rotate_back(ein("uhqk,uqhd->ukhd", grad_scores, query) * scale, cosine, sine)
    grad_projected = jnp.stack([grad_query, grad_keys, grad_values], axis=2).astype(LOW)
    grad_projected = grad_projected.reshape(all_tokens, 3 * att_share)
    qkv_grad = dot(normed_one, grad_projected, CONTRACT_FIRST)
    att_grad = combine(jnp.concatenate([qkv_grad, out_grad], axis=1).astype(LOW))
    grad_normed_one = dot(grad_projected, qkv_low, CONTRACT_LAST).astype(LOW)
    grad_normed_one = sum_layer(grad_normed_one.reshape(team, count, width), 3)
    grad_tokens = (grad_resid + normalize_back(flat, grad_normed_one)).reshape(units, length, width)
    fed = dot(hidden, down_low, CONTRACT_LAST).astype(LOW)
    fed = sum_layer(fed.reshape(team, count, width), 3)
    out_tokens = (resid + fed).astype(LOW).reshape(units, length, width)

    mlp_state, mlp_out = None, None
    for grads, bases in ((down_grad, [2 * team]), (gate_grad, [0, team])):
        *mlp_state, diff = adam_chunk(
            trade(grads, 4 if len(bases) == 1 else 5),
            mlp_master, mlp_first, mlp_second, bases, hid_share, mlp_state,
        )
        mlp_out = outer_chunk(
            reps, diff, swap(diff), mlp_master, mlp_outer, bases, hid_share, mlp_out
        )
    bases = [0, team, 2 * team, 3 * team]
    *att_state, diff = adam_chunk(
        trade(att_grad, 4), att_master, att_first, att_second, bases, att_share, None
    )
    att_out = outer_chunk(reps, diff, swap(diff), att_master, att_outer, bases, att_share, None)
    return (
        out_tokens,
        grad_tokens,
        *(att_out[1], *att_state, att_out[0], att_out[2]),
        *(mlp_out[1], *mlp_state, mlp_out[0], mlp_out[2]),
    )


def solution(mesh):
    in_specs = (
        P(("rep", "dp"), None, None),
        P(("rep", "dp"), None, None),
        P(("rep", "dp"), None),
        P("dp", None),
        P("rep", "dp", None),
        P("rep", "dp", None),
        P("dp", None),
        P("dp", None),
        P("rep", "dp", None),
        P("rep", "dp", None),
        P("dp", None),
    )
    out_specs = (
        P(("rep", "dp"), None, None),
        P(("rep", "dp"), None, None),
        P("dp", None),
        P("rep", "dp", None),
        P("rep", "dp", None),
        P("dp", None),
        P("dp", None),
        P("dp", None),
        P("rep", "dp", None),
        P("rep", "dp", None),
        P("dp", None),
        P("dp", None),
    )

    def body(*args):
        return on_device(mesh.shape["rep"], mesh.shape["dp"], *args)

    return jax.shard_map(
        body, mesh=mesh, in_specs=in_specs, out_specs=out_specs, check_vma=False
    )
```

```python
import functools
import math

import jax
import jax.numpy as jnp
from jax import lax
from jax.experimental import pallas as pl
from jax.experimental.pallas import tpu as pltpu
from jax.sharding import PartitionSpec as P

HEAD_DIM = 128
PROMPT = 128
CLEN = 64
CONT = 2
STEP = 10
TEAM = 8


LN_EPS = 1e-05
BETA_ONE = 0.9
BETA_TWO = 0.95
ADAM_EPS = 1e-08
DECAY = 0.1
RATE = 0.05
OUTER_RATE = 0.7
OUTER_MOMENTUM = 0.9
CONTRACT_LAST = (((1,), (1,)), ((), ()))
CONTRACT_FIRST = (((0,), (0,)), ((), ()))
LOW = jnp.bfloat16
FULL = jnp.float32


def normalize(values):
    centre = values - jnp.mean(values, axis=-1, keepdims=True)
    factor = lax.rsqrt(jnp.mean(centre * centre, axis=-1, keepdims=True) + LN_EPS)
    return (centre * factor, factor)


def normalize_back(values, gradient):
    normed, factor = normalize(values)
    projection = jnp.mean(gradient * normed, axis=-1, keepdims=True)
    return factor * (gradient - jnp.mean(gradient, axis=-1, keepdims=True) - normed * projection)


def token_layout(seen, length):
    places = jnp.arange(length, dtype=jnp.int32)
    segment = jnp.where(places < PROMPT, -1, (places - PROMPT) // CLEN)
    within = jnp.where(places < PROMPT, places, (places - PROMPT) % CLEN)
    lookup = jnp.arange(CONT, dtype=jnp.int32)
    reach = jnp.sum(jnp.where(segment[:, None] == lookup[None, :], seen[None, :], 0), axis=1)
    position = jnp.where(segment < 0, places, reach + within)
    allowed = (segment[:, None] == segment[None, :]) & (within[None, :] <= within[:, None]) | (
        segment[None, :] < 0
    ) & (segment[:, None] >= 0) & (places[None, :] < reach[:, None])
    return (position, allowed)


def rotary_tables(position, depth):
    half_depth = depth // 2
    freqs = jnp.exp(jnp.arange(half_depth, dtype=jnp.float32) * (-2.0 * math.log(10000.0) / depth))
    angle = position.astype(jnp.float32)[:, None] * freqs[None, :]
    return (jnp.cos(angle)[:, None, :], jnp.sin(angle)[:, None, :])


def rotate(values, cosine, sine):
    half_depth = values.shape[-1] // 2
    first = values[..., :half_depth]
    second = values[..., half_depth:]
    return jnp.concatenate(
        [first * cosine - second * sine, second * cosine + first * sine], axis=-1
    )


def rotate_back(gradient, cosine, sine):
    half_depth = gradient.shape[-1] // 2
    first = gradient[..., :half_depth]
    second = gradient[..., half_depth:]
    return jnp.concatenate(
        [first * cosine + second * sine, second * cosine - first * sine], axis=-1
    )


def adam_step(master, gradient, first, second):
    first_new = BETA_ONE * first + (1.0 - BETA_ONE) * gradient
    second_new = BETA_TWO * second + (1.0 - BETA_TWO) * gradient * gradient
    ratio = (
        first_new
        / (1.0 - BETA_ONE**STEP)
        / (jnp.sqrt(second_new / (1.0 - BETA_TWO**STEP)) + ADAM_EPS)
    )
    return (master - RATE * (ratio + DECAY * master), first_new, second_new)


def outer_step(master, mean_diff, momentum):
    momentum_new = OUTER_MOMENTUM * momentum + mean_diff
    return (master - OUTER_RATE * (mean_diff + OUTER_MOMENTUM * momentum_new), momentum_new)


def dot(left, right, dims=(((1,), (0,)), ((), ()))):
    return lax.dot_general(left, right, dims, preferred_element_type=FULL)


MESH = pl.DeviceIdType.MESH
ANYWHERE = pl.BlockSpec(memory_space=pl.ANY)
BITS = (1, 2, 4)
PIECES = 4
STRIP = 16
GATHER_COPIES = 6 * PIECES + 1
VMEM_BYTES = 56 * 1024 * 1024


def flip(me, bit):
    return me + bit - 2 * bit * ((me // bit) % 2)


def across(me, other):
    bit = 1
    while bit <= other:
        if other & bit:
            me = flip(me, bit)
        bit *= 2
    return me


def greet(me, others, with_rep):
    barrier = pltpu.get_barrier_semaphore()
    for other in others:
        pl.semaphore_signal(
            barrier, inc=1, device_id={"dp": across(me, other)}, device_id_type=MESH
        )
    if with_rep:
        rep = lax.axis_index("rep")
        pl.semaphore_signal(barrier, inc=1, device_id={"rep": 1 - rep}, device_id_type=MESH)
    pl.semaphore_wait(barrier, len(others) + (1 if with_rep else 0))


class Sender:
    def __init__(self, sent, came):
        self.sent, self.came, self.index = sent, came, 0

    def __call__(self, source, target, where):
        copy = pltpu.make_async_remote_copy(
            src_ref=source,
            dst_ref=target,
            send_sem=self.sent.at[self.index],
            recv_sem=self.came.at[self.index],
            device_id=where,
            device_id_type=MESH,
        )
        copy.start()
        self.index += 1
        return copy


class TeamGather:
    def __init__(self, me, own, out, send):
        self.out, self.send = out, send
        self.piece = own.shape[0] // PIECES
        self.core, self.second, self.third = ({"dp": flip(me, bit)} for bit in BITS)
        self.late = list(range(PIECES // 2, PIECES)) + list(range(PIECES // 2))
        self.early = list(range(PIECES))
        self.own = own
        self.over_second, self.over_third, self.rest = {}, {}, []

    def cut(self, ref, p):
        return ref.at[pl.ds(p * self.piece, self.piece)]

    def begin(self):
        own, out, cut = self.own, self.out, self.cut
        for a, b in zip(self.late, self.early):
            self.over_second[a] = self.send(cut(own, a), cut(out.at[2], a), self.second)
            self.over_third[b] = self.send(cut(own, b), cut(out.at[4], b), self.third)
        self.rest.append(self.send(own, out.at[1], self.core))

    def finish(self, middle=None):
        out, cut, send = self.out, self.cut, self.send
        half = PIECES // 2
        corner = {}
        for a, b in zip(self.late, self.early):
            self.over_second[a].wait_recv()
            if a >= half:
                corner[a] = send(cut(out.at[2], a), cut(out.at[6], a), self.third)
            self.rest.append(send(cut(out.at[2], a), cut(out.at[3], a), self.core))
            self.over_third[b].wait_recv()
            if b < half:
                corner[b] = send(cut(out.at[4], b), cut(out.at[6], b), self.second)
            self.rest.append(send(cut(out.at[4], b), cut(out.at[5], b), self.core))
        if middle is not None:
            middle()
        for p in range(half):
            for q in (p, p + half):
                corner[q].wait_recv()
                self.rest.append(send(cut(out.at[6], q), cut(out.at[7], q), self.core))
        for group in (self.over_second, self.over_third, corner):
            for copy in group.values():
                copy.wait_send()
        for copy in self.rest:
            copy.wait()


SUM_COPIES = 6


def sum_scratch(count, width):
    return [
        pltpu.VMEM((TEAM // 2, count, width), LOW),
        pltpu.VMEM((TEAM // 2, count, width), LOW),
        pltpu.VMEM((3, count, width), LOW),
    ]


def team_sum(me, parts, own, got, edge, send, loads, total, between=None, after=None):
    core = {"dp": flip(me, 1)}
    loading = [pltpu.make_async_copy(parts.at[2 * j], own.at[j], loads.at[j]) for j in range(4)]
    first = {}
    for j in (3, 2, 1, 0):
        loading[j].start()
        first[j] = send(parts.at[2 * j + 1], got.at[j], core)
    for copy in loading:
        copy.wait()
    sum_steps(me, own, got, edge, first, send, total, between, after)


def sum_steps(me, own, got, edge, first, send, total, between=None, after=None):
    count = own.shape[1]
    half = count // 2
    _, second, third = ({"dp": flip(me, bit)} for bit in BITS)

    def cut(ref, h):
        return ref.at[pl.ds(h * half, half)]

    def add(j, h, extra=None):
        @pl.loop(0, half // STRIP)
        def _(step):
            at = pl.ds(h * half + step * STRIP, STRIP)
            value = own[j, at].astype(FULL) + got[j, at].astype(FULL)
            if extra is not None:
                value = value + extra[at].astype(FULL)
            own[j, at] = value.astype(LOW)

    first[3].wait_recv()
    add(3, 0)
    corner_second = send(cut(own.at[3], 0), cut(edge.at[0], 0), second)
    add(3, 1)
    corner_third = send(cut(own.at[3], 1), cut(edge.at[0], 1), third)
    first[2].wait_recv()
    add(2, 1)
    third_late = send(cut(own.at[2], 1), cut(edge.at[2], 1), third)
    first[1].wait_recv()
    add(1, 0)
    second_early = send(cut(own.at[1], 0), cut(edge.at[1], 0), second)
    if between is not None:
        between()
    corner_second.wait_recv()
    add(2, 0, edge.at[0])
    third_early = send(cut(own.at[2], 0), cut(edge.at[2], 0), third)
    corner_third.wait_recv()
    add(1, 1, edge.at[0])
    second_late = send(cut(own.at[1], 1), cut(edge.at[1], 1), second)
    if after is not None:
        after()
    first[0].wait_recv()
    for h, waits in ((0, (second_early, third_early)), (1, (third_late, second_late))):
        for copy in waits:
            copy.wait_recv()

        @pl.loop(0, half // STRIP)
        def _(step, h=h):
            start = h * half + step * STRIP
            at = pl.ds(start, STRIP)
            value = own[0, at].astype(FULL) + got[0, at].astype(FULL)
            total(start, value + edge[1, at].astype(FULL) + edge[2, at].astype(FULL))

    for copy in (
        corner_second, corner_third, third_late, second_early, third_early, second_late
    ):
        copy.wait_send()
    for j in range(4):
        first[j].wait_send()


def params(collective_id):
    return pltpu.CompilerParams(
        collective_id=collective_id, has_side_effects=True, vmem_limit_bytes=VMEM_BYTES
    )


def strip_normalize(value):
    width = value.shape[1]
    centre = value - jnp.sum(value, axis=1, keepdims=True) * (1.0 / width)
    factor = lax.rsqrt(jnp.sum(centre * centre, axis=1, keepdims=True) * (1.0 / width) + LN_EPS)
    return (centre * factor, factor)


class RowGather:
    def __init__(self, ranks, me, rep, weights, send, send_x, local):
        self.me, self.rep, self.weights, self.local = me, rep, weights, local
        self.send, self.send_x = send, send_x
        self.rows = weights.shape[0] // ranks
        self.half = self.rows // 2
        self.order = list(range(TEAM, ranks)) + list(range(1, TEAM))

    def place(self, device):
        return self.weights.at[pl.ds(device * self.rows + self.rep * self.half, self.half)]

    def begin(self, pack):
        me, rep = self.me, self.rep
        at = self.weights.at[pl.ds(me * self.rows, self.rows)]
        self.own = pltpu.make_async_copy(pack.at[me % TEAM], at, self.local)
        self.own.start()
        self.ways = []
        for other in self.order:
            where = across(me, other)
            source = pack.at[where % TEAM, pl.ds(rep * self.half, self.half)]
            self.ways.append(self.send(source, self.place(me), {"dp": where}))

    def forward(self):
        self.swaps = []
        for other, copy in zip(self.order, self.ways):
            copy.wait_recv()
            at = self.place(across(self.me, other))
            self.swaps.append(self.send_x(at, at, {"rep": 1 - self.rep}))

    def finish(self):
        for copy in self.ways:
            copy.wait_send()
        for copy in self.swaps + [self.own]:
            copy.wait()


def attend_unit(values, cosine, sine, bias, share):
    depth = HEAD_DIM
    parts = []
    for p in range(2):
        turned = []
        for at in range(p * share, (p + 1) * share, depth):
            head = values[:, at : at + depth]
            turned.append((head * cosine + pltpu.roll(head, depth // 2, 1) * sine).astype(LOW))
        parts.append(turned)
    query, keys = parts
    value = [
        values[:, at : at + depth].astype(LOW) for at in range(2 * share, 3 * share, depth)
    ]
    mixed = []
    for one, two, three in zip(query, keys, value):
        scores = dot(one, two, CONTRACT_LAST) * depth ** (-0.5) + bias
        powers = jnp.exp(scores - jnp.max(scores, axis=1, keepdims=True))
        prob = powers / jnp.sum(powers, axis=1, keepdims=True)
        mixed.append(dot(prob.astype(LOW), three).astype(LOW))
    return jnp.concatenate(query + keys + value, axis=1), jnp.concatenate(mixed, axis=1)


def forward_kernel(
    ranks,
    flat,
    normed_own,
    cot,
    att_pack,
    mlp_master,
    cosine,
    sine,
    bias,
    normed_all,
    cot_all,
    att_weights,
    gate_weights,
    down_weights,
    gate_pack,
    down_pack,
    projected_all,
    mixed_all,
    resid,
    normed_two_all,
    gate_all,
    up_all,
    hidden_all,
    att,
    gate,
    block,
    odd,
    own,
    got,
    edge,
    normed,
    *sems,
):
    sent_team, came_team, sent_rows, came_rows, sent_x, came_x, first_sent, first_came, local = sems
    me = lax.axis_index("dp")
    rep = lax.axis_index("rep")
    rows, share = att_pack.shape[1], att_pack.shape[2] // 4
    hid = gate_pack.shape[2] // 2
    core = {"dp": flip(me, 1)}
    greet(me, range(1, ranks), True)
    send = Sender(sent_team, came_team)
    send_rows = Sender(sent_rows, came_rows)
    send_x = Sender(sent_x, came_x)
    tokens = TeamGather(me, normed_own, normed_all, send)
    tokens.begin()
    gathers = [
        RowGather(ranks, me, rep, weights, send_rows, send_x, local.at[i])
        for i, weights in enumerate((att_weights, gate_weights, down_weights))
    ]
    gathers[0].begin(att_pack)
    keep = [pltpu.make_async_copy(normed_own, normed_all.at[0], local.at[3])]
    keep.append(pltpu.make_async_copy(cot, cot_all.at[0], local.at[4]))
    for copy in keep:
        copy.start()

    def pack(wide, low):
        def loads(t, slot):
            return [
                pltpu.make_async_copy(
                    mlp_master.at[:, pl.ds((p * TEAM + t) * hid, hid)],
                    wide.at[slot, p],
                    local.at[5 + 3 * slot + p],
                )
                for p in range(3)
            ]

        for copy in loads(0, 0):
            copy.start()

        @pl.loop(0, TEAM)
        def _(t):
            slot = t % 2

            @pl.when(t + 1 < TEAM)
            def _():
                for copy in loads(t + 1, 1 - slot):
                    copy.start()

            for copy in loads(t, slot):
                copy.wait()
            low[:, : 2 * hid] = jnp.concatenate(
                [wide[slot, 0].astype(LOW), wide[slot, 1].astype(LOW)], axis=1
            )
            low[:, 2 * hid :] = wide[slot, 2].astype(LOW)
            out_copies = [
                pltpu.make_async_copy(low.at[:, pl.ds(0, 2 * hid)], gate_pack.at[t], local.at[11]),
                pltpu.make_async_copy(low.at[:, pl.ds(2 * hid, hid)], down_pack.at[t], local.at[12]),
            ]
            for copy in out_copies:
                copy.start()
            for copy in out_copies:
                copy.wait()

    pl.run_scoped(
        pack, pltpu.VMEM((2, 3, rows, hid), FULL), pltpu.VMEM((rows, 3 * hid), LOW)
    )
    tokens.finish()
    gathers[1].begin(gate_pack)
    gathers[0].forward()
    gathers[0].finish()
    for copy in keep:
        copy.wait()
    load = pltpu.make_async_copy(att_weights, att, local.at[0])
    load.start()
    load.wait()

    def unit_of(step):
        return 2 * (TEAM // 2 - 1 - step % (TEAM // 2)) + jnp.where(step < TEAM // 2, 1, 0)

    def fetch(step, slot):
        return pltpu.make_async_copy(
            normed_all.at[unit_of(step)], block.at[slot], local.at[5 + slot]
        )

    fetch(0, 0).start()

    @pl.loop(0, TEAM)
    def _(step):
        slot = step % 2
        unit = unit_of(step)

        @pl.when(step + 1 < TEAM)
        def _():
            fetch(step + 1, 1 - slot).start()

        fetch(step, slot).wait()
        values = dot(block[slot], att[:, : 3 * share])
        projected, mixed = attend_unit(values, cosine[unit], sine[unit], bias[unit], share)
        projected_all[unit] = projected
        mixed_all[unit] = mixed
        term = dot(mixed, att[:, 3 * share :], CONTRACT_LAST).astype(LOW)
        j = unit // 2

        @pl.when(step < TEAM // 2)
        def _():
            odd[j] = term
            pltpu.make_async_remote_copy(
                src_ref=odd.at[j],
                dst_ref=got.at[j],
                send_sem=first_sent.at[j],
                recv_sem=first_came.at[j],
                device_id=core,
                device_id_type=MESH,
            ).start()

        @pl.when(step >= TEAM // 2)
        def _():
            own[j] = term

    first = [
        pltpu.make_async_remote_copy(
            src_ref=odd.at[j],
            dst_ref=got.at[j],
            send_sem=first_sent.at[j],
            recv_sem=first_came.at[j],
            device_id=core,
            device_id_type=MESH,
        )
        for j in range(TEAM // 2)
    ]

    def total(start, value):
        at = pl.ds(start, STRIP)
        value = value + flat[at].astype(FULL)
        resid[at] = value
        normed[at] = strip_normalize(value)[0].astype(LOW)

    sum_steps(me, own, got, edge, first, send, total, gathers[1].forward)
    tokens = TeamGather(me, normed, normed_two_all, send)
    tokens.begin()
    keep = pltpu.make_async_copy(normed, normed_two_all.at[0], local.at[3])
    keep.start()
    tokens.finish()
    cots = TeamGather(me, cot, cot_all, send)
    cots.begin()
    gathers[2].begin(down_pack)
    keep.wait()
    gathers[1].finish()
    load = pltpu.make_async_copy(gate_weights, gate, local.at[1])
    load.start()
    load.wait()

    def feed(low):
        def fetch(unit, slot):
            return pltpu.make_async_copy(
                normed_two_all.at[unit], block.at[slot], local.at[5 + slot]
            )

        def stores(unit, slot):
            return [
                pltpu.make_async_copy(low.at[slot, i], out.at[unit], local.at[7 + 3 * slot + i])
                for i, out in enumerate((gate_all, up_all, hidden_all))
            ]

        fetch(0, 0).start()

        @pl.loop(0, TEAM)
        def _(unit):
            slot = unit % 2

            @pl.when(unit + 1 < TEAM)
            def _():
                fetch(unit + 1, 1 - slot).start()

            fetch(unit, slot).wait()

            @pl.when(unit >= 2)
            def _():
                for copy in stores(unit - 2, slot):
                    copy.wait()

            tile = 256

            @pl.loop(0, hid // tile)
            def _(column):
                at = pl.ds(pl.multiple_of(column * tile, tile), tile)
                later = pl.ds(pl.multiple_of(hid + column * tile, tile), tile)
                gate_value = dot(block[slot], gate[:, at])
                up_value = dot(block[slot], gate[:, later])
                low[slot, 0, :, at] = gate_value.astype(LOW)
                low[slot, 1, :, at] = up_value.astype(LOW)
                hidden = gate_value * jax.nn.sigmoid(gate_value) * up_value
                low[slot, 2, :, at] = hidden.astype(LOW)

            for copy in stores(unit, slot):
                copy.start()

        for unit in (TEAM - 2, TEAM - 1):
            for copy in stores(unit, unit % 2):
                copy.wait()

    pl.run_scoped(feed, pltpu.VMEM((2, 3, normed.shape[0], hid), LOW))
    cots.finish()
    gathers[2].forward()
    gathers[2].finish()


def forward_layer(ranks, flat, normed, cot, att_pack, mlp_master, cosine, sine, bias):
    count, width = normed.shape
    rows, share = att_pack.shape[1], att_pack.shape[2] // 4
    hid = mlp_master.shape[1] // (3 * TEAM)
    gathered = jax.ShapeDtypeStruct((TEAM, count, width), LOW)
    hidden = jax.ShapeDtypeStruct((TEAM, count, hid), LOW)
    vmem = pl.BlockSpec(memory_space=pltpu.VMEM)

    def weights(columns):
        return jax.ShapeDtypeStruct((ranks * rows, columns), LOW)

    def packs(columns):
        return jax.ShapeDtypeStruct((TEAM, rows, columns), LOW)

    out = [
        (gathered, ANYWHERE),
        (gathered, ANYWHERE),
        (weights(4 * share), ANYWHERE),
        (weights(2 * hid), ANYWHERE),
        (weights(hid), ANYWHERE),
        (packs(2 * hid), ANYWHERE),
        (packs(hid), ANYWHERE),
        (jax.ShapeDtypeStruct((TEAM, count, 3 * share), LOW), vmem),
        (jax.ShapeDtypeStruct((TEAM, count, share), LOW), vmem),
        (jax.ShapeDtypeStruct((count, width), FULL), vmem),
        (gathered, ANYWHERE),
        (hidden, ANYWHERE),
        (hidden, ANYWHERE),
        (hidden, ANYWHERE),
    ]
    team_copies = 3 * GATHER_COPIES + SUM_COPIES
    pairs = [team_copies] * 2 + [3 * (ranks - 1)] * 4 + [TEAM // 2] * 2 + [13]
    return pl.pallas_call(
        functools.partial(forward_kernel, ranks),
        out_shape=[shape for shape, _ in out],
        in_specs=[vmem] + [ANYWHERE] * 4 + [vmem] * 3,
        out_specs=[spec for _, spec in out],
        scratch_shapes=[
            pltpu.VMEM((ranks * rows, 4 * share), LOW),
            pltpu.VMEM((ranks * rows, 2 * hid), LOW),
            pltpu.VMEM((2, count, width), LOW),
            pltpu.VMEM((TEAM // 2, count, width), LOW),
            pltpu.VMEM((TEAM // 2, count, width), LOW),
            pltpu.VMEM((TEAM // 2, count, width), LOW),
            pltpu.VMEM((3, count, width), LOW),
            pltpu.VMEM((count, width), LOW),
        ]
        + [pltpu.SemaphoreType.DMA((number,)) for number in pairs],
        compiler_params=params(0),
        name="forward_layer",
    )(flat, normed, cot, att_pack, mlp_master, cosine, sine, bias)


def attend_unit_back(values, given, cosine, sine, bias, share):
    depth = HEAD_DIM
    scale = depth ** (-0.5)
    grads = ([], [], [])
    for at in range(0, share, depth):
        query, keys, value = (values[:, p * share + at : p * share + at + depth] for p in range(3))
        grad = given[:, at : at + depth]
        scores = dot(query, keys, CONTRACT_LAST) * scale + bias
        powers = jnp.exp(scores - jnp.max(scores, axis=1, keepdims=True))
        prob = powers / jnp.sum(powers, axis=1, keepdims=True)
        grad_prob = dot(grad, value, CONTRACT_LAST)
        grad_value = dot(prob.astype(LOW), grad, CONTRACT_FIRST)
        along = jnp.sum(grad_prob * prob, axis=1, keepdims=True)
        grad_scores = (prob * (grad_prob - along)).astype(LOW)
        turned = (
            dot(grad_scores, keys) * scale,
            dot(grad_scores, query, CONTRACT_FIRST) * scale,
        )
        for p in range(2):
            back = turned[p] * cosine - pltpu.roll(turned[p], depth // 2, 1) * sine
            grads[p].append(back.astype(LOW))
        grads[2].append(grad_value.astype(LOW))
    return jnp.concatenate(grads[0] + grads[1] + grads[2], axis=1)


UNIT = 256


def unit_of(step):
    return 2 * (TEAM // 2 - 1 - step % (TEAM // 2)) + jnp.where(step < TEAM // 2, 1, 0)


class Terms:
    def __init__(self, me, odd, own, got, sent, came):
        self.odd, self.own, self.got, self.sent, self.came = odd, own, got, sent, came
        self.core = {"dp": flip(me, 1)}

    def copy(self, j):
        return pltpu.make_async_remote_copy(
            src_ref=self.odd.at[j],
            dst_ref=self.got.at[j],
            send_sem=self.sent.at[j],
            recv_sem=self.came.at[j],
            device_id=self.core,
            device_id_type=MESH,
        )

    def put(self, step, term):
        j = unit_of(step) // 2

        @pl.when(step < TEAM // 2)
        def _():
            self.odd[j] = term
            self.copy(j).start()

        @pl.when(step >= TEAM // 2)
        def _():
            self.own[j] = term

    def first(self):
        return [self.copy(j) for j in range(TEAM // 2)]


def stream(steps, loads, body):
    for copy in loads(0, 0):
        copy.start()

    @pl.loop(0, steps)
    def _(step):
        slot = step % 2

        @pl.when(step + 1 < steps)
        def _():
            for copy in loads(step + 1, 1 - slot):
                copy.start()

        for copy in loads(step, slot):
            copy.wait()
        body(step, slot)


def stream_out(steps, loads, stores, body):
    def whole(step, slot):
        @pl.when(step >= 2)
        def _():
            for copy in stores(step - 2, slot):
                copy.wait()

        body(step, slot)
        for copy in stores(step, slot):
            copy.start()

    stream(steps, loads, whole)
    for step in (steps - 2, steps - 1):
        for copy in stores(step, step % 2):
            copy.wait()


def rows_at(step, size):
    return pl.ds(pl.multiple_of(step * size, size), size)


def backward_kernel(
    ranks,
    flat,
    resid,
    cot,
    cosine,
    sine,
    bias,
    cot_all,
    hidden_all,
    gate_all,
    up_all,
    normed_two_all,
    normed_one_all,
    projected_all,
    mixed_all,
    att_weights,
    gate_weights,
    down_weights,
    att_master,
    att_first,
    att_second,
    mlp_master,
    mlp_first,
    mlp_second,
    out_tokens,
    grad_tokens,
    got_att,
    got_gate,
    got_down,
    att_diff,
    att_other,
    mlp_diff,
    mlp_other,
    grad_all,
    att_grad,
    gate_grad,
    down_grad,
    fed_all,
    own,
    got,
    edge,
    odd,
    own_two,
    got_two,
    edge_two,
    grad_low,
    grad_resid,
    stage,
    sent,
    came,
    sent_rows,
    came_rows,
    sent_first,
    came_first,
    sent_x,
    came_x,
    kept,
    local,
):
    me = lax.axis_index("dp")
    rep = lax.axis_index("rep")
    tops = ranks // TEAM
    rows = got_att.shape[1]
    share = mixed_all.shape[1]
    hid = hidden_all.shape[1]
    count, width = resid.shape
    tokens = TEAM * count
    tiles = width // UNIT
    greet(me, range(1, ranks), True)
    send = Sender(sent, came)
    order = []
    for low_bits in range(TEAM):
        order += [top * TEAM + low_bits for top in range(1, tops)]
        order += [low_bits] if low_bits else []

    chunks = ((down_grad, got_down), (gate_grad, got_gate), (att_grad, got_att))

    def block_copy(chunk, other):
        grad, target = chunks[chunk]
        index = chunk * (ranks - 1) + other - 1
        where = across(me, other)
        return pltpu.make_async_remote_copy(
            src_ref=grad.at[pl.ds(where * rows, rows)],
            dst_ref=target.at[me],
            send_sem=sent_rows.at[index],
            recv_sem=came_rows.at[index],
            device_id={"dp": where},
            device_id_type=MESH,
        )

    def keep_own(grad, target, index):
        copy = pltpu.make_async_copy(
            grad.at[pl.ds(me * rows, rows)], target.at[me], kept.at[index]
        )
        copy.start()
        return copy

    def down_phase(hidden, tile, low):
        whole = pltpu.make_async_copy(hidden_all, hidden, local.at[0])
        whole.start()

        def loads(step, slot):
            at = rows_at(step, UNIT)
            return [pltpu.make_async_copy(cot_all.at[:, at], tile.at[slot], local.at[2 + slot])]

        def stores(step, slot):
            at = rows_at(step, UNIT)
            return [pltpu.make_async_copy(low.at[slot], down_grad.at[at], local.at[4 + slot])]

        def body(step, slot):
            low[slot] = dot(tile[slot], hidden[...], CONTRACT_FIRST).astype(LOW)

        whole.wait()
        stream_out(tiles, loads, stores, body)

    pl.run_scoped(
        down_phase,
        pltpu.VMEM((tokens, hid), LOW),
        pltpu.VMEM((2, tokens, UNIT), LOW),
        pltpu.VMEM((2, UNIT, hid), LOW),
    )
    for other in order:
        block_copy(0, other).start()
    own_copies = [keep_own(down_grad, got_down, 0)]

    def fed_phase(hidden, down, term):
        whole = [
            pltpu.make_async_copy(hidden_all, hidden, local.at[0]),
            pltpu.make_async_copy(down_weights, down, local.at[1]),
        ]
        for copy in whole:
            copy.start()
        for copy in whole:
            copy.wait()

        def fed_stores(step, slot):
            return [pltpu.make_async_copy(term.at[slot], fed_all.at[step], local.at[6 + slot])]

        def fed_body(step, slot):
            term[slot] = dot(hidden[rows_at(step, count)], down[...], CONTRACT_LAST).astype(LOW)

        stream_out(TEAM, lambda step, slot: [], fed_stores, fed_body)

    pl.run_scoped(
        fed_phase,
        pltpu.VMEM((tokens, hid), LOW),
        pltpu.VMEM((width, hid), LOW),
        pltpu.VMEM((2, count, width), LOW),
    )
    gate_order = list(order)

    def more(number):
        def some():
            for _ in range(min(number, len(gate_order))):
                block_copy(1, gate_order.pop(0)).start()

        return some

    terms = Terms(me, odd, own, got, sent_first.at[0], came_first.at[0])

    def gate_phase(grad_gate):
        def hidden_phase(down, block, gate, up):
            whole = pltpu.make_async_copy(down_weights, down, local.at[1])
            whole.start()

            def loads(step, slot):
                at = rows_at(step, count)
                return [
                    pltpu.make_async_copy(cot_all.at[at], block.at[slot], local.at[2 + slot]),
                    pltpu.make_async_copy(gate_all.at[at], gate.at[slot], local.at[4 + slot]),
                    pltpu.make_async_copy(up_all.at[at], up.at[slot], local.at[6 + slot]),
                ]

            def body(step, slot):
                at = rows_at(step, count)

                @pl.loop(0, hid // UNIT)
                def _(column):
                    place = rows_at(column, UNIT)
                    later = pl.ds(pl.multiple_of(hid + column * UNIT, UNIT), UNIT)
                    grad = dot(block[slot], down[:, place])
                    value = gate[slot, :, place].astype(FULL)
                    sigmoid = jax.nn.sigmoid(value)
                    slope = sigmoid * (1.0 + value * (1.0 - sigmoid))
                    up_value = up[slot, :, place].astype(FULL)
                    grad_gate[at, place] = (grad * up_value * slope).astype(LOW)
                    grad_gate[at, later] = (grad * value * sigmoid).astype(LOW)

            whole.wait()
            stream(TEAM, loads, body)

        pl.run_scoped(
            hidden_phase,
            pltpu.VMEM((width, hid), LOW),
            pltpu.VMEM((2, count, width), LOW),
            pltpu.VMEM((2, count, hid), LOW),
            pltpu.VMEM((2, count, hid), LOW),
        )

        def weight_phase(tile, low):
            def loads(step, slot):
                at = rows_at(step, UNIT)
                return [
                    pltpu.make_async_copy(
                        normed_two_all.at[:, at], tile.at[slot], local.at[2 + slot]
                    )
                ]

            def stores(step, slot):
                at = rows_at(step, UNIT)
                return [pltpu.make_async_copy(low.at[slot], gate_grad.at[at], local.at[4 + slot])]

            def body(step, slot):
                low[slot] = dot(tile[slot], grad_gate[...], CONTRACT_FIRST).astype(LOW)

            stream_out(tiles, loads, stores, body)

        pl.run_scoped(
            weight_phase, pltpu.VMEM((2, tokens, UNIT), LOW), pltpu.VMEM((2, UNIT, 2 * hid), LOW)
        )
        more(GATE_FIRST)()

        def back_phase(gate):
            whole = pltpu.make_async_copy(gate_weights, gate, local.at[0])
            whole.start()
            whole.wait()

            @pl.loop(0, TEAM)
            def _(step):
                at = rows_at(unit_of(step), count)
                terms.put(step, dot(grad_gate[at], gate[...], CONTRACT_LAST).astype(LOW))

        pl.run_scoped(back_phase, pltpu.VMEM((width, 2 * hid), LOW))

    pl.run_scoped(gate_phase, pltpu.VMEM((tokens, 2 * hid), LOW))
    own_copies.append(keep_own(gate_grad, got_gate, 1))

    def resid_total(start, value):
        at = pl.ds(start, STRIP)
        normed, factor = strip_normalize(resid[at])
        along = jnp.sum(value * normed, axis=1, keepdims=True) * (1.0 / width)
        middle = jnp.sum(value, axis=1, keepdims=True) * (1.0 / width)
        value = cot[at].astype(FULL) + factor * (value - middle - normed * along)
        grad_resid[at] = value
        grad_low[at] = value.astype(LOW)

    sum_steps(
        me, own, got, edge, terms.first(), send, resid_total, more(GATE_EARLY), more(GATE_LATE)
    )
    gather = TeamGather(me, grad_low, grad_all, send)
    gather.begin()
    more(GATE_GATHER)()
    keep = pltpu.make_async_copy(grad_low, grad_all.at[0], local.at[0])
    keep.start()
    gather.finish(more(len(gate_order)))
    keep.wait()

    terms = Terms(me, odd, own, got, sent_first.at[1], came_first.at[1])

    def att_phase(att, grad_projected):
        def unit_phase(block, projected, tables, mask):
            def loads(step, slot):
                unit = unit_of(step)
                return [
                    pltpu.make_async_copy(grad_all.at[unit], block.at[slot], local.at[slot]),
                    pltpu.make_async_copy(
                        projected_all.at[unit], projected.at[slot], local.at[2 + slot]
                    ),
                    pltpu.make_async_copy(cosine.at[unit], tables.at[slot, 0], local.at[4 + slot]),
                    pltpu.make_async_copy(sine.at[unit], tables.at[slot, 1], local.at[6 + slot]),
                    pltpu.make_async_copy(bias.at[unit], mask.at[slot], local.at[8 + slot]),
                ]

            def body(step, slot):
                given = dot(block[slot], att[:, 3 * share :]).astype(LOW)
                grads = attend_unit_back(
                    projected[slot], given, tables[slot, 0], tables[slot, 1], mask[slot], share
                )
                grad_projected[rows_at(unit_of(step), count)] = grads
                terms.put(step, dot(grads, att[:, : 3 * share], CONTRACT_LAST).astype(LOW))

            whole = pltpu.make_async_copy(att_weights, att, local.at[10])
            whole.start()
            whole.wait()
            stream(TEAM, loads, body)

        pl.run_scoped(
            unit_phase,
            pltpu.VMEM((2, count, width), LOW),
            pltpu.VMEM((2, count, 3 * share), LOW),
            pltpu.VMEM((2, 2, count, HEAD_DIM), FULL),
            pltpu.VMEM((2, count, count), FULL),
        )

        def weight_phase(normed, grad, mixed, low):
            def loads(step, slot):
                at = rows_at(step, UNIT)
                return [
                    pltpu.make_async_copy(
                        normed_one_all.at[:, at], normed.at[slot], local.at[slot]
                    ),
                    pltpu.make_async_copy(
                        grad_all.at[:, :, at], grad.at[slot], local.at[2 + slot]
                    ),
                ]

            def stores(step, slot):
                at = rows_at(step, UNIT)
                return [pltpu.make_async_copy(low.at[slot], att_grad.at[at], local.at[4 + slot])]

            def body(step, slot):
                left = normed[slot]
                low[slot, :, : 3 * share] = dot(left, grad_projected[...], CONTRACT_FIRST).astype(LOW)
                left = grad[slot].reshape(tokens, UNIT)
                low[slot, :, 3 * share :] = dot(left, mixed[...], CONTRACT_FIRST).astype(LOW)

            whole = pltpu.make_async_copy(mixed_all, mixed, local.at[10])
            whole.start()
            whole.wait()
            stream_out(tiles, loads, stores, body)

        pl.run_scoped(
            weight_phase,
            pltpu.VMEM((2, tokens, UNIT), LOW),
            pltpu.VMEM((2, TEAM, count, UNIT), LOW),
            pltpu.VMEM((tokens, share), LOW),
            pltpu.VMEM((2, UNIT, 4 * share), LOW),
        )

    pl.run_scoped(
        att_phase, pltpu.VMEM((width, 4 * share), LOW), pltpu.VMEM((tokens, 3 * share), LOW)
    )
    for other in order:
        block_copy(2, other).start()
    own_copies.append(keep_own(att_grad, got_att, 2))

    def differ(chunk, pieces, states, diff, other, column, mates):
        master, first, second = states
        each = hid // mates

        def near(block):
            return pltpu.make_async_copy(
                stage.at[block], diff.at[:, column(block)], kept.at[3 + block]
            )

        def far(block):
            index = chunk * TEAM + block
            return pltpu.make_async_remote_copy(
                src_ref=stage.at[block],
                dst_ref=other.at[:, column(block)],
                send_sem=sent_x.at[index],
                recv_sem=came_x.at[index],
                device_id={"rep": 1 - rep},
                device_id_type=MESH,
            )

        def run(wide, low):
            def loads(block, slot):
                at = column(block)
                return [
                    pltpu.make_async_copy(master.at[:, at], wide.at[slot, 0], local.at[slot]),
                    pltpu.make_async_copy(first.at[0, :, at], wide.at[slot, 1], local.at[2 + slot]),
                    pltpu.make_async_copy(second.at[0, :, at], wide.at[slot, 2], local.at[4 + slot]),
                ] + [
                    pltpu.make_async_copy(
                        pieces(block, top, i),
                        low.at[slot, top, i],
                        local.at[6 + slot + 2 * (top * mates + i)],
                    )
                    for top in range(tops)
                    for i in range(mates)
                ]

            def body(block, slot):
                @pl.loop(0, rows // STRIP)
                def _(step):
                    at = pl.ds(step * STRIP, STRIP)
                    for i in range(mates):
                        span = slice(i * each, (i + 1) * each)
                        grad = low[slot, 0, i, at].astype(FULL)
                        for top in range(1, tops):
                            grad = grad + low[slot, top, i, at].astype(FULL)
                        value = wide[slot, 0, at, span]
                        inner, _, _ = adam_step(
                            value, grad, wide[slot, 1, at, span], wide[slot, 2, at, span]
                        )
                        stage[block, at, span] = (value - inner).astype(LOW)

                near(block).start()
                far(block).start()

            stream(TEAM, loads, body)

            @pl.loop(0, TEAM)
            def _(block):
                near(block).wait()
                far(block).wait_send()

        pl.run_scoped(
            run,
            pltpu.VMEM((2, 3, rows, hid), FULL),
            pltpu.VMEM((2, tops, mates, rows, each), LOW),
        )

        def finish():
            @pl.loop(0, TEAM)
            def _(block):
                far(block).wait_recv()

        return finish

    def mlp_chunk(chunk, part, source, offset):
        return differ(
            chunk,
            lambda block, top, i: source.at[top * TEAM + block, :, pl.ds(offset, hid)],
            (mlp_master, mlp_first, mlp_second),
            mlp_diff,
            mlp_other,
            lambda block: pl.ds(pl.multiple_of((part * TEAM + block) * hid, hid), hid),
            1,
        )

    def att_chunk(chunk):
        mates = hid // share
        steps = TEAM // mates

        def piece(block, top, i):
            part = block // steps
            mate = (block % steps) * mates + i
            at = pl.ds(pl.multiple_of(part * share, share), share)
            return got_att.at[top * TEAM + mate, :, at]

        return differ(
            chunk,
            piece,
            (att_master, att_first, att_second),
            att_diff,
            att_other,
            lambda block: pl.ds(pl.multiple_of(block * hid, hid), hid),
            mates,
        )

    waits = []

    def down_changes():
        own_copies[0].wait()
        for other in order:
            block_copy(0, other).wait_recv()
        waits.append(mlp_chunk(0, 2, got_down, 0))

    def gate_changes():
        own_copies[1].wait()
        for other in order:
            block_copy(1, other).wait_recv()
        waits.append(mlp_chunk(1, 0, got_gate, 0))
        waits.append(mlp_chunk(2, 1, got_gate, hid))

    def tokens_total(start, value):
        at = pl.ds(start, STRIP)
        normed, factor = strip_normalize(flat[at].astype(FULL))
        along = jnp.sum(value * normed, axis=1, keepdims=True) * (1.0 / width)
        middle = jnp.sum(value, axis=1, keepdims=True) * (1.0 / width)
        grad_tokens[at] = grad_resid[at] + factor * (value - middle - normed * along)

    def out_total(start, value):
        at = pl.ds(start, STRIP)
        out_tokens[at] = (resid[at] + value).astype(LOW)

    def fed_sum():
        team_sum(
            me, fed_all, own_two, got_two, edge_two, send, local, out_total, gate_changes
        )

    down_changes()
    sum_steps(me, own, got, edge, terms.first(), send, tokens_total, fed_sum)
    own_copies[2].wait()
    for other in order:
        block_copy(2, other).wait_recv()
    waits.append(att_chunk(3))
    for chunk in range(3):
        for other in order:
            block_copy(chunk, other).wait_send()
    for wait in waits:
        wait()


GATE_FIRST, GATE_EARLY, GATE_LATE, GATE_GATHER = 2, 2, 2, 2


def backward_layer(ranks, tokens, att, mlp, *rest):
    flat, resid, cot = tokens
    hidden_all, projected_all, gate_weights = rest[4], rest[9], rest[12]
    count, width = flat.shape
    all_tokens, hid = hidden_all.shape
    share = projected_all.shape[2] // 3
    rows = width // ranks
    vmem = pl.BlockSpec(memory_space=pltpu.VMEM)
    low = functools.partial(jax.ShapeDtypeStruct, dtype=LOW)
    out = [
        (low((count, width)), vmem),
        (jax.ShapeDtypeStruct((count, width), FULL), vmem),
        (low((ranks, rows, 4 * share)), ANYWHERE),
        (low((ranks, rows, 2 * hid)), ANYWHERE),
        (low((ranks, rows, hid)), ANYWHERE),
        (low(att[0].shape), ANYWHERE),
        (low(att[0].shape), ANYWHERE),
        (low(mlp[0].shape), ANYWHERE),
        (low(mlp[0].shape), ANYWHERE),
        (low((TEAM, count, width)), ANYWHERE),
        (low((width, 4 * share)), ANYWHERE),
        (low((width, 2 * hid)), ANYWHERE),
        (low((width, hid)), ANYWHERE),
        (low((TEAM, count, width)), ANYWHERE),
    ]
    team_copies = GATHER_COPIES + 2 * SUM_COPIES + SUM_COPIES + TEAM // 2
    locals_needed = 6 + 2 * (ranks // TEAM) * (hid // share) + 2
    sems = [team_copies] * 2 + [3 * (ranks - 1)] * 2
    return pl.pallas_call(
        functools.partial(backward_kernel, ranks),
        out_shape=[shape for shape, _ in out],
        in_specs=[vmem] * 3 + [ANYWHERE] * (len(rest) + 6),
        out_specs=[spec for _, spec in out],
        scratch_shapes=sum_scratch(count, width)
        + [pltpu.VMEM((TEAM // 2, count, width), LOW)]
        + sum_scratch(count, width)
        + [
            pltpu.VMEM((count, width), LOW),
            pltpu.VMEM((count, width), FULL),
            pltpu.VMEM((TEAM, rows, hid), LOW),
        ]
        + [pltpu.SemaphoreType.DMA((number,)) for number in sems]
        + [pltpu.SemaphoreType.DMA((2, TEAM // 2))] * 2
        + [pltpu.SemaphoreType.DMA((4 * TEAM,))] * 2
        + [
            pltpu.SemaphoreType.DMA((3 + TEAM,)),
            pltpu.SemaphoreType.DMA((max(locals_needed, 12),)),
        ],
        compiler_params=params(2),
        name="backward_layer",
    )(flat, resid, cot, *rest, *att, *mlp)


def pack_kernel(*refs):
    share = refs[0].shape[1]
    for p, ref in enumerate(refs[:-1]):
        refs[-1][0, :, p * share : (p + 1) * share] = ref[...].astype(LOW)


def pack_shares(master, bases, share):
    rows = master.shape[0]
    return pl.pallas_call(
        pack_kernel,
        grid=(TEAM,),
        out_shape=jax.ShapeDtypeStruct((TEAM, rows, len(bases) * share), LOW),
        in_specs=[
            pl.BlockSpec((rows, share), lambda i, base=base: (0, base + i)) for base in bases
        ],
        out_specs=pl.BlockSpec((1, rows, len(bases) * share), lambda i: (i, 0, 0)),
        name="pack_shares",
    )(*[master] * len(bases))


LANES = 1024


def finish_kernel(reps, share, grads, master, first, second, outer, diff, other, *refs):
    first_new, second_new, mean_out, new, outer_new = refs[-5:]
    for t in range(grads.shape[1]):
        at = slice(t * share, (t + 1) * share)
        grad = grads[0, t].astype(FULL)
        for top in range(1, grads.shape[0]):
            grad = grad + grads[top, t].astype(FULL)
        first_new[0, :, at] = BETA_ONE * first[0, :, at] + (1.0 - BETA_ONE) * grad
        second_new[0, :, at] = BETA_TWO * second[0, :, at] + (1.0 - BETA_TWO) * grad * grad
    mean = (diff[...].astype(FULL) + other[...].astype(FULL)) / reps
    mean_out[...] = mean
    new[...], outer_new[...] = outer_step(master[...], mean, outer[...])


def finish_chunk(reps, grads, master, first, second, outer, diff, other, bases, written):
    ranks, rows, columns = grads.shape
    parts = len(bases)
    share = columns // parts
    lanes = max(LANES, share)
    per = lanes // share
    steps = TEAM // per

    def column(p, t):
        place = bases[0]
        for q in range(1, parts):
            place = place + jnp.where(p >= q, bases[q] - bases[q - 1], 0)
        return place * steps + t

    grad = pl.BlockSpec((ranks // TEAM, per, rows, share), lambda p, t: (0, t, 0, p))
    wide = pl.BlockSpec((1, rows, lanes), lambda p, t: (0, 0, column(p, t)))
    flat = pl.BlockSpec((rows, lanes), lambda p, t: (0, column(p, t)))
    extra = [] if written is None else list(written)
    state = jax.ShapeDtypeStruct(first.shape, FULL)
    plain = jax.ShapeDtypeStruct(master.shape, FULL)
    return pl.pallas_call(
        functools.partial(finish_kernel, reps, share),
        grid=(parts, steps),
        out_shape=[state, state, plain, plain, plain],
        in_specs=[grad, flat, wide, wide, flat, flat, flat] + [ANYWHERE] * len(extra),
        out_specs=[wide, wide, flat, flat, flat],
        input_output_aliases={7 + i: i for i in range(len(extra))},
        compiler_params=pltpu.CompilerParams(vmem_limit_bytes=VMEM_BYTES),
        name="finish_chunk",
    )(
        grads.reshape(ranks // TEAM, TEAM, rows, columns),
        master, first, second, outer, diff, other, *extra,
    )


def on_device(
    reps,
    ranks,
    tokens,
    cotangent,
    branch,
    att_master,
    att_first,
    att_second,
    att_outer,
    mlp_master,
    mlp_first,
    mlp_second,
    mlp_outer,
):
    units, length, width = tokens.shape
    hidden_width = mlp_master.shape[1] // 3
    depth = HEAD_DIM
    count = units * length
    rows = att_master.shape[0]
    team = TEAM
    tops = ranks // team
    all_tokens = team * count
    att_share = width // team
    hid_share = hidden_width // team
    me = lax.axis_index("dp")
    rep = lax.axis_index("rep")
    top = me // team

    def hop(values, other):
        pairs = [(r * ranks + i, r * ranks + (i ^ other)) for r in range(reps) for i in range(ranks)]
        return lax.ppermute(values, ("rep", "dp"), pairs)

    flat_low = tokens.reshape(count, width)
    flat = flat_low.astype(FULL)
    cot = cotangent.reshape(count, width)
    seen_all = jnp.stack([branch if k == 0 else hop(branch, k) for k in range(team)])
    seen_all = seen_all.reshape(team * units, CONT)
    position, allowed = jax.vmap(lambda seen: token_layout(seen, length))(seen_all)
    cosine, sine = jax.vmap(lambda places: rotary_tables(places, depth))(position)
    bias = jnp.where(allowed, 0.0, -1e30).astype(FULL)
    wide_cosine = jnp.concatenate([cosine, cosine], axis=-1).reshape(team, count, depth)
    wide_sine = jnp.concatenate([-sine, sine], axis=-1).reshape(team, count, depth)
    att_pack = pack_shares(att_master, [0, team, 2 * team, 3 * team], att_share)
    (
        normed_one,
        grad_fed,
        att_low,
        gate_low,
        down_low,
        _,
        _,
        projected,
        mixed,
        resid,
        normed_two,
        gate_value,
        up_value,
        hidden,
    ) = forward_layer(
        ranks,
        flat_low,
        normalize(flat)[0].astype(LOW),
        cot,
        att_pack,
        mlp_master,
        wide_cosine,
        wide_sine,
        bias,
    )
    (
        out_tokens,
        grad_tokens,
        got_att,
        got_gate,
        got_down,
        att_diff,
        att_other,
        mlp_diff,
        mlp_other,
        *_,
    ) = backward_layer(
        ranks,
        (flat_low, resid, cot),
        (att_master, att_first, att_second),
        (mlp_master, mlp_first, mlp_second),
        wide_cosine,
        wide_sine,
        bias,
        grad_fed.reshape(all_tokens, width),
        hidden.reshape(all_tokens, hid_share),
        gate_value.reshape(all_tokens, hid_share),
        up_value.reshape(all_tokens, hid_share),
        normed_two.reshape(all_tokens, width),
        normed_one.reshape(all_tokens, width),
        projected,
        mixed.reshape(all_tokens, att_share),
        att_low,
        gate_low,
        down_low,
    )
    mlp = (mlp_master, mlp_first, mlp_second, mlp_outer, mlp_diff, mlp_other)
    mlp_out = finish_chunk(reps, got_down, *mlp, [2], None)
    mlp_out = finish_chunk(reps, got_gate, *mlp, [0, 1], mlp_out)
    att_out = finish_chunk(
        reps, got_att, att_master, att_first, att_second, att_outer, att_diff, att_other,
        [0, 1, 2, 3], None,
    )
    return (
        out_tokens.reshape(units, length, width),
        grad_tokens.reshape(units, length, width),
        *(att_out[3], att_out[0], att_out[1], att_out[2], att_out[4]),
        *(mlp_out[3], mlp_out[0], mlp_out[1], mlp_out[2], mlp_out[4]),
    )


def solution(mesh):
    in_specs = (
        P(("rep", "dp"), None, None),
        P(("rep", "dp"), None, None),
        P(("rep", "dp"), None),
        P("dp", None),
        P("rep", "dp", None),
        P("rep", "dp", None),
        P("dp", None),
        P("dp", None),
        P("rep", "dp", None),
        P("rep", "dp", None),
        P("dp", None),
    )
    out_specs = (
        P(("rep", "dp"), None, None),
        P(("rep", "dp"), None, None),
        P("dp", None),
        P("rep", "dp", None),
        P("rep", "dp", None),
        P("dp", None),
        P("dp", None),
        P("dp", None),
        P("rep", "dp", None),
        P("rep", "dp", None),
        P("dp", None),
        P("dp", None),
    )

    def body(*args):
        return on_device(mesh.shape["rep"], mesh.shape["dp"], *args)

    return jax.shard_map(
        body, mesh=mesh, in_specs=in_specs, out_specs=out_specs, check_vma=False
    )
```

```python
import functools
import math

import jax
import jax.numpy as jnp
from jax import lax
from jax.experimental import pallas as pl
from jax.experimental.pallas import tpu as pltpu
from jax.sharding import PartitionSpec as P

HEAD_DIM = 128
PROMPT = 128
CLEN = 64
CONT = 2
STEP = 10
TEAM = 8


LN_EPS = 1e-05
BETA_ONE = 0.9
BETA_TWO = 0.95
ADAM_EPS = 1e-08
DECAY = 0.1
RATE = 0.05
OUTER_RATE = 0.7
OUTER_MOMENTUM = 0.9
CONTRACT_LAST = (((1,), (1,)), ((), ()))
CONTRACT_FIRST = (((0,), (0,)), ((), ()))
LOW = jnp.bfloat16
FULL = jnp.float32


def normalize(values):
    centre = values - jnp.mean(values, axis=-1, keepdims=True)
    factor = lax.rsqrt(jnp.mean(centre * centre, axis=-1, keepdims=True) + LN_EPS)
    return (centre * factor, factor)


def normalize_back(values, gradient):
    normed, factor = normalize(values)
    projection = jnp.mean(gradient * normed, axis=-1, keepdims=True)
    return factor * (gradient - jnp.mean(gradient, axis=-1, keepdims=True) - normed * projection)


def token_layout(seen, length):
    places = jnp.arange(length, dtype=jnp.int32)
    segment = jnp.where(places < PROMPT, -1, (places - PROMPT) // CLEN)
    within = jnp.where(places < PROMPT, places, (places - PROMPT) % CLEN)
    lookup = jnp.arange(CONT, dtype=jnp.int32)
    reach = jnp.sum(jnp.where(segment[:, None] == lookup[None, :], seen[None, :], 0), axis=1)
    position = jnp.where(segment < 0, places, reach + within)
    allowed = (segment[:, None] == segment[None, :]) & (within[None, :] <= within[:, None]) | (
        segment[None, :] < 0
    ) & (segment[:, None] >= 0) & (places[None, :] < reach[:, None])
    return (position, allowed)


def rotary_tables(position, depth):
    half_depth = depth // 2
    freqs = jnp.exp(jnp.arange(half_depth, dtype=jnp.float32) * (-2.0 * math.log(10000.0) / depth))
    angle = position.astype(jnp.float32)[:, None] * freqs[None, :]
    return (jnp.cos(angle)[:, None, :], jnp.sin(angle)[:, None, :])


def rotate(values, cosine, sine):
    half_depth = values.shape[-1] // 2
    first = values[..., :half_depth]
    second = values[..., half_depth:]
    return jnp.concatenate(
        [first * cosine - second * sine, second * cosine + first * sine], axis=-1
    )


def rotate_back(gradient, cosine, sine):
    half_depth = gradient.shape[-1] // 2
    first = gradient[..., :half_depth]
    second = gradient[..., half_depth:]
    return jnp.concatenate(
        [first * cosine + second * sine, second * cosine - first * sine], axis=-1
    )


def adam_step(master, gradient, first, second):
    first_new = BETA_ONE * first + (1.0 - BETA_ONE) * gradient
    second_new = BETA_TWO * second + (1.0 - BETA_TWO) * gradient * gradient
    ratio = (
        first_new
        / (1.0 - BETA_ONE**STEP)
        / (jnp.sqrt(second_new / (1.0 - BETA_TWO**STEP)) + ADAM_EPS)
    )
    return (master - RATE * (ratio + DECAY * master), first_new, second_new)


def outer_step(master, mean_diff, momentum):
    momentum_new = OUTER_MOMENTUM * momentum + mean_diff
    return (master - OUTER_RATE * (mean_diff + OUTER_MOMENTUM * momentum_new), momentum_new)


def dot(left, right, dims=(((1,), (0,)), ((), ()))):
    return lax.dot_general(left, right, dims, preferred_element_type=FULL)


MESH = pl.DeviceIdType.MESH
ANYWHERE = pl.BlockSpec(memory_space=pl.ANY)
BITS = (1, 2, 4)
PIECES = 4
FEED_EARLY = 6
SPLIT_TOKENS, SPLIT_ATTENDED, SPLIT_NORMED, SPLIT_COT, SPLIT_BACK = 3, 3, 3, 3, 3
STRIP = 16
GATHER_COPIES = 6 * PIECES + 1
VMEM_BYTES = 60 * 1024 * 1024


def flip(me, bit):
    return me + bit - 2 * bit * ((me // bit) % 2)


def across(me, other):
    bit = 1
    while bit <= other:
        if other & bit:
            me = flip(me, bit)
        bit *= 2
    return me


def greet(me, others, with_rep):
    barrier = pltpu.get_barrier_semaphore()
    for other in others:
        pl.semaphore_signal(
            barrier, inc=1, device_id={"dp": across(me, other)}, device_id_type=MESH
        )
    if with_rep:
        rep = lax.axis_index("rep")
        pl.semaphore_signal(barrier, inc=1, device_id={"rep": 1 - rep}, device_id_type=MESH)
    pl.semaphore_wait(barrier, len(others) + (1 if with_rep else 0))


class Sender:
    def __init__(self, sent, came):
        self.sent, self.came, self.index = sent, came, 0

    def __call__(self, source, target, where):
        copy = pltpu.make_async_remote_copy(
            src_ref=source,
            dst_ref=target,
            send_sem=self.sent.at[self.index],
            recv_sem=self.came.at[self.index],
            device_id=where,
            device_id_type=MESH,
        )
        copy.start()
        self.index += 1
        return copy


class TeamGather:
    def __init__(self, me, own, out, send, split):
        self.out, self.send, self.split = out, send, split
        self.piece = own.shape[0] // PIECES
        self.core, self.second, self.third = ({"dp": flip(me, bit)} for bit in BITS)
        self.late = list(range(split, PIECES)) + list(range(split))
        self.early = list(range(PIECES))
        self.own = own
        self.over_second, self.over_third, self.corner = {}, {}, {}
        self.rest, self.settled = [], []

    def cut(self, ref, p):
        return ref.at[pl.ds(p * self.piece, self.piece)]

    def begin(self):
        own, out, cut = self.own, self.out, self.cut
        for a, b in zip(self.late, self.early):
            self.over_second[a] = self.send(cut(own, a), cut(out.at[2], a), self.second)
            self.over_third[b] = self.send(cut(own, b), cut(out.at[4], b), self.third)
        self.rest.append(self.send(own, out.at[1], self.core))

    def turn(self):
        out, cut, send = self.out, self.cut, self.send
        for a, b in zip(self.late, self.early):
            self.over_second[a].wait_recv()
            if a >= self.split:
                self.corner[a] = send(cut(out.at[2], a), cut(out.at[6], a), self.third)
            self.rest.append(send(cut(out.at[2], a), cut(out.at[3], a), self.core))
            self.over_third[b].wait_recv()
            if b < self.split:
                self.corner[b] = send(cut(out.at[4], b), cut(out.at[6], b), self.second)
            self.rest.append(send(cut(out.at[4], b), cut(out.at[5], b), self.core))

    def settle(self):
        for copy in self.rest:
            copy.wait_recv()
        self.settled, self.rest = self.rest, []

    def finish(self):
        for p, copy in self.corner.items():
            copy.wait_recv()
            at = self.cut(self.out.at[6], p), self.cut(self.out.at[7], p)
            self.rest.append(self.send(*at, self.core))
        for group in (self.over_second, self.over_third, self.corner):
            for copy in group.values():
                copy.wait_send()
        for copy in self.settled:
            copy.wait_send()
        for copy in self.rest:
            copy.wait()


SUM_COPIES = 6


def sum_scratch(count, width):
    return [
        pltpu.VMEM((TEAM // 2, count, width), LOW),
        pltpu.VMEM((TEAM // 2, count, width), LOW),
        pltpu.VMEM((3, count, width), LOW),
    ]


def team_sum(me, parts, own, got, edge, send, loads, total, split):
    core = {"dp": flip(me, 1)}
    loading = [pltpu.make_async_copy(parts.at[2 * j], own.at[j], loads.at[j]) for j in range(4)]
    first = {}
    for j in (3, 2, 1, 0):
        loading[j].start()
        first[j] = send(parts.at[2 * j + 1], got.at[j], core)
    for copy in loading:
        copy.wait()
    yield from sum_steps(me, own, got, edge, first, send, total, split)


def sum_steps(me, own, got, edge, first, send, total, split):
    count = own.shape[1]
    _, second, third = ({"dp": flip(me, bit)} for bit in BITS)
    spans = [pl.ds(0, split), pl.ds(split, count - split)]

    def add(j, h, extra=None):
        span = spans[h]

        @pl.loop(0, span.size // STRIP)
        def _(step):
            at = pl.ds(span.start + step * STRIP, STRIP)
            value = own[j, at].astype(FULL) + got[j, at].astype(FULL)
            if extra is not None:
                value = value + extra[at].astype(FULL)
            own[j, at] = value.astype(LOW)

    def go(j, h, slot, where):
        return send(own.at[j].at[spans[h]], edge.at[slot].at[spans[h]], where)

    both = split < count
    sends = []
    first[3].wait_recv()
    add(3, 0)
    corner_second = go(3, 0, 0, second)
    if both:
        add(3, 1)
        corner_third = go(3, 1, 0, third)
        sends.append(corner_third)
        first[2].wait_recv()
        add(2, 1)
        sends.append(go(2, 1, 2, third))
    first[1].wait_recv()
    add(1, 0)
    sends.append(go(1, 0, 1, second))
    yield
    if not both:
        first[2].wait_recv()
    corner_second.wait_recv()
    add(2, 0, edge.at[0])
    sends.append(go(2, 0, 2, third))
    if both:
        corner_third.wait_recv()
        add(1, 1, edge.at[0])
        sends.append(go(1, 1, 1, second))
    yield
    first[0].wait_recv()
    for copy in sends:
        if not both or copy is not corner_third:
            copy.wait_recv()

    @pl.loop(0, count // STRIP)
    def _(step):
        start = step * STRIP
        at = pl.ds(start, STRIP)
        value = own[0, at].astype(FULL) + got[0, at].astype(FULL)
        total(start, value + edge[1, at].astype(FULL) + edge[2, at].astype(FULL))

    for copy in sends + [corner_second] + [first[j] for j in range(4)]:
        copy.wait_send()


def params(collective_id):
    return pltpu.CompilerParams(
        collective_id=collective_id, has_side_effects=True, vmem_limit_bytes=VMEM_BYTES
    )


def strip_normalize(value):
    width = value.shape[1]
    centre = value - jnp.sum(value, axis=1, keepdims=True) * (1.0 / width)
    factor = lax.rsqrt(jnp.sum(centre * centre, axis=1, keepdims=True) * (1.0 / width) + LN_EPS)
    return (centre * factor, factor)


UNIT = 256


def unit_of(step):
    return 2 * (TEAM // 2 - 1 - step % (TEAM // 2)) + jnp.where(step < TEAM // 2, 1, 0)


def stream(steps, loads, body, arrive=None):
    if arrive is not None:
        arrive(0)
    for copy in loads(0, 0):
        copy.start()

    @pl.loop(0, steps)
    def _(step):
        slot = step % 2

        @pl.when(step + 1 < steps)
        def _():
            if arrive is not None:
                arrive(step + 1)
            for copy in loads(step + 1, 1 - slot):
                copy.start()

        for copy in loads(step, slot):
            copy.wait()
        body(step, slot)


def stream_out(steps, loads, stores, body):
    def whole(step, slot):
        @pl.when(step >= 2)
        def _():
            for copy in stores(step - 2, slot):
                copy.wait()

        body(step, slot)
        for copy in stores(step, slot):
            copy.start()

    stream(steps, loads, whole)
    for step in (steps - 2, steps - 1):
        for copy in stores(step, step % 2):
            copy.wait()


def rows_at(step, size):
    return pl.ds(pl.multiple_of(step * size, size), size)


class RowGather:
    def __init__(self, ranks, me, rep, weights, send, send_x, local):
        self.me, self.rep, self.weights, self.local = me, rep, weights, local
        self.send, self.send_x = send, send_x
        self.rows = weights.shape[0] // ranks
        self.half = self.rows // 2
        self.order = list(range(TEAM, ranks)) + list(range(1, TEAM))
        self.ways, self.swaps = {}, []
        near = [other for other in self.order if other < 4]
        self.turns = near + [other for other in self.order if other >= 4]

    def place(self, device):
        return self.weights.at[pl.ds(device * self.rows + self.rep * self.half, self.half)]

    def begin(self, pack, number=None):
        me, rep = self.me, self.rep
        if not self.ways:
            at = self.weights.at[pl.ds(me * self.rows, self.rows)]
            self.own = pltpu.make_async_copy(pack.at[me % TEAM], at, self.local)
            self.own.start()
        started = len(self.ways)
        number = len(self.order) - started if number is None else number
        for other in self.order[started : started + number]:
            where = across(me, other)
            source = pack.at[where % TEAM, pl.ds(rep * self.half, self.half)]
            self.ways[other] = self.send(source, self.place(me), {"dp": where})

    def forward(self, number=None):
        done = len(self.swaps)
        number = len(self.order) - done if number is None else number
        for other in self.turns[done : done + number]:
            self.ways[other].wait_recv()
            at = self.place(across(self.me, other))
            self.swaps.append(self.send_x(at, at, {"rep": 1 - self.rep}))

    def finish(self):
        for copy in self.ways.values():
            copy.wait_send()
        for copy in self.swaps + [self.own]:
            copy.wait()


def attend_unit(values, cosine, sine, bias, share):
    depth = HEAD_DIM
    parts = []
    for p in range(2):
        turned = []
        for at in range(p * share, (p + 1) * share, depth):
            head = values[:, at : at + depth]
            turned.append((head * cosine + pltpu.roll(head, depth // 2, 1) * sine).astype(LOW))
        parts.append(turned)
    query, keys = parts
    value = [
        values[:, at : at + depth].astype(LOW) for at in range(2 * share, 3 * share, depth)
    ]
    mixed = []
    for one, two, three in zip(query, keys, value):
        scores = dot(one, two, CONTRACT_LAST) * depth ** (-0.5) + bias
        powers = jnp.exp(scores - jnp.max(scores, axis=1, keepdims=True))
        prob = powers / jnp.sum(powers, axis=1, keepdims=True)
        mixed.append(dot(prob.astype(LOW), three).astype(LOW))
    return jnp.concatenate(query + keys + value, axis=1), jnp.concatenate(mixed, axis=1)


def forward_kernel(
    ranks,
    flat,
    normed_own,
    cot,
    att_pack,
    mlp_master,
    cosine,
    sine,
    bias,
    normed_all,
    cot_all,
    att_weights,
    gate_weights,
    down_weights,
    gate_pack,
    down_pack,
    projected_all,
    mixed_all,
    resid,
    normed_two_all,
    gate_all,
    up_all,
    hidden_all,
    att,
    gate,
    block,
    odd,
    own,
    got,
    edge,
    normed,
    *sems,
):
    sent_team, came_team, sent_rows, came_rows, sent_x, came_x, first_sent, first_came, local = sems
    me = lax.axis_index("dp")
    rep = lax.axis_index("rep")
    rows, share = att_pack.shape[1], att_pack.shape[2] // 4
    hid = gate_pack.shape[2] // 2
    core = {"dp": flip(me, 1)}
    greet(me, range(1, ranks), True)
    send = Sender(sent_team, came_team)
    send_rows = Sender(sent_rows, came_rows)
    send_x = Sender(sent_x, came_x)
    tokens = TeamGather(me, normed_own, normed_all, send, SPLIT_TOKENS)
    tokens.begin()
    gathers = [
        RowGather(ranks, me, rep, weights, send_rows, send_x, local.at[i])
        for i, weights in enumerate((att_weights, gate_weights, down_weights))
    ]
    gathers[0].begin(att_pack)
    keep = [pltpu.make_async_copy(normed_own, normed_all.at[0], local.at[3])]
    keep.append(pltpu.make_async_copy(cot, cot_all.at[0], local.at[4]))
    for copy in keep:
        copy.start()

    def pack(wide, low):
        def loads(t, slot):
            return [
                pltpu.make_async_copy(
                    mlp_master.at[:, rows_at(p * TEAM + t, hid)],
                    wide.at[slot, p],
                    local.at[5 + 3 * slot + p],
                )
                for p in range(3)
            ]

        def stores(t, slot):
            near = low.at[slot]
            return [
                pltpu.make_async_copy(
                    near.at[:, pl.ds(0, 2 * hid)], gate_pack.at[t], local.at[11 + slot]
                ),
                pltpu.make_async_copy(
                    near.at[:, pl.ds(2 * hid, hid)], down_pack.at[t], local.at[13 + slot]
                ),
            ]

        def body(t, slot):
            for p in range(3):
                low[slot, :, p * hid : (p + 1) * hid] = wide[slot, p].astype(LOW)

        stream_out(TEAM, loads, stores, body)

    pl.run_scoped(
        pack, pltpu.VMEM((2, 3, rows, hid), FULL), pltpu.VMEM((2, rows, 3 * hid), LOW)
    )
    tokens.turn()
    gathers[1].begin(gate_pack)
    gathers[0].forward()
    tokens.finish()
    gathers[0].finish()
    for copy in keep:
        copy.wait()
    load = pltpu.make_async_copy(att_weights, att, local.at[0])
    load.start()
    load.wait()

    def fetch(step, slot):
        return pltpu.make_async_copy(
            normed_all.at[unit_of(step)], block.at[slot], local.at[5 + slot]
        )

    fetch(0, 0).start()

    @pl.loop(0, TEAM)
    def _(step):
        slot = step % 2
        unit = unit_of(step)

        @pl.when(step + 1 < TEAM)
        def _():
            fetch(step + 1, 1 - slot).start()

        fetch(step, slot).wait()
        values = dot(block[slot], att[:, : 3 * share])
        projected, mixed = attend_unit(values, cosine[unit], sine[unit], bias[unit], share)
        projected_all[unit] = projected
        mixed_all[unit] = mixed
        term = dot(mixed, att[:, 3 * share :], CONTRACT_LAST).astype(LOW)
        j = unit // 2

        @pl.when(step < TEAM // 2)
        def _():
            odd[j] = term
            pltpu.make_async_remote_copy(
                src_ref=odd.at[j],
                dst_ref=got.at[j],
                send_sem=first_sent.at[j],
                recv_sem=first_came.at[j],
                device_id=core,
                device_id_type=MESH,
            ).start()

        @pl.when(step >= TEAM // 2)
        def _():
            own[j] = term

    first = [
        pltpu.make_async_remote_copy(
            src_ref=odd.at[j],
            dst_ref=got.at[j],
            send_sem=first_sent.at[j],
            recv_sem=first_came.at[j],
            device_id=core,
            device_id_type=MESH,
        )
        for j in range(TEAM // 2)
    ]

    def total(start, value):
        at = pl.ds(start, STRIP)
        value = value + flat[at].astype(FULL)
        resid[at] = value
        normed[at] = strip_normalize(value)[0].astype(LOW)

    steps = sum_steps(me, own, got, edge, first, send, total, SPLIT_ATTENDED * UNIT // PIECES)
    next(steps)
    early = len(gathers[2].order) // 2
    gathers[2].begin(down_pack, early)
    gathers[1].forward()
    next(steps)
    for _ in steps:
        pass
    tokens = TeamGather(me, normed, normed_two_all, send, SPLIT_NORMED)
    tokens.begin()
    gathers[2].begin(down_pack)
    cots = TeamGather(me, cot, cot_all, send, SPLIT_COT)
    cots.begin()
    keep = pltpu.make_async_copy(normed, normed_two_all.at[0], local.at[3])
    keep.start()
    gathers[2].forward(early)
    tokens.turn()
    keep.wait()
    gathers[1].finish()
    tokens.settle()
    load = pltpu.make_async_copy(gate_weights, gate, local.at[1])
    load.start()
    load.wait()

    def feed(base, low):
        def loads(step, slot):
            source = normed_two_all.at[base + step]
            return [pltpu.make_async_copy(source, block.at[slot], local.at[5 + slot])]

        def stores(step, slot):
            return [
                pltpu.make_async_copy(
                    low.at[slot, i], out.at[base + step], local.at[7 + 3 * slot + i]
                )
                for i, out in enumerate((gate_all, up_all, hidden_all))
            ]

        def body(step, slot):
            @pl.loop(0, hid // UNIT)
            def _(column):
                at = rows_at(column, UNIT)
                later = pl.ds(pl.multiple_of(hid + column * UNIT, UNIT), UNIT)
                gate_value = dot(block[slot], gate[:, at])
                up_value = dot(block[slot], gate[:, later])
                low[slot, 0, :, at] = gate_value.astype(LOW)
                low[slot, 1, :, at] = up_value.astype(LOW)
                hidden = gate_value * jax.nn.sigmoid(gate_value) * up_value
                low[slot, 2, :, at] = hidden.astype(LOW)

        stream_out(FEED_EARLY if base == 0 else TEAM - FEED_EARLY, loads, stores, body)

    fed = pltpu.VMEM((2, 3, normed.shape[0], hid), LOW)
    pl.run_scoped(functools.partial(feed, 0), fed)
    tokens.finish()
    cots.turn()
    gathers[2].forward()
    pl.run_scoped(functools.partial(feed, FEED_EARLY), fed)
    cots.finish()
    gathers[2].finish()


def forward_layer(ranks, flat, normed, cot, att_pack, mlp_master, cosine, sine, bias):
    count, width = normed.shape
    rows, share = att_pack.shape[1], att_pack.shape[2] // 4
    hid = mlp_master.shape[1] // (3 * TEAM)
    gathered = jax.ShapeDtypeStruct((TEAM, count, width), LOW)
    hidden = jax.ShapeDtypeStruct((TEAM, count, hid), LOW)
    vmem = pl.BlockSpec(memory_space=pltpu.VMEM)

    def weights(columns):
        return jax.ShapeDtypeStruct((ranks * rows, columns), LOW)

    def packs(columns):
        return jax.ShapeDtypeStruct((TEAM, rows, columns), LOW)

    out = [
        (gathered, ANYWHERE),
        (gathered, ANYWHERE),
        (weights(4 * share), ANYWHERE),
        (weights(2 * hid), ANYWHERE),
        (weights(hid), ANYWHERE),
        (packs(2 * hid), ANYWHERE),
        (packs(hid), ANYWHERE),
        (jax.ShapeDtypeStruct((TEAM, count, 3 * share), LOW), vmem),
        (jax.ShapeDtypeStruct((TEAM, count, share), LOW), vmem),
        (jax.ShapeDtypeStruct((count, width), FULL), vmem),
        (gathered, ANYWHERE),
        (hidden, ANYWHERE),
        (hidden, ANYWHERE),
        (hidden, ANYWHERE),
    ]
    team_copies = 3 * GATHER_COPIES + SUM_COPIES
    pairs = [team_copies] * 2 + [3 * (ranks - 1)] * 4 + [TEAM // 2] * 2 + [15]
    return pl.pallas_call(
        functools.partial(forward_kernel, ranks),
        out_shape=[shape for shape, _ in out],
        in_specs=[vmem] + [ANYWHERE] * 4 + [vmem] * 3,
        out_specs=[spec for _, spec in out],
        scratch_shapes=[
            pltpu.VMEM((ranks * rows, 4 * share), LOW),
            pltpu.VMEM((ranks * rows, 2 * hid), LOW),
            pltpu.VMEM((2, count, width), LOW),
            pltpu.VMEM((TEAM // 2, count, width), LOW),
            pltpu.VMEM((TEAM // 2, count, width), LOW),
            pltpu.VMEM((TEAM // 2, count, width), LOW),
            pltpu.VMEM((3, count, width), LOW),
            pltpu.VMEM((count, width), LOW),
        ]
        + [pltpu.SemaphoreType.DMA((number,)) for number in pairs],
        compiler_params=params(0),
        name="forward_layer",
    )(flat, normed, cot, att_pack, mlp_master, cosine, sine, bias)


def attend_unit_back(values, given, cosine, sine, bias, share):
    depth = HEAD_DIM
    scale = depth ** (-0.5)
    grads = ([], [], [])
    for at in range(0, share, depth):
        query, keys, value = (values[:, p * share + at : p * share + at + depth] for p in range(3))
        grad = given[:, at : at + depth]
        scores = dot(query, keys, CONTRACT_LAST) * scale + bias
        powers = jnp.exp(scores - jnp.max(scores, axis=1, keepdims=True))
        prob = powers / jnp.sum(powers, axis=1, keepdims=True)
        grad_prob = dot(grad, value, CONTRACT_LAST)
        grad_value = dot(prob.astype(LOW), grad, CONTRACT_FIRST)
        along = jnp.sum(grad_prob * prob, axis=1, keepdims=True)
        grad_scores = (prob * (grad_prob - along)).astype(LOW)
        turned = (
            dot(grad_scores, keys) * scale,
            dot(grad_scores, query, CONTRACT_FIRST) * scale,
        )
        for p in range(2):
            back = turned[p] * cosine - pltpu.roll(turned[p], depth // 2, 1) * sine
            grads[p].append(back.astype(LOW))
        grads[2].append(grad_value.astype(LOW))
    return jnp.concatenate(grads[0] + grads[1] + grads[2], axis=1)


class Terms:
    def __init__(self, me, odd, own, got, sent, came):
        self.odd, self.own, self.got, self.sent, self.came = odd, own, got, sent, came
        self.core = {"dp": flip(me, 1)}

    def copy(self, j):
        return pltpu.make_async_remote_copy(
            src_ref=self.odd.at[j],
            dst_ref=self.got.at[j],
            send_sem=self.sent.at[j],
            recv_sem=self.came.at[j],
            device_id=self.core,
            device_id_type=MESH,
        )

    def put(self, step, term):
        j = unit_of(step) // 2

        @pl.when(step < TEAM // 2)
        def _():
            self.odd[j] = term
            self.copy(j).start()

        @pl.when(step >= TEAM // 2)
        def _():
            self.own[j] = term

    def first(self):
        return [self.copy(j) for j in range(TEAM // 2)]


LOWS = (0, 4, 2, 6, 1, 5, 3, 7)


def backward_kernel(
    ranks,
    flat,
    resid,
    cot,
    cosine,
    sine,
    bias,
    cot_all,
    hidden_all,
    gate_all,
    up_all,
    normed_two_all,
    normed_one_all,
    projected_all,
    mixed_all,
    att_weights,
    gate_weights,
    down_weights,
    mlp_master,
    mlp_first,
    mlp_second,
    out_tokens,
    grad_tokens,
    got_att,
    got_gate,
    got_down,
    mlp_diff,
    mlp_other,
    grad_all,
    att_grad,
    gate_grad,
    down_grad,
    fed_all,
    own,
    got,
    edge,
    odd,
    own_two,
    got_two,
    edge_two,
    grad_low,
    grad_resid,
    stage,
    wide,
    sent,
    came,
    sent_rows,
    came_rows,
    sent_first,
    came_first,
    sent_x,
    came_x,
    kept,
    local,
):
    me = lax.axis_index("dp")
    rep = lax.axis_index("rep")
    tops = ranks // TEAM
    rows = got_att.shape[1]
    share = mixed_all.shape[1]
    hid = hidden_all.shape[1]
    count, width = resid.shape
    tokens = TEAM * count
    tiles = width // UNIT
    greet(me, range(1, ranks), True)
    send = Sender(sent, came)
    order = []
    for low_bits in LOWS:
        order += [top * TEAM + low_bits for top in range(1, tops)]
        order += [low_bits] if low_bits else []

    chunks = ((down_grad, got_down), (gate_grad, got_gate), (att_grad, got_att))

    def block_copy(chunk, other):
        grad, target = chunks[chunk]
        index = chunk * (ranks - 1) + other - 1
        where = across(me, other)
        return pltpu.make_async_remote_copy(
            src_ref=grad.at[pl.ds(where * rows, rows)],
            dst_ref=target.at[me],
            send_sem=sent_rows.at[index],
            recv_sem=came_rows.at[index],
            device_id={"dp": where},
            device_id_type=MESH,
        )

    def keep_own(grad, target, index):
        copy = pltpu.make_async_copy(
            grad.at[pl.ds(me * rows, rows)], target.at[me], kept.at[index]
        )
        copy.start()
        return copy

    def down_phase(hidden, tile, low):
        whole = pltpu.make_async_copy(hidden_all, hidden, local.at[0])
        whole.start()

        def loads(step, slot):
            at = rows_at(step, UNIT)
            return [pltpu.make_async_copy(cot_all.at[:, at], tile.at[slot], local.at[2 + slot])]

        def stores(step, slot):
            at = rows_at(step, UNIT)
            return [pltpu.make_async_copy(low.at[slot], down_grad.at[at], local.at[4 + slot])]

        def body(step, slot):
            low[slot] = dot(tile[slot], hidden[...], CONTRACT_FIRST).astype(LOW)

        whole.wait()
        stream_out(tiles, loads, stores, body)

    pl.run_scoped(
        down_phase,
        pltpu.VMEM((tokens, hid), LOW),
        pltpu.VMEM((2, tokens, UNIT), LOW),
        pltpu.VMEM((2, UNIT, hid), LOW),
    )
    for other in order:
        block_copy(0, other).start()
    own_copies = [keep_own(down_grad, got_down, 0)]

    gate_order = list(order)

    def more(number):
        for _ in range(min(number, len(gate_order))):
            block_copy(1, gate_order.pop(0)).start()

    terms = Terms(me, odd, own, got, sent_first.at[0], came_first.at[0])

    grad_gate = wide.at[pl.ds(0, tokens), pl.ds(0, 2 * hid)]

    def hidden_phase(down, block, gate, up):
        whole = pltpu.make_async_copy(down_weights, down, local.at[1])
        whole.start()

        def loads(step, slot):
            at = rows_at(step, count)
            return [
                pltpu.make_async_copy(cot_all.at[at], block.at[slot], local.at[2 + slot]),
                pltpu.make_async_copy(gate_all.at[at], gate.at[slot], local.at[4 + slot]),
                pltpu.make_async_copy(up_all.at[at], up.at[slot], local.at[6 + slot]),
            ]

        def body(step, slot):
            at = rows_at(step, count)

            @pl.loop(0, hid // UNIT)
            def _(column):
                place = rows_at(column, UNIT)
                later = pl.ds(pl.multiple_of(hid + column * UNIT, UNIT), UNIT)
                grad = dot(block[slot], down[:, place])
                value = gate[slot, :, place].astype(FULL)
                sigmoid = jax.nn.sigmoid(value)
                slope = sigmoid * (1.0 + value * (1.0 - sigmoid))
                up_value = up[slot, :, place].astype(FULL)
                grad_gate[at, place] = (grad * up_value * slope).astype(LOW)
                grad_gate[at, later] = (grad * value * sigmoid).astype(LOW)

        whole.wait()
        stream(TEAM, loads, body)

    pl.run_scoped(
        hidden_phase,
        pltpu.VMEM((width, hid), LOW),
        pltpu.VMEM((2, count, width), LOW),
        pltpu.VMEM((2, count, hid), LOW),
        pltpu.VMEM((2, count, hid), LOW),
    )

    def back_phase(gate):
        whole = pltpu.make_async_copy(gate_weights, gate, local.at[0])
        whole.start()
        whole.wait()

        @pl.loop(0, TEAM)
        def _(step):
            at = rows_at(unit_of(step), count)
            terms.put(step, dot(grad_gate[at, :], gate[...], CONTRACT_LAST).astype(LOW))

    pl.run_scoped(back_phase, pltpu.VMEM((width, 2 * hid), LOW))

    def weight_phase(tile, low):
        def loads(step, slot):
            at = rows_at(step, UNIT)
            return [
                pltpu.make_async_copy(
                    normed_two_all.at[:, at], tile.at[slot], local.at[2 + slot]
                )
            ]

        def stores(step, slot):
            at = rows_at(step, UNIT)
            return [pltpu.make_async_copy(low.at[slot], gate_grad.at[at], local.at[4 + slot])]

        def body(step, slot):
            low[slot] = dot(tile[slot], grad_gate[...], CONTRACT_FIRST).astype(LOW)

        stream_out(tiles, loads, stores, body)


    def resid_total(start, value):
        at = pl.ds(start, STRIP)
        normed, factor = strip_normalize(resid[at])
        along = jnp.sum(value * normed, axis=1, keepdims=True) * (1.0 / width)
        middle = jnp.sum(value, axis=1, keepdims=True) * (1.0 / width)
        value = cot[at].astype(FULL) + factor * (value - middle - normed * along)
        grad_resid[at] = value
        grad_low[at] = value.astype(LOW)

    split = SPLIT_BACK * UNIT // PIECES
    steps = sum_steps(me, own, got, edge, terms.first(), send, resid_total, split)
    next(steps)
    pl.run_scoped(
        weight_phase, pltpu.VMEM((2, tokens, UNIT), LOW), pltpu.VMEM((2, UNIT, 2 * hid), LOW)
    )
    own_copies.append(keep_own(gate_grad, got_gate, 1))
    more(GATE_FIRST)
    next(steps)
    more(GATE_LATE)
    for _ in steps:
        pass
    gather = TeamGather(me, grad_low, grad_all, send, SPLIT_BACK)
    gather.begin()
    more(GATE_GATHER)
    keep = pltpu.make_async_copy(grad_low, grad_all.at[0], local.at[8])
    keep.start()
    def fed_phase(hidden, down, term):
        whole = [
            pltpu.make_async_copy(hidden_all, hidden, local.at[0]),
            pltpu.make_async_copy(down_weights, down, local.at[1]),
        ]
        for copy in whole:
            copy.start()
        for copy in whole:
            copy.wait()

        def fed_stores(step, slot):
            return [pltpu.make_async_copy(term.at[slot], fed_all.at[step], local.at[6 + slot])]

        def fed_body(step, slot):
            term[slot] = dot(hidden[rows_at(step, count)], down[...], CONTRACT_LAST).astype(LOW)

        stream_out(TEAM, lambda step, slot: [], fed_stores, fed_body)

    pl.run_scoped(
        fed_phase,
        pltpu.VMEM((tokens, hid), LOW),
        pltpu.VMEM((width, hid), LOW),
        pltpu.VMEM((2, count, width), LOW),
    )
    gather.turn()
    more(len(gate_order))
    gather.finish()
    keep.wait()

    terms = Terms(me, odd, own, got, sent_first.at[1], came_first.at[1])

    def att_phase():
        att = wide.at[pl.ds(0, width), pl.ds(0, 4 * share)]
        grad_projected = wide.at[pl.ds(0, tokens), pl.ds(4 * share, 3 * share)]

        def unit_phase(block, projected, tables, mask):
            def loads(step, slot):
                unit = unit_of(step)
                return [
                    pltpu.make_async_copy(grad_all.at[unit], block.at[slot], local.at[slot]),
                    pltpu.make_async_copy(
                        projected_all.at[unit], projected.at[slot], local.at[2 + slot]
                    ),
                    pltpu.make_async_copy(cosine.at[unit], tables.at[slot, 0], local.at[4 + slot]),
                    pltpu.make_async_copy(sine.at[unit], tables.at[slot, 1], local.at[6 + slot]),
                    pltpu.make_async_copy(bias.at[unit], mask.at[slot], local.at[8 + slot]),
                ]

            def body(step, slot):
                given = dot(block[slot], att[:, 3 * share :]).astype(LOW)
                grads = attend_unit_back(
                    projected[slot], given, tables[slot, 0], tables[slot, 1], mask[slot], share
                )
                grad_projected[rows_at(unit_of(step), count), :] = grads
                terms.put(step, dot(grads, att[:, : 3 * share], CONTRACT_LAST).astype(LOW))

            whole = pltpu.make_async_copy(att_weights, att, local.at[10])
            whole.start()
            whole.wait()
            stream(TEAM, loads, body)

        pl.run_scoped(
            unit_phase,
            pltpu.VMEM((2, count, width), LOW),
            pltpu.VMEM((2, count, 3 * share), LOW),
            pltpu.VMEM((2, 2, count, HEAD_DIM), FULL),
            pltpu.VMEM((2, count, count), FULL),
        )

        def weight_phase(normed, grad, mixed, low):
            def loads(step, slot):
                at = rows_at(step, UNIT)
                return [
                    pltpu.make_async_copy(
                        normed_one_all.at[:, at], normed.at[slot], local.at[slot]
                    ),
                    pltpu.make_async_copy(
                        grad_all.at[:, :, at], grad.at[slot], local.at[2 + slot]
                    ),
                ]

            def stores(step, slot):
                at = rows_at(step, UNIT)
                return [pltpu.make_async_copy(low.at[slot], att_grad.at[at], local.at[4 + slot])]

            def body(step, slot):
                left = normed[slot]
                low[slot, :, : 3 * share] = dot(left, grad_projected[...], CONTRACT_FIRST).astype(LOW)
                left = grad[slot].reshape(tokens, UNIT)
                low[slot, :, 3 * share :] = dot(left, mixed[...], CONTRACT_FIRST).astype(LOW)

            whole = pltpu.make_async_copy(mixed_all, mixed, local.at[10])
            whole.start()
            whole.wait()
            stream_out(tiles, loads, stores, body)

        pl.run_scoped(
            weight_phase,
            pltpu.VMEM((2, tokens, UNIT), LOW),
            pltpu.VMEM((2, TEAM, count, UNIT), LOW),
            pltpu.VMEM((tokens, share), LOW),
            pltpu.VMEM((2, UNIT, 4 * share), LOW),
        )

    att_phase()
    for other in order:
        block_copy(2, other).start()
    own_copies.append(keep_own(att_grad, got_att, 2))

    def mate_at(low):
        mate = 0
        for bit in BITS:
            mine, its = (me // bit) % 2, (low // bit) % 2
            mate = mate + bit * (mine + its - 2 * mine * its)
        return mate

    def differ(chunk, parts, first_part, base):
        source = chunks[chunk][1]

        def low_at(step):
            turn = step // parts
            return 4 * (turn % 2) + 2 * ((turn // 2) % 2) + turn // 4

        def column(step):
            return rows_at((first_part + step % parts) * TEAM + mate_at(low_at(step)), hid)

        def near(step):
            at = column(step)
            return pltpu.make_async_copy(
                stage.at[step % 2], mlp_diff.at[:, at], kept.at[3 + step % 2]
            )

        def far(step):
            at = column(step)
            return pltpu.make_async_remote_copy(
                src_ref=mlp_diff.at[:, at],
                dst_ref=mlp_other.at[:, at],
                send_sem=sent_x.at[base + step],
                recv_sem=came_x.at[base + step],
                device_id={"rep": 1 - rep},
                device_id_type=MESH,
            )

        def arrive(step):
            low = low_at(step)

            @pl.when(step % parts == 0)
            def _():
                for top in range(tops):
                    index = chunk * (ranks - 1) + top * TEAM + low - 1

                    def wait():
                        pltpu.make_async_remote_copy(
                            src_ref=source.at[me],
                            dst_ref=source.at[me],
                            send_sem=sent_rows.at[index],
                            recv_sem=came_rows.at[index],
                            device_id={"dp": flip(me, 1)},
                            device_id_type=MESH,
                        ).wait_recv()

                    if top:
                        wait()
                    else:
                        pl.when(low > 0)(wait)
                        pl.when(low == 0)(own_copies[chunk].wait)

        def run(big, low):
            def loads(step, slot):
                at = column(step)
                mate = mate_at(low_at(step))
                part = rows_at(step % parts, hid)
                return [
                    pltpu.make_async_copy(mlp_master.at[:, at], big.at[slot, 0], local.at[slot]),
                    pltpu.make_async_copy(mlp_first.at[0, :, at], big.at[slot, 1], local.at[2 + slot]),
                    pltpu.make_async_copy(mlp_second.at[0, :, at], big.at[slot, 2], local.at[4 + slot]),
                ] + [
                    pltpu.make_async_copy(
                        source.at[top * TEAM + mate, :, part],
                        low.at[slot, top],
                        local.at[6 + slot + 2 * top],
                    )
                    for top in range(tops)
                ]

            def body(step, slot):
                @pl.loop(0, rows // STRIP)
                def _(strip):
                    at = pl.ds(strip * STRIP, STRIP)
                    grad = low[slot, 0, at].astype(FULL)
                    for top in range(1, tops):
                        grad = grad + low[slot, top, at].astype(FULL)
                    value = big[slot, 0, at]
                    inner, _, _ = adam_step(value, grad, big[slot, 1, at], big[slot, 2, at])
                    stage[slot, at] = (value - inner).astype(LOW)

                near(step).start()

                @pl.when(step > 0)
                def _():
                    near(step - 1).wait()
                    far(step - 1).start()

            steps = parts * TEAM
            stream(steps, loads, body, arrive)
            near(steps - 1).wait()
            far(steps - 1).start()

        pl.run_scoped(
            run, pltpu.VMEM((2, 3, rows, hid), FULL), pltpu.VMEM((2, tops, rows, hid), LOW)
        )

        def finish():
            @pl.loop(0, parts * TEAM)
            def _(step):
                far(step).wait()

        return finish

    def tokens_total(start, value):
        at = pl.ds(start, STRIP)
        normed, factor = strip_normalize(flat[at].astype(FULL))
        along = jnp.sum(value * normed, axis=1, keepdims=True) * (1.0 / width)
        middle = jnp.sum(value, axis=1, keepdims=True) * (1.0 / width)
        grad_tokens[at] = grad_resid[at] + factor * (value - middle - normed * along)

    def out_total(start, value):
        at = pl.ds(start, STRIP)
        out_tokens[at] = (resid[at] + value).astype(LOW)

    waits = [differ(0, 1, 2, 0)]
    one = sum_steps(me, own, got, edge, terms.first(), send, tokens_total, split)
    two = team_sum(
        me, fed_all, own_two, got_two, edge_two, send, local, out_total, split
    )
    next(one)
    next(two)
    waits.append(differ(1, 2, 0, TEAM))
    for _ in range(2):
        for steps in (one, two):
            next(steps, None)
    own_copies[2].wait()
    for other in order:
        block_copy(2, other).wait_recv()
    for chunk in range(3):
        for other in order:
            block_copy(chunk, other).wait_send()
    for wait in waits:
        wait()


GATE_FIRST, GATE_LATE, GATE_GATHER = 0, 1, 2


def backward_layer(ranks, tokens, mlp, *rest):
    flat, resid, cot = tokens
    hidden_all, projected_all, gate_weights = rest[4], rest[9], rest[12]
    count, width = flat.shape
    all_tokens, hid = hidden_all.shape
    share = projected_all.shape[2] // 3
    rows = width // ranks
    vmem = pl.BlockSpec(memory_space=pltpu.VMEM)
    low = functools.partial(jax.ShapeDtypeStruct, dtype=LOW)
    out = [
        (low((count, width)), vmem),
        (jax.ShapeDtypeStruct((count, width), FULL), vmem),
        (low((ranks, rows, 4 * share)), ANYWHERE),
        (low((ranks, rows, 2 * hid)), ANYWHERE),
        (low((ranks, rows, hid)), ANYWHERE),
        (low(mlp[0].shape), ANYWHERE),
        (low(mlp[0].shape), ANYWHERE),
        (low((TEAM, count, width)), ANYWHERE),
        (low((width, 4 * share)), ANYWHERE),
        (low((width, 2 * hid)), ANYWHERE),
        (low((width, hid)), ANYWHERE),
        (low((TEAM, count, width)), ANYWHERE),
    ]
    team_copies = GATHER_COPIES + 2 * SUM_COPIES + SUM_COPIES + TEAM // 2
    locals_needed = 6 + 2 * (ranks // TEAM) * (hid // share) + 2
    sems = [team_copies] * 2 + [3 * (ranks - 1)] * 2
    return pl.pallas_call(
        functools.partial(backward_kernel, ranks),
        out_shape=[shape for shape, _ in out],
        in_specs=[vmem] * 3 + [ANYWHERE] * (len(rest) + 3),
        out_specs=[spec for _, spec in out],
        scratch_shapes=sum_scratch(count, width)
        + [pltpu.VMEM((TEAM // 2, count, width), LOW)]
        + sum_scratch(count, width)
        + [
            pltpu.VMEM((count, width), LOW),
            pltpu.VMEM((count, width), FULL),
            pltpu.VMEM((2, rows, hid), LOW),
            pltpu.VMEM((max(width, all_tokens), max(2 * hid, 7 * share)), LOW),
        ]
        + [pltpu.SemaphoreType.DMA((number,)) for number in sems]
        + [pltpu.SemaphoreType.DMA((2, TEAM // 2))] * 2
        + [pltpu.SemaphoreType.DMA((3 * TEAM,))] * 2
        + [
            pltpu.SemaphoreType.DMA((3 + TEAM,)),
            pltpu.SemaphoreType.DMA((max(locals_needed, 12),)),
        ],
        compiler_params=params(2),
        name="backward_layer",
    )(flat, resid, cot, *rest, *mlp)


def pack_kernel(*refs):
    share = refs[0].shape[1]
    for p, ref in enumerate(refs[:-1]):
        refs[-1][0, :, p * share : (p + 1) * share] = ref[...].astype(LOW)


def pack_shares(master, bases, share):
    rows = master.shape[0]
    return pl.pallas_call(
        pack_kernel,
        grid=(TEAM,),
        out_shape=jax.ShapeDtypeStruct((TEAM, rows, len(bases) * share), LOW),
        in_specs=[
            pl.BlockSpec((rows, share), lambda i, base=base: (0, base + i)) for base in bases
        ],
        out_specs=pl.BlockSpec((1, rows, len(bases) * share), lambda i: (i, 0, 0)),
        name="pack_shares",
    )(*[master] * len(bases))


LANES = 1024


def finish_kernel(reps, share, grads, master, first, second, outer, diff, other, *refs):
    first_new, second_new, mean_out, new, outer_new = refs[-5:]
    for t in range(grads.shape[1]):
        at = slice(t * share, (t + 1) * share)
        grad = grads[0, t].astype(FULL)
        for top in range(1, grads.shape[0]):
            grad = grad + grads[top, t].astype(FULL)
        first_new[0, :, at] = BETA_ONE * first[0, :, at] + (1.0 - BETA_ONE) * grad
        second_new[0, :, at] = BETA_TWO * second[0, :, at] + (1.0 - BETA_TWO) * grad * grad
    mean = (diff[...].astype(FULL) + other[...].astype(FULL)) / reps
    mean_out[...] = mean
    new[...], outer_new[...] = outer_step(master[...], mean, outer[...])


def finish_chunk(reps, grads, master, first, second, outer, diff, other, bases, written):
    ranks, rows, columns = grads.shape
    parts = len(bases)
    share = columns // parts
    lanes = max(LANES, share)
    per = lanes // share
    steps = TEAM // per

    def column(p, t):
        place = bases[0]
        for q in range(1, parts):
            place = place + jnp.where(p >= q, bases[q] - bases[q - 1], 0)
        return place * steps + t

    grad = pl.BlockSpec((ranks // TEAM, per, rows, share), lambda p, t: (0, t, 0, p))
    wide = pl.BlockSpec((1, rows, lanes), lambda p, t: (0, 0, column(p, t)))
    flat = pl.BlockSpec((rows, lanes), lambda p, t: (0, column(p, t)))
    extra = [] if written is None else list(written)
    state = jax.ShapeDtypeStruct(first.shape, FULL)
    plain = jax.ShapeDtypeStruct(master.shape, FULL)
    return pl.pallas_call(
        functools.partial(finish_kernel, reps, share),
        grid=(parts, steps),
        out_shape=[state, state, plain, plain, plain],
        in_specs=[grad, flat, wide, wide, flat, flat, flat] + [ANYWHERE] * len(extra),
        out_specs=[wide, wide, flat, flat, flat],
        input_output_aliases={7 + i: i for i in range(len(extra))},
        compiler_params=pltpu.CompilerParams(vmem_limit_bytes=VMEM_BYTES),
        name="finish_chunk",
    )(
        grads.reshape(ranks // TEAM, TEAM, rows, columns),
        master, first, second, outer, diff, other, *extra,
    )


def adam_kernel(share, grad, master, first, second, *refs):
    first_new, second_new, diff = refs[-3:]
    for t in range(grad.shape[1]):
        at = slice(t * share, (t + 1) * share)
        gradient = grad[0, t].astype(FULL)
        for top in range(1, grad.shape[0]):
            gradient = gradient + grad[top, t].astype(FULL)
        inner, first_new[0, :, at], second_new[0, :, at] = adam_step(
            master[:, at], gradient, first[0, :, at], second[0, :, at]
        )
        diff[:, at] = (master[:, at] - inner).astype(LOW)


def chunk_specs(tops, rows, bases, share, lanes):
    per = lanes // share
    steps = TEAM // per
    parts = len(bases)

    def column(p, t):
        place = bases[0]
        for q in range(1, parts):
            place = place + jnp.where(p >= q, bases[q] - bases[q - 1], 0)
        return place * steps + t

    return (
        (parts, steps),
        pl.BlockSpec((tops, per, rows, share), lambda p, t: (0, t, 0, p)),
        pl.BlockSpec((1, rows, lanes), lambda p, t: (0, 0, column(p, t))),
        pl.BlockSpec((rows, lanes), lambda p, t: (0, column(p, t))),
        pl.BlockSpec((rows, lanes), lambda p, t: (0, p * steps + t)),
    )


def adam_chunk(grads, master, first, second, bases):
    ranks, rows, columns = grads.shape
    share = columns // len(bases)
    tops = ranks // TEAM
    grid, grad, wide, flat, packed = chunk_specs(tops, rows, bases, share, max(LANES, share))
    state = jax.ShapeDtypeStruct(first.shape, FULL)
    return pl.pallas_call(
        functools.partial(adam_kernel, share),
        grid=grid,
        out_shape=[
            state,
            state,
            jax.ShapeDtypeStruct((rows, TEAM * len(bases) * share), LOW),
        ],
        in_specs=[grad, flat, wide, wide],
        out_specs=[wide, wide, packed],
        compiler_params=pltpu.CompilerParams(vmem_limit_bytes=VMEM_BYTES),
        name="adam_chunk",
    )(grads.reshape(tops, TEAM, rows, columns), master, first, second)


def outer_kernel(reps, diff, other, master, momentum, *refs):
    mean_out, new, momentum_new = refs[-3:]
    mean = (diff[...].astype(FULL) + other[...].astype(FULL)) / reps
    mean_out[...] = mean
    new[...], momentum_new[...] = outer_step(master[...], mean, momentum[...])


def outer_chunk(reps, diff, other, master, momentum, bases):
    rows = master.shape[0]
    share = diff.shape[1] // (TEAM * len(bases))
    grid, _, _, flat, packed = chunk_specs(1, rows, bases, share, max(LANES, share))
    return pl.pallas_call(
        functools.partial(outer_kernel, reps),
        grid=grid,
        out_shape=[jax.ShapeDtypeStruct(master.shape, FULL)] * 3,
        in_specs=[packed, packed, flat, flat],
        out_specs=[flat] * 3,
        compiler_params=pltpu.CompilerParams(vmem_limit_bytes=VMEM_BYTES),
        name="outer_chunk",
    )(diff, other, master, momentum)


def on_device(
    reps,
    ranks,
    tokens,
    cotangent,
    branch,
    att_master,
    att_first,
    att_second,
    att_outer,
    mlp_master,
    mlp_first,
    mlp_second,
    mlp_outer,
):
    units, length, width = tokens.shape
    hidden_width = mlp_master.shape[1] // 3
    depth = HEAD_DIM
    count = units * length
    rows = att_master.shape[0]
    team = TEAM
    tops = ranks // team
    all_tokens = team * count
    att_share = width // team
    hid_share = hidden_width // team
    me = lax.axis_index("dp")
    rep = lax.axis_index("rep")
    top = me // team

    def hop(values, other):
        pairs = [(r * ranks + i, r * ranks + (i ^ other)) for r in range(reps) for i in range(ranks)]
        return lax.ppermute(values, ("rep", "dp"), pairs)

    def swap(values):
        pairs = [(r * ranks + i, (1 - r) * ranks + i) for r in range(reps) for i in range(ranks)]
        return lax.ppermute(values, ("rep", "dp"), pairs)

    flat_low = tokens.reshape(count, width)
    flat = flat_low.astype(FULL)
    cot = cotangent.reshape(count, width)
    seen_all = jnp.stack([branch if k == 0 else hop(branch, k) for k in range(team)])
    seen_all = seen_all.reshape(team * units, CONT)
    position, allowed = jax.vmap(lambda seen: token_layout(seen, length))(seen_all)
    cosine, sine = jax.vmap(lambda places: rotary_tables(places, depth))(position)
    bias = jnp.where(allowed, 0.0, -1e30).astype(FULL)
    wide_cosine = jnp.concatenate([cosine, cosine], axis=-1).reshape(team, count, depth)
    wide_sine = jnp.concatenate([-sine, sine], axis=-1).reshape(team, count, depth)
    att_pack = pack_shares(att_master, [0, team, 2 * team, 3 * team], att_share)
    (
        normed_one,
        grad_fed,
        att_low,
        gate_low,
        down_low,
        _,
        _,
        projected,
        mixed,
        resid,
        normed_two,
        gate_value,
        up_value,
        hidden,
    ) = forward_layer(
        ranks,
        flat_low,
        normalize(flat)[0].astype(LOW),
        cot,
        att_pack,
        mlp_master,
        wide_cosine,
        wide_sine,
        bias,
    )
    (
        out_tokens,
        grad_tokens,
        got_att,
        got_gate,
        got_down,
        mlp_diff,
        mlp_other,
        *_,
    ) = backward_layer(
        ranks,
        (flat_low, resid, cot),
        (mlp_master, mlp_first, mlp_second),
        wide_cosine,
        wide_sine,
        bias,
        grad_fed.reshape(all_tokens, width),
        hidden.reshape(all_tokens, hid_share),
        gate_value.reshape(all_tokens, hid_share),
        up_value.reshape(all_tokens, hid_share),
        normed_two.reshape(all_tokens, width),
        normed_one.reshape(all_tokens, width),
        projected,
        mixed.reshape(all_tokens, att_share),
        att_low,
        gate_low,
        down_low,
    )
    mlp = (mlp_master, mlp_first, mlp_second, mlp_outer, mlp_diff, mlp_other)
    bases = [0, 1, 2, 3]
    *att_state, att_diff = adam_chunk(got_att, att_master, att_first, att_second, bases)
    mlp_out = finish_chunk(reps, got_down, *mlp, [2], None)
    mlp_out = finish_chunk(reps, got_gate, *mlp, [0, 1], mlp_out)
    att_new = outer_chunk(reps, att_diff, swap(att_diff), att_master, att_outer, bases)
    return (
        out_tokens.reshape(units, length, width),
        grad_tokens.reshape(units, length, width),
        *(att_new[1], *att_state, att_new[0], att_new[2]),
        *(mlp_out[3], mlp_out[0], mlp_out[1], mlp_out[2], mlp_out[4]),
    )


def solution(mesh):
    in_specs = (
        P(("rep", "dp"), None, None),
        P(("rep", "dp"), None, None),
        P(("rep", "dp"), None),
        P("dp", None),
        P("rep", "dp", None),
        P("rep", "dp", None),
        P("dp", None),
        P("dp", None),
        P("rep", "dp", None),
        P("rep", "dp", None),
        P("dp", None),
    )
    out_specs = (
        P(("rep", "dp"), None, None),
        P(("rep", "dp"), None, None),
        P("dp", None),
        P("rep", "dp", None),
        P("rep", "dp", None),
        P("dp", None),
        P("dp", None),
        P("dp", None),
        P("rep", "dp", None),
        P("rep", "dp", None),
        P("dp", None),
        P("dp", None),
    )

    def body(*args):
        return on_device(mesh.shape["rep"], mesh.shape["dp"], *args)

    return jax.shard_map(
        body, mesh=mesh, in_specs=in_specs, out_specs=out_specs, check_vma=False
    )
```

```python
import functools
import math

import jax
import jax.numpy as jnp
from jax import lax
from jax.experimental import pallas as pl
from jax.experimental.pallas import tpu as pltpu
from jax.sharding import PartitionSpec as P

HEAD_DIM = 128
PROMPT = 128
CLEN = 64
CONT = 2
STEP = 10
TEAM = 8


LN_EPS = 1e-05
BETA_ONE = 0.9
BETA_TWO = 0.95
ADAM_EPS = 1e-08
DECAY = 0.1
RATE = 0.05
OUTER_RATE = 0.7
OUTER_MOMENTUM = 0.9
CONTRACT_LAST = (((1,), (1,)), ((), ()))
CONTRACT_FIRST = (((0,), (0,)), ((), ()))
LOW = jnp.bfloat16
FULL = jnp.float32


def normalize(values):
    centre = values - jnp.mean(values, axis=-1, keepdims=True)
    factor = lax.rsqrt(jnp.mean(centre * centre, axis=-1, keepdims=True) + LN_EPS)
    return (centre * factor, factor)


def normalize_back(values, gradient):
    normed, factor = normalize(values)
    projection = jnp.mean(gradient * normed, axis=-1, keepdims=True)
    return factor * (gradient - jnp.mean(gradient, axis=-1, keepdims=True) - normed * projection)


def token_layout(seen, length):
    places = jnp.arange(length, dtype=jnp.int32)
    segment = jnp.where(places < PROMPT, -1, (places - PROMPT) // CLEN)
    within = jnp.where(places < PROMPT, places, (places - PROMPT) % CLEN)
    lookup = jnp.arange(CONT, dtype=jnp.int32)
    reach = jnp.sum(jnp.where(segment[:, None] == lookup[None, :], seen[None, :], 0), axis=1)
    position = jnp.where(segment < 0, places, reach + within)
    allowed = (segment[:, None] == segment[None, :]) & (within[None, :] <= within[:, None]) | (
        segment[None, :] < 0
    ) & (segment[:, None] >= 0) & (places[None, :] < reach[:, None])
    return (position, allowed)


def rotary_tables(position, depth):
    half_depth = depth // 2
    freqs = jnp.exp(jnp.arange(half_depth, dtype=jnp.float32) * (-2.0 * math.log(10000.0) / depth))
    angle = position.astype(jnp.float32)[:, None] * freqs[None, :]
    return (jnp.cos(angle)[:, None, :], jnp.sin(angle)[:, None, :])


def rotate(values, cosine, sine):
    half_depth = values.shape[-1] // 2
    first = values[..., :half_depth]
    second = values[..., half_depth:]
    return jnp.concatenate(
        [first * cosine - second * sine, second * cosine + first * sine], axis=-1
    )


def rotate_back(gradient, cosine, sine):
    half_depth = gradient.shape[-1] // 2
    first = gradient[..., :half_depth]
    second = gradient[..., half_depth:]
    return jnp.concatenate(
        [first * cosine + second * sine, second * cosine - first * sine], axis=-1
    )


def adam_step(master, gradient, first, second):
    first_new = BETA_ONE * first + (1.0 - BETA_ONE) * gradient
    second_new = BETA_TWO * second + (1.0 - BETA_TWO) * gradient * gradient
    ratio = (
        first_new
        / (1.0 - BETA_ONE**STEP)
        / (jnp.sqrt(second_new / (1.0 - BETA_TWO**STEP)) + ADAM_EPS)
    )
    return (master - RATE * (ratio + DECAY * master), first_new, second_new)


def outer_step(master, mean_diff, momentum):
    momentum_new = OUTER_MOMENTUM * momentum + mean_diff
    return (master - OUTER_RATE * (mean_diff + OUTER_MOMENTUM * momentum_new), momentum_new)


def dot(left, right, dims=(((1,), (0,)), ((), ()))):
    return lax.dot_general(left, right, dims, preferred_element_type=FULL)


MESH = pl.DeviceIdType.MESH
ANYWHERE = pl.BlockSpec(memory_space=pl.ANY)
BITS = (1, 2, 4)
PIECES = 4
GATE_AHEAD, GATE_MIDDLE = 7, 3
DOWN_EARLY = 15
FEED_EARLY = 6
SPLIT_TOKENS, SPLIT_ATTENDED, SPLIT_NORMED, SPLIT_COT, SPLIT_BACK = 3, 3, 3, 2, 3
STRIP = 16
GATHER_COPIES = 6 * PIECES + 1
VMEM_BYTES = 60 * 1024 * 1024


def flip(me, bit):
    return me + bit - 2 * bit * ((me // bit) % 2)


def across(me, other):
    bit = 1
    while bit <= other:
        if other & bit:
            me = flip(me, bit)
        bit *= 2
    return me


def greet(me, others, with_rep):
    barrier = pltpu.get_barrier_semaphore()
    for other in others:
        pl.semaphore_signal(
            barrier, inc=1, device_id={"dp": across(me, other)}, device_id_type=MESH
        )
    if with_rep:
        rep = lax.axis_index("rep")
        pl.semaphore_signal(barrier, inc=1, device_id={"rep": 1 - rep}, device_id_type=MESH)
    pl.semaphore_wait(barrier, len(others) + (1 if with_rep else 0))


class Sender:
    def __init__(self, sent, came):
        self.sent, self.came, self.index = sent, came, 0

    def __call__(self, source, target, where):
        copy = pltpu.make_async_remote_copy(
            src_ref=source,
            dst_ref=target,
            send_sem=self.sent.at[self.index],
            recv_sem=self.came.at[self.index],
            device_id=where,
            device_id_type=MESH,
        )
        copy.start()
        self.index += 1
        return copy


class TeamGather:
    def __init__(self, me, own, out, send, split):
        self.out, self.send, self.split = out, send, split
        self.piece = own.shape[0] // PIECES
        self.core, self.second, self.third = ({"dp": flip(me, bit)} for bit in BITS)
        self.late = list(range(split, PIECES)) + list(range(split))
        self.early = list(range(PIECES))
        self.own = own
        self.over_second, self.over_third, self.corner = {}, {}, {}
        self.rest, self.settled = [], []

    def cut(self, ref, p):
        return ref.at[pl.ds(p * self.piece, self.piece)]

    def begin(self):
        own, out, cut = self.own, self.out, self.cut
        for a, b in zip(self.late, self.early):
            self.over_second[a] = self.send(cut(own, a), cut(out.at[2], a), self.second)
            self.over_third[b] = self.send(cut(own, b), cut(out.at[4], b), self.third)
        self.rest.append(self.send(own, out.at[1], self.core))

    def turn(self):
        out, cut, send = self.out, self.cut, self.send
        for a, b in zip(self.late, self.early):
            self.over_second[a].wait_recv()
            if a >= self.split:
                self.corner[a] = send(cut(out.at[2], a), cut(out.at[6], a), self.third)
            self.rest.append(send(cut(out.at[2], a), cut(out.at[3], a), self.core))
            self.over_third[b].wait_recv()
            if b < self.split:
                self.corner[b] = send(cut(out.at[4], b), cut(out.at[6], b), self.second)
            self.rest.append(send(cut(out.at[4], b), cut(out.at[5], b), self.core))

    def settle(self):
        for copy in self.rest:
            copy.wait_recv()
        self.settled, self.rest = self.rest, []

    def finish(self):
        for p, copy in self.corner.items():
            copy.wait_recv()
            at = self.cut(self.out.at[6], p), self.cut(self.out.at[7], p)
            self.rest.append(self.send(*at, self.core))
        for group in (self.over_second, self.over_third, self.corner):
            for copy in group.values():
                copy.wait_send()
        for copy in self.settled:
            copy.wait_send()
        for copy in self.rest:
            copy.wait()


SUM_COPIES = 6


def sum_scratch(count, width):
    return [
        pltpu.VMEM((TEAM // 2, count, width), LOW),
        pltpu.VMEM((TEAM // 2, count, width), LOW),
        pltpu.VMEM((3, count, width), LOW),
    ]


def fold_steps(me, own, got, edge, first, send, split):
    count = own.shape[1]
    _, second, third = ({"dp": flip(me, bit)} for bit in BITS)
    spans = [pl.ds(0, split), pl.ds(split, count - split)]

    def add(j, span, extra=None):
        @pl.loop(0, span.size // STRIP)
        def _(step):
            at = pl.ds(span.start + step * STRIP, STRIP)
            value = own[j, at].astype(FULL)
            if extra is None:
                value = value + got[j, at].astype(FULL)
            else:
                value = value + extra[at].astype(FULL)
            own[j, at] = value.astype(LOW)

    whole = pl.ds(0, count)
    first[3].wait_recv()
    add(3, whole)
    corners = [
        send(own.at[3].at[span], edge.at[0].at[span], where)
        for span, where in zip(spans, (second, third))
    ]
    for j in (2, 1, 0):
        first[j].wait_recv()
        add(j, whole)
    yield
    for j, span, copy in zip((2, 1), spans, corners):
        copy.wait_recv()
        add(j, span, edge.at[0])
    for copy in corners + [first[j] for j in range(4)]:
        copy.wait_send()


def fold_parts(me, parts, own, got, edge, send, loads, split):
    core = {"dp": flip(me, 1)}
    loading = [pltpu.make_async_copy(parts.at[2 * j], own.at[j], loads.at[j]) for j in range(4)]
    first = {}
    for j in (3, 2, 1, 0):
        loading[j].start()
        first[j] = send(parts.at[2 * j + 1], got.at[j], core)
    for copy in loading:
        copy.wait()
    yield from fold_steps(me, own, got, edge, first, send, split)


def sum_steps(me, own, got, edge, first, send, total, split):
    count = own.shape[1]
    _, second, third = ({"dp": flip(me, bit)} for bit in BITS)
    spans = [pl.ds(0, split), pl.ds(split, count - split)]

    def add(j, h, extra=None):
        span = spans[h]

        @pl.loop(0, span.size // STRIP)
        def _(step):
            at = pl.ds(span.start + step * STRIP, STRIP)
            value = own[j, at].astype(FULL) + got[j, at].astype(FULL)
            if extra is not None:
                value = value + extra[at].astype(FULL)
            own[j, at] = value.astype(LOW)

    def go(j, h, slot, where):
        return send(own.at[j].at[spans[h]], edge.at[slot].at[spans[h]], where)

    both = split < count
    sends = []
    first[3].wait_recv()
    add(3, 0)
    corner_second = go(3, 0, 0, second)
    if both:
        add(3, 1)
        corner_third = go(3, 1, 0, third)
        sends.append(corner_third)
        first[2].wait_recv()
        add(2, 1)
        sends.append(go(2, 1, 2, third))
    first[1].wait_recv()
    add(1, 0)
    sends.append(go(1, 0, 1, second))
    yield
    if not both:
        first[2].wait_recv()
    corner_second.wait_recv()
    add(2, 0, edge.at[0])
    sends.append(go(2, 0, 2, third))
    if both:
        corner_third.wait_recv()
        add(1, 1, edge.at[0])
        sends.append(go(1, 1, 1, second))
    yield
    first[0].wait_recv()
    for copy in sends:
        if not both or copy is not corner_third:
            copy.wait_recv()

    @pl.loop(0, count // STRIP)
    def _(step):
        start = step * STRIP
        at = pl.ds(start, STRIP)
        value = own[0, at].astype(FULL) + got[0, at].astype(FULL)
        total(start, value + edge[1, at].astype(FULL) + edge[2, at].astype(FULL))

    for copy in sends + [corner_second] + [first[j] for j in range(4)]:
        copy.wait_send()


def params(collective_id):
    return pltpu.CompilerParams(
        collective_id=collective_id, has_side_effects=True, vmem_limit_bytes=VMEM_BYTES
    )


def strip_normalize(value):
    width = value.shape[1]
    centre = value - jnp.sum(value, axis=1, keepdims=True) * (1.0 / width)
    factor = lax.rsqrt(jnp.sum(centre * centre, axis=1, keepdims=True) * (1.0 / width) + LN_EPS)
    return (centre * factor, factor)


UNIT = 256


def unit_of(step):
    return 2 * (TEAM // 2 - 1 - step % (TEAM // 2)) + jnp.where(step < TEAM // 2, 1, 0)


def stream(steps, loads, body, arrive=None):
    if arrive is not None:
        arrive(0)
    for copy in loads(0, 0):
        copy.start()

    @pl.loop(0, steps)
    def _(step):
        slot = step % 2

        @pl.when(step + 1 < steps)
        def _():
            if arrive is not None:
                arrive(step + 1)
            for copy in loads(step + 1, 1 - slot):
                copy.start()

        for copy in loads(step, slot):
            copy.wait()
        body(step, slot)


def stream_out(steps, loads, stores, body):
    def whole(step, slot):
        @pl.when(step >= 2)
        def _():
            for copy in stores(step - 2, slot):
                copy.wait()

        body(step, slot)
        for copy in stores(step, slot):
            copy.start()

    stream(steps, loads, whole)
    for step in (steps - 2, steps - 1):
        for copy in stores(step, step % 2):
            copy.wait()


def rows_at(step, size):
    return pl.ds(pl.multiple_of(step * size, size), size)


class RowGather:
    def __init__(self, ranks, me, rep, weights, send, send_x, local):
        self.me, self.rep, self.weights, self.local = me, rep, weights, local
        self.send, self.send_x = send, send_x
        self.rows = weights.shape[0] // ranks
        self.half = self.rows // 2
        self.order = list(range(1, ranks))
        self.ways, self.swaps = {}, []

    def place(self, device):
        return self.weights.at[pl.ds(device * self.rows + self.rep * self.half, self.half)]

    def begin(self, pack, number=None):
        me, rep = self.me, self.rep
        if not self.ways:
            at = self.weights.at[pl.ds(me * self.rows, self.rows)]
            self.own = pltpu.make_async_copy(pack.at[me % TEAM], at, self.local)
            self.own.start()
        started = len(self.ways)
        number = len(self.order) - started if number is None else number
        for other in self.order[started : started + number]:
            where = across(me, other)
            source = pack.at[where % TEAM, pl.ds(rep * self.half, self.half)]
            self.ways[other] = self.send(source, self.place(me), {"dp": where})

    def forward(self, number=None):
        done = len(self.swaps)
        number = len(self.order) - done if number is None else number
        for other in self.order[done : done + number]:
            self.ways[other].wait_recv()
            at = self.place(across(self.me, other))
            self.swaps.append(self.send_x(at, at, {"rep": 1 - self.rep}))

    def finish(self):
        for copy in self.ways.values():
            copy.wait_send()
        for copy in self.swaps + [self.own]:
            copy.wait()


def attend_unit(values, cosine, sine, bias, share):
    depth = HEAD_DIM
    parts = []
    for p in range(2):
        turned = []
        for at in range(p * share, (p + 1) * share, depth):
            head = values[:, at : at + depth]
            turned.append((head * cosine + pltpu.roll(head, depth // 2, 1) * sine).astype(LOW))
        parts.append(turned)
    query, keys = parts
    value = [
        values[:, at : at + depth].astype(LOW) for at in range(2 * share, 3 * share, depth)
    ]
    mixed = []
    for one, two, three in zip(query, keys, value):
        scores = dot(one, two, CONTRACT_LAST) * depth ** (-0.5) + bias
        powers = jnp.exp(scores - jnp.max(scores, axis=1, keepdims=True))
        prob = powers / jnp.sum(powers, axis=1, keepdims=True)
        mixed.append(dot(prob.astype(LOW), three).astype(LOW))
    return jnp.concatenate(query + keys + value, axis=1), jnp.concatenate(mixed, axis=1)


def forward_kernel(
    ranks,
    flat,
    normed_own,
    cot,
    att_pack,
    mlp_master,
    cosine,
    sine,
    bias,
    normed_all,
    cot_all,
    att_weights,
    gate_weights,
    down_weights,
    gate_pack,
    down_pack,
    projected_all,
    mixed_all,
    resid,
    normed_two_all,
    gate_all,
    up_all,
    hidden_all,
    att,
    gate,
    block,
    odd,
    own,
    got,
    edge,
    normed,
    *sems,
):
    sent_team, came_team, sent_rows, came_rows, sent_x, came_x, first_sent, first_came, local = sems
    me = lax.axis_index("dp")
    rep = lax.axis_index("rep")
    rows, share = att_pack.shape[1], att_pack.shape[2] // 4
    hid = gate_pack.shape[2] // 2
    core = {"dp": flip(me, 1)}
    greet(me, range(1, ranks), True)
    send = Sender(sent_team, came_team)
    send_rows = Sender(sent_rows, came_rows)
    send_x = Sender(sent_x, came_x)
    tokens = TeamGather(me, normed_own, normed_all, send, SPLIT_TOKENS)
    tokens.begin()
    gathers = [
        RowGather(ranks, me, rep, weights, send_rows, send_x, local.at[i])
        for i, weights in enumerate((att_weights, gate_weights, down_weights))
    ]
    gathers[0].begin(att_pack)
    keep = [pltpu.make_async_copy(normed_own, normed_all.at[0], local.at[3])]
    keep.append(pltpu.make_async_copy(cot, cot_all.at[0], local.at[4]))
    for copy in keep:
        copy.start()

    def pack(wide, low):
        def loads(t, slot):
            return [
                pltpu.make_async_copy(
                    mlp_master.at[:, rows_at(p * TEAM + t, hid)],
                    wide.at[slot, p],
                    local.at[5 + 3 * slot + p],
                )
                for p in range(3)
            ]

        def stores(t, slot):
            near = low.at[slot]
            return [
                pltpu.make_async_copy(
                    near.at[:, pl.ds(0, 2 * hid)], gate_pack.at[t], local.at[11 + slot]
                ),
                pltpu.make_async_copy(
                    near.at[:, pl.ds(2 * hid, hid)], down_pack.at[t], local.at[13 + slot]
                ),
            ]

        def body(t, slot):
            for p in range(3):
                low[slot, :, p * hid : (p + 1) * hid] = wide[slot, p].astype(LOW)

        stream_out(TEAM, loads, stores, body)

    pl.run_scoped(
        pack, pltpu.VMEM((2, 3, rows, hid), FULL), pltpu.VMEM((2, rows, 3 * hid), LOW)
    )
    tokens.turn()
    gathers[1].begin(gate_pack)
    gathers[0].forward()
    tokens.finish()
    gathers[0].finish()
    for copy in keep:
        copy.wait()
    load = pltpu.make_async_copy(att_weights, att, local.at[0])
    load.start()
    load.wait()

    gathers[1].forward(GATE_AHEAD)

    def fetch(step, slot):
        return pltpu.make_async_copy(
            normed_all.at[unit_of(step)], block.at[slot], local.at[5 + slot]
        )

    fetch(0, 0).start()

    @pl.loop(0, TEAM)
    def _(step):
        slot = step % 2
        unit = unit_of(step)

        @pl.when(step + 1 < TEAM)
        def _():
            fetch(step + 1, 1 - slot).start()

        fetch(step, slot).wait()
        values = dot(block[slot], att[:, : 3 * share])
        projected, mixed = attend_unit(values, cosine[unit], sine[unit], bias[unit], share)
        projected_all[unit] = projected
        mixed_all[unit] = mixed
        term = dot(mixed, att[:, 3 * share :], CONTRACT_LAST).astype(LOW)
        j = unit // 2

        @pl.when(step < TEAM // 2)
        def _():
            odd[j] = term
            pltpu.make_async_remote_copy(
                src_ref=odd.at[j],
                dst_ref=got.at[j],
                send_sem=first_sent.at[j],
                recv_sem=first_came.at[j],
                device_id=core,
                device_id_type=MESH,
            ).start()

        @pl.when(step >= TEAM // 2)
        def _():
            own[j] = term

    first = [
        pltpu.make_async_remote_copy(
            src_ref=odd.at[j],
            dst_ref=got.at[j],
            send_sem=first_sent.at[j],
            recv_sem=first_came.at[j],
            device_id=core,
            device_id_type=MESH,
        )
        for j in range(TEAM // 2)
    ]

    def total(start, value):
        at = pl.ds(start, STRIP)
        value = value + flat[at].astype(FULL)
        resid[at] = value
        normed[at] = strip_normalize(value)[0].astype(LOW)

    steps = sum_steps(me, own, got, edge, first, send, total, SPLIT_ATTENDED * UNIT // PIECES)
    next(steps)
    early = DOWN_EARLY * (ranks - 1) // 15
    gathers[2].begin(down_pack, early)
    gathers[1].forward(GATE_MIDDLE * (ranks - TEAM) // TEAM)
    next(steps)
    for _ in steps:
        pass
    tokens = TeamGather(me, normed, normed_two_all, send, SPLIT_NORMED)
    tokens.begin()
    gathers[2].begin(down_pack)
    cots = TeamGather(me, cot, cot_all, send, SPLIT_COT)
    cots.begin()
    keep = pltpu.make_async_copy(normed, normed_two_all.at[0], local.at[3])
    keep.start()
    gathers[1].forward()
    gathers[2].forward(early)
    tokens.turn()
    keep.wait()
    gathers[1].finish()
    tokens.settle()
    load = pltpu.make_async_copy(gate_weights, gate, local.at[1])
    load.start()
    load.wait()

    def feed(base, low):
        def loads(step, slot):
            source = normed_two_all.at[base + step]
            return [pltpu.make_async_copy(source, block.at[slot], local.at[5 + slot])]

        def stores(step, slot):
            return [
                pltpu.make_async_copy(
                    low.at[slot, i], out.at[base + step], local.at[7 + 3 * slot + i]
                )
                for i, out in enumerate((gate_all, up_all, hidden_all))
            ]

        def body(step, slot):
            @pl.loop(0, hid // UNIT)
            def _(column):
                at = rows_at(column, UNIT)
                later = pl.ds(pl.multiple_of(hid + column * UNIT, UNIT), UNIT)
                gate_value = dot(block[slot], gate[:, at])
                up_value = dot(block[slot], gate[:, later])
                low[slot, 0, :, at] = gate_value.astype(LOW)
                low[slot, 1, :, at] = up_value.astype(LOW)
                hidden = gate_value * jax.nn.sigmoid(gate_value) * up_value
                low[slot, 2, :, at] = hidden.astype(LOW)

        stream_out(FEED_EARLY if base == 0 else TEAM - FEED_EARLY, loads, stores, body)

    fed = pltpu.VMEM((2, 3, normed.shape[0], hid), LOW)
    pl.run_scoped(functools.partial(feed, 0), fed)
    tokens.finish()
    cots.turn()
    gathers[2].forward()
    pl.run_scoped(functools.partial(feed, FEED_EARLY), fed)
    cots.finish()
    gathers[2].finish()


def forward_layer(ranks, flat, normed, cot, att_pack, mlp_master, cosine, sine, bias):
    count, width = normed.shape
    rows, share = att_pack.shape[1], att_pack.shape[2] // 4
    hid = mlp_master.shape[1] // (3 * TEAM)
    gathered = jax.ShapeDtypeStruct((TEAM, count, width), LOW)
    hidden = jax.ShapeDtypeStruct((TEAM, count, hid), LOW)
    vmem = pl.BlockSpec(memory_space=pltpu.VMEM)

    def weights(columns):
        return jax.ShapeDtypeStruct((ranks * rows, columns), LOW)

    def packs(columns):
        return jax.ShapeDtypeStruct((TEAM, rows, columns), LOW)

    out = [
        (gathered, ANYWHERE),
        (gathered, ANYWHERE),
        (weights(4 * share), ANYWHERE),
        (weights(2 * hid), ANYWHERE),
        (weights(hid), ANYWHERE),
        (packs(2 * hid), ANYWHERE),
        (packs(hid), ANYWHERE),
        (jax.ShapeDtypeStruct((TEAM, count, 3 * share), LOW), vmem),
        (jax.ShapeDtypeStruct((TEAM, count, share), LOW), vmem),
        (jax.ShapeDtypeStruct((count, width), FULL), vmem),
        (gathered, ANYWHERE),
        (hidden, ANYWHERE),
        (hidden, ANYWHERE),
        (hidden, ANYWHERE),
    ]
    team_copies = 3 * GATHER_COPIES + SUM_COPIES
    pairs = [team_copies] * 2 + [3 * (ranks - 1)] * 4 + [TEAM // 2] * 2 + [15]
    return pl.pallas_call(
        functools.partial(forward_kernel, ranks),
        out_shape=[shape for shape, _ in out],
        in_specs=[vmem] + [ANYWHERE] * 4 + [vmem] * 3,
        out_specs=[spec for _, spec in out],
        scratch_shapes=[
            pltpu.VMEM((ranks * rows, 4 * share), LOW),
            pltpu.VMEM((ranks * rows, 2 * hid), LOW),
            pltpu.VMEM((2, count, width), LOW),
            pltpu.VMEM((TEAM // 2, count, width), LOW),
            pltpu.VMEM((TEAM // 2, count, width), LOW),
            pltpu.VMEM((TEAM // 2, count, width), LOW),
            pltpu.VMEM((3, count, width), LOW),
            pltpu.VMEM((count, width), LOW),
        ]
        + [pltpu.SemaphoreType.DMA((number,)) for number in pairs],
        compiler_params=params(0),
        name="forward_layer",
    )(flat, normed, cot, att_pack, mlp_master, cosine, sine, bias)


def attend_unit_back(values, given, cosine, sine, bias, share):
    depth = HEAD_DIM
    scale = depth ** (-0.5)
    grads = ([], [], [])
    for at in range(0, share, depth):
        query, keys, value = (values[:, p * share + at : p * share + at + depth] for p in range(3))
        grad = given[:, at : at + depth]
        scores = dot(query, keys, CONTRACT_LAST) * scale + bias
        powers = jnp.exp(scores - jnp.max(scores, axis=1, keepdims=True))
        prob = powers / jnp.sum(powers, axis=1, keepdims=True)
        grad_prob = dot(grad, value, CONTRACT_LAST)
        grad_value = dot(prob.astype(LOW), grad, CONTRACT_FIRST)
        along = jnp.sum(grad_prob * prob, axis=1, keepdims=True)
        grad_scores = (prob * (grad_prob - along)).astype(LOW)
        turned = (
            dot(grad_scores, keys) * scale,
            dot(grad_scores, query, CONTRACT_FIRST) * scale,
        )
        for p in range(2):
            back = turned[p] * cosine - pltpu.roll(turned[p], depth // 2, 1) * sine
            grads[p].append(back.astype(LOW))
        grads[2].append(grad_value.astype(LOW))
    return jnp.concatenate(grads[0] + grads[1] + grads[2], axis=1)


class Terms:
    def __init__(self, me, odd, own, got, sent, came):
        self.odd, self.own, self.got, self.sent, self.came = odd, own, got, sent, came
        self.core = {"dp": flip(me, 1)}

    def copy(self, j):
        return pltpu.make_async_remote_copy(
            src_ref=self.odd.at[j],
            dst_ref=self.got.at[j],
            send_sem=self.sent.at[j],
            recv_sem=self.came.at[j],
            device_id=self.core,
            device_id_type=MESH,
        )

    def put(self, step, term):
        j = unit_of(step) // 2

        @pl.when(step < TEAM // 2)
        def _():
            self.odd[j] = term
            self.copy(j).start()

        @pl.when(step >= TEAM // 2)
        def _():
            self.own[j] = term

    def first(self):
        return [self.copy(j) for j in range(TEAM // 2)]


LOWS = (0, 4, 2, 6, 1, 5, 3, 7)


def backward_kernel(
    ranks,
    resid,
    cot,
    cosine,
    sine,
    bias,
    cot_all,
    hidden_all,
    gate_all,
    up_all,
    normed_two_all,
    normed_one_all,
    projected_all,
    mixed_all,
    att_weights,
    gate_weights,
    down_weights,
    mlp_master,
    mlp_first,
    mlp_second,
    grad_resid,
    one_folded,
    two_folded,
    got_att,
    got_gate,
    got_down,
    mlp_diff,
    mlp_other,
    grad_all,
    att_grad,
    gate_grad,
    down_grad,
    fed_all,
    own,
    got,
    edge,
    odd,
    own_two,
    got_two,
    edge_two,
    grad_low,
    stage,
    wide,
    sent,
    came,
    sent_rows,
    came_rows,
    sent_first,
    came_first,
    sent_x,
    came_x,
    kept,
    local,
):
    me = lax.axis_index("dp")
    rep = lax.axis_index("rep")
    tops = ranks // TEAM
    rows = got_att.shape[1]
    share = mixed_all.shape[1]
    hid = hidden_all.shape[1]
    count, width = resid.shape
    tokens = TEAM * count
    tiles = width // UNIT
    greet(me, range(1, ranks), True)
    send = Sender(sent, came)
    order = []
    for low_bits in LOWS:
        order += [top * TEAM + low_bits for top in range(1, tops)]
        order += [low_bits] if low_bits else []

    chunks = ((down_grad, got_down), (gate_grad, got_gate), (att_grad, got_att))

    def block_copy(chunk, other):
        grad, target = chunks[chunk]
        index = chunk * (ranks - 1) + other - 1
        where = across(me, other)
        return pltpu.make_async_remote_copy(
            src_ref=grad.at[pl.ds(where * rows, rows)],
            dst_ref=target.at[me],
            send_sem=sent_rows.at[index],
            recv_sem=came_rows.at[index],
            device_id={"dp": where},
            device_id_type=MESH,
        )

    def keep_own(grad, target, index):
        copy = pltpu.make_async_copy(
            grad.at[pl.ds(me * rows, rows)], target.at[me], kept.at[index]
        )
        copy.start()
        return copy

    def down_phase(hidden, tile, low):
        whole = pltpu.make_async_copy(hidden_all, hidden, local.at[0])
        whole.start()

        def loads(step, slot):
            at = rows_at(step, UNIT)
            return [pltpu.make_async_copy(cot_all.at[:, at], tile.at[slot], local.at[2 + slot])]

        def stores(step, slot):
            at = rows_at(step, UNIT)
            return [pltpu.make_async_copy(low.at[slot], down_grad.at[at], local.at[4 + slot])]

        def body(step, slot):
            low[slot] = dot(tile[slot], hidden[...], CONTRACT_FIRST).astype(LOW)

        whole.wait()
        stream_out(tiles, loads, stores, body)

    pl.run_scoped(
        down_phase,
        pltpu.VMEM((tokens, hid), LOW),
        pltpu.VMEM((2, tokens, UNIT), LOW),
        pltpu.VMEM((2, UNIT, hid), LOW),
    )
    for other in order:
        block_copy(0, other).start()
    own_copies = [keep_own(down_grad, got_down, 0)]

    gate_order = list(order)

    def more(number):
        for _ in range(min(number, len(gate_order))):
            block_copy(1, gate_order.pop(0)).start()

    terms = Terms(me, odd, own, got, sent_first.at[0], came_first.at[0])

    grad_gate = wide.at[pl.ds(0, tokens), pl.ds(0, 2 * hid)]

    def hidden_phase(down, block, gate, up):
        whole = pltpu.make_async_copy(down_weights, down, local.at[1])
        whole.start()

        def loads(step, slot):
            at = rows_at(step, count)
            return [
                pltpu.make_async_copy(cot_all.at[at], block.at[slot], local.at[2 + slot]),
                pltpu.make_async_copy(gate_all.at[at], gate.at[slot], local.at[4 + slot]),
                pltpu.make_async_copy(up_all.at[at], up.at[slot], local.at[6 + slot]),
            ]

        def body(step, slot):
            at = rows_at(step, count)

            @pl.loop(0, hid // UNIT)
            def _(column):
                place = rows_at(column, UNIT)
                later = pl.ds(pl.multiple_of(hid + column * UNIT, UNIT), UNIT)
                grad = dot(block[slot], down[:, place])
                value = gate[slot, :, place].astype(FULL)
                sigmoid = jax.nn.sigmoid(value)
                slope = sigmoid * (1.0 + value * (1.0 - sigmoid))
                up_value = up[slot, :, place].astype(FULL)
                grad_gate[at, place] = (grad * up_value * slope).astype(LOW)
                grad_gate[at, later] = (grad * value * sigmoid).astype(LOW)

        whole.wait()
        stream(TEAM, loads, body)

    pl.run_scoped(
        hidden_phase,
        pltpu.VMEM((width, hid), LOW),
        pltpu.VMEM((2, count, width), LOW),
        pltpu.VMEM((2, count, hid), LOW),
        pltpu.VMEM((2, count, hid), LOW),
    )

    def back_phase(gate):
        whole = pltpu.make_async_copy(gate_weights, gate, local.at[0])
        whole.start()
        whole.wait()

        @pl.loop(0, TEAM)
        def _(step):
            at = rows_at(unit_of(step), count)
            terms.put(step, dot(grad_gate[at, :], gate[...], CONTRACT_LAST).astype(LOW))

    pl.run_scoped(back_phase, pltpu.VMEM((width, 2 * hid), LOW))

    def weight_phase(tile, low):
        def loads(step, slot):
            at = rows_at(step, UNIT)
            return [
                pltpu.make_async_copy(
                    normed_two_all.at[:, at], tile.at[slot], local.at[2 + slot]
                )
            ]

        def stores(step, slot):
            at = rows_at(step, UNIT)
            return [pltpu.make_async_copy(low.at[slot], gate_grad.at[at], local.at[4 + slot])]

        def body(step, slot):
            low[slot] = dot(tile[slot], grad_gate[...], CONTRACT_FIRST).astype(LOW)

        stream_out(tiles, loads, stores, body)


    def resid_total(start, value):
        at = pl.ds(start, STRIP)
        normed, factor = strip_normalize(resid[at])
        along = jnp.sum(value * normed, axis=1, keepdims=True) * (1.0 / width)
        middle = jnp.sum(value, axis=1, keepdims=True) * (1.0 / width)
        value = cot[at].astype(FULL) + factor * (value - middle - normed * along)
        grad_resid[at] = value
        grad_low[at] = value.astype(LOW)

    split = SPLIT_BACK * UNIT // PIECES
    steps = sum_steps(me, own, got, edge, terms.first(), send, resid_total, split)
    next(steps)
    pl.run_scoped(
        weight_phase, pltpu.VMEM((2, tokens, UNIT), LOW), pltpu.VMEM((2, UNIT, 2 * hid), LOW)
    )
    own_copies.append(keep_own(gate_grad, got_gate, 1))
    more(GATE_FIRST)
    next(steps)
    more(GATE_LATE)
    for _ in steps:
        pass
    gather = TeamGather(me, grad_low, grad_all, send, SPLIT_BACK)
    gather.begin()
    more(GATE_GATHER)
    keep = pltpu.make_async_copy(grad_low, grad_all.at[0], local.at[8])
    keep.start()
    def fed_phase(hidden, down, term):
        whole = [
            pltpu.make_async_copy(hidden_all, hidden, local.at[0]),
            pltpu.make_async_copy(down_weights, down, local.at[1]),
        ]
        for copy in whole:
            copy.start()
        for copy in whole:
            copy.wait()

        def fed_stores(step, slot):
            return [pltpu.make_async_copy(term.at[slot], fed_all.at[step], local.at[6 + slot])]

        def fed_body(step, slot):
            term[slot] = dot(hidden[rows_at(step, count)], down[...], CONTRACT_LAST).astype(LOW)

        stream_out(TEAM, lambda step, slot: [], fed_stores, fed_body)

    pl.run_scoped(
        fed_phase,
        pltpu.VMEM((tokens, hid), LOW),
        pltpu.VMEM((width, hid), LOW),
        pltpu.VMEM((2, count, width), LOW),
    )
    gather.turn()
    more(len(gate_order))
    gather.finish()
    keep.wait()

    terms = Terms(me, odd, own, got, sent_first.at[1], came_first.at[1])

    def att_phase():
        att = wide.at[pl.ds(0, width), pl.ds(0, 4 * share)]
        grad_projected = wide.at[pl.ds(0, tokens), pl.ds(4 * share, 3 * share)]

        def unit_phase(block, projected, tables, mask):
            def loads(step, slot):
                unit = unit_of(step)
                return [
                    pltpu.make_async_copy(grad_all.at[unit], block.at[slot], local.at[slot]),
                    pltpu.make_async_copy(
                        projected_all.at[unit], projected.at[slot], local.at[2 + slot]
                    ),
                    pltpu.make_async_copy(cosine.at[unit], tables.at[slot, 0], local.at[4 + slot]),
                    pltpu.make_async_copy(sine.at[unit], tables.at[slot, 1], local.at[6 + slot]),
                    pltpu.make_async_copy(bias.at[unit], mask.at[slot], local.at[8 + slot]),
                ]

            def body(step, slot):
                given = dot(block[slot], att[:, 3 * share :]).astype(LOW)
                grads = attend_unit_back(
                    projected[slot], given, tables[slot, 0], tables[slot, 1], mask[slot], share
                )
                grad_projected[rows_at(unit_of(step), count), :] = grads
                terms.put(step, dot(grads, att[:, : 3 * share], CONTRACT_LAST).astype(LOW))

            whole = pltpu.make_async_copy(att_weights, att, local.at[10])
            whole.start()
            whole.wait()
            stream(TEAM, loads, body)

        pl.run_scoped(
            unit_phase,
            pltpu.VMEM((2, count, width), LOW),
            pltpu.VMEM((2, count, 3 * share), LOW),
            pltpu.VMEM((2, 2, count, HEAD_DIM), FULL),
            pltpu.VMEM((2, count, count), FULL),
        )

        def weight_phase(normed, grad, mixed, low):
            def loads(step, slot):
                at = rows_at(step, UNIT)
                return [
                    pltpu.make_async_copy(
                        normed_one_all.at[:, at], normed.at[slot], local.at[slot]
                    ),
                    pltpu.make_async_copy(
                        grad_all.at[:, :, at], grad.at[slot], local.at[2 + slot]
                    ),
                ]

            def stores(step, slot):
                at = rows_at(step, UNIT)
                return [pltpu.make_async_copy(low.at[slot], att_grad.at[at], local.at[4 + slot])]

            def body(step, slot):
                left = normed[slot]
                low[slot, :, : 3 * share] = dot(left, grad_projected[...], CONTRACT_FIRST).astype(LOW)
                left = grad[slot].reshape(tokens, UNIT)
                low[slot, :, 3 * share :] = dot(left, mixed[...], CONTRACT_FIRST).astype(LOW)

            whole = pltpu.make_async_copy(mixed_all, mixed, local.at[10])
            whole.start()
            whole.wait()
            stream_out(tiles, loads, stores, body)

        pl.run_scoped(
            weight_phase,
            pltpu.VMEM((2, tokens, UNIT), LOW),
            pltpu.VMEM((2, TEAM, count, UNIT), LOW),
            pltpu.VMEM((tokens, share), LOW),
            pltpu.VMEM((2, UNIT, 4 * share), LOW),
        )

    att_phase()
    for other in order:
        block_copy(2, other).start()
    own_copies.append(keep_own(att_grad, got_att, 2))

    def mate_at(low):
        mate = 0
        for bit in BITS:
            mine, its = (me // bit) % 2, (low // bit) % 2
            mate = mate + bit * (mine + its - 2 * mine * its)
        return mate

    def differ(chunk, parts, first_part, base):
        source = chunks[chunk][1]

        def low_at(step):
            turn = step // parts
            return 4 * (turn % 2) + 2 * ((turn // 2) % 2) + turn // 4

        def column(step):
            return rows_at((first_part + step % parts) * TEAM + mate_at(low_at(step)), hid)

        def near(step):
            at = column(step)
            return pltpu.make_async_copy(
                stage.at[step % 2], mlp_diff.at[:, at], kept.at[3 + step % 2]
            )

        def far(step):
            at = column(step)
            return pltpu.make_async_remote_copy(
                src_ref=mlp_diff.at[:, at],
                dst_ref=mlp_other.at[:, at],
                send_sem=sent_x.at[base + step],
                recv_sem=came_x.at[base + step],
                device_id={"rep": 1 - rep},
                device_id_type=MESH,
            )

        def arrive(step):
            low = low_at(step)

            @pl.when(step % parts == 0)
            def _():
                for top in range(tops):
                    index = chunk * (ranks - 1) + top * TEAM + low - 1

                    def wait():
                        pltpu.make_async_remote_copy(
                            src_ref=source.at[me],
                            dst_ref=source.at[me],
                            send_sem=sent_rows.at[index],
                            recv_sem=came_rows.at[index],
                            device_id={"dp": flip(me, 1)},
                            device_id_type=MESH,
                        ).wait_recv()

                    if top:
                        wait()
                    else:
                        pl.when(low > 0)(wait)
                        pl.when(low == 0)(own_copies[chunk].wait)

        def run(big, low):
            def loads(step, slot):
                at = column(step)
                mate = mate_at(low_at(step))
                part = rows_at(step % parts, hid)
                return [
                    pltpu.make_async_copy(mlp_master.at[:, at], big.at[slot, 0], local.at[slot]),
                    pltpu.make_async_copy(mlp_first.at[0, :, at], big.at[slot, 1], local.at[2 + slot]),
                    pltpu.make_async_copy(mlp_second.at[0, :, at], big.at[slot, 2], local.at[4 + slot]),
                ] + [
                    pltpu.make_async_copy(
                        source.at[top * TEAM + mate, :, part],
                        low.at[slot, top],
                        local.at[6 + slot + 2 * top],
                    )
                    for top in range(tops)
                ]

            def body(step, slot):
                @pl.loop(0, rows // STRIP)
                def _(strip):
                    at = pl.ds(strip * STRIP, STRIP)
                    grad = low[slot, 0, at].astype(FULL)
                    for top in range(1, tops):
                        grad = grad + low[slot, top, at].astype(FULL)
                    value = big[slot, 0, at]
                    inner, _, _ = adam_step(value, grad, big[slot, 1, at], big[slot, 2, at])
                    stage[slot, at] = (value - inner).astype(LOW)

                near(step).start()

                @pl.when(step > 0)
                def _():
                    near(step - 1).wait()
                    far(step - 1).start()

            steps = parts * TEAM
            stream(steps, loads, body, arrive)
            near(steps - 1).wait()
            far(steps - 1).start()

        pl.run_scoped(
            run, pltpu.VMEM((2, 3, rows, hid), FULL), pltpu.VMEM((2, tops, rows, hid), LOW)
        )

        def finish():
            @pl.loop(0, parts * TEAM)
            def _(step):
                far(step).wait()

        return finish

    waits = [differ(0, 1, 2, 0)]
    folds = [
        fold_steps(me, own, got, edge, terms.first(), send, split),
        fold_parts(me, fed_all, own_two, got_two, edge_two, send, local, split),
    ]
    for steps in folds:
        next(steps)
    waits.append(differ(1, 2, 0, TEAM))
    outs = []
    for steps, terms_now, folded in zip(folds, (own, own_two), (one_folded, two_folded)):
        for _ in steps:
            pass
        outs.append(
            pltpu.make_async_copy(
                terms_now.at[pl.ds(0, 3)], folded, local.at[len(outs)]
            )
        )
        outs[-1].start()
    for copy in outs:
        copy.wait()
    own_copies[2].wait()
    for other in order:
        block_copy(2, other).wait_recv()
    for chunk in range(3):
        for other in order:
            block_copy(chunk, other).wait_send()
    for wait in waits:
        wait()


GATE_FIRST, GATE_LATE, GATE_GATHER = 0, 1, 2


def backward_layer(ranks, tokens, mlp, *rest):
    resid, cot = tokens
    hidden_all, projected_all, gate_weights = rest[4], rest[9], rest[12]
    count, width = resid.shape
    all_tokens, hid = hidden_all.shape
    share = projected_all.shape[2] // 3
    rows = width // ranks
    vmem = pl.BlockSpec(memory_space=pltpu.VMEM)
    low = functools.partial(jax.ShapeDtypeStruct, dtype=LOW)
    out = [
        (jax.ShapeDtypeStruct((count, width), FULL), vmem),
        (low((3, count, width)), ANYWHERE),
        (low((3, count, width)), ANYWHERE),
        (low((ranks, rows, 4 * share)), ANYWHERE),
        (low((ranks, rows, 2 * hid)), ANYWHERE),
        (low((ranks, rows, hid)), ANYWHERE),
        (low(mlp[0].shape), ANYWHERE),
        (low(mlp[0].shape), ANYWHERE),
        (low((TEAM, count, width)), ANYWHERE),
        (low((width, 4 * share)), ANYWHERE),
        (low((width, 2 * hid)), ANYWHERE),
        (low((width, hid)), ANYWHERE),
        (low((TEAM, count, width)), ANYWHERE),
    ]
    team_copies = GATHER_COPIES + 2 * SUM_COPIES + SUM_COPIES + TEAM // 2
    locals_needed = 6 + 2 * (ranks // TEAM) * (hid // share) + 2
    sems = [team_copies] * 2 + [3 * (ranks - 1)] * 2
    return pl.pallas_call(
        functools.partial(backward_kernel, ranks),
        out_shape=[shape for shape, _ in out],
        in_specs=[vmem] * 2 + [ANYWHERE] * (len(rest) + 3),
        out_specs=[spec for _, spec in out],
        scratch_shapes=sum_scratch(count, width)
        + [pltpu.VMEM((TEAM // 2, count, width), LOW)]
        + sum_scratch(count, width)
        + [
            pltpu.VMEM((count, width), LOW),
            pltpu.VMEM((2, rows, hid), LOW),
            pltpu.VMEM((max(width, all_tokens), max(2 * hid, 7 * share)), LOW),
        ]
        + [pltpu.SemaphoreType.DMA((number,)) for number in sems]
        + [pltpu.SemaphoreType.DMA((2, TEAM // 2))] * 2
        + [pltpu.SemaphoreType.DMA((3 * TEAM,))] * 2
        + [
            pltpu.SemaphoreType.DMA((3 + TEAM,)),
            pltpu.SemaphoreType.DMA((max(locals_needed, 12),)),
        ],
        compiler_params=params(2),
        name="backward_layer",
    )(resid, cot, *rest, *mlp)


def pack_kernel(*refs):
    share = refs[0].shape[1]
    for p, ref in enumerate(refs[:-1]):
        refs[-1][0, :, p * share : (p + 1) * share] = ref[...].astype(LOW)


def pack_shares(master, bases, share):
    rows = master.shape[0]
    return pl.pallas_call(
        pack_kernel,
        grid=(TEAM,),
        out_shape=jax.ShapeDtypeStruct((TEAM, rows, len(bases) * share), LOW),
        in_specs=[
            pl.BlockSpec((rows, share), lambda i, base=base: (0, base + i)) for base in bases
        ],
        out_specs=pl.BlockSpec((1, rows, len(bases) * share), lambda i: (i, 0, 0)),
        name="pack_shares",
    )(*[master] * len(bases))


LANES = 1024


def finish_kernel(reps, share, grads, master, first, second, outer, diff, other, *refs):
    first_new, second_new, mean_out, new, outer_new = refs[-5:]
    for t in range(grads.shape[1]):
        at = slice(t * share, (t + 1) * share)
        grad = grads[0, t].astype(FULL)
        for top in range(1, grads.shape[0]):
            grad = grad + grads[top, t].astype(FULL)
        first_new[0, :, at] = BETA_ONE * first[0, :, at] + (1.0 - BETA_ONE) * grad
        second_new[0, :, at] = BETA_TWO * second[0, :, at] + (1.0 - BETA_TWO) * grad * grad
    mean = (diff[...].astype(FULL) + other[...].astype(FULL)) / reps
    mean_out[...] = mean
    new[...], outer_new[...] = outer_step(master[...], mean, outer[...])


def finish_chunk(reps, grads, master, first, second, outer, diff, other, bases, written):
    ranks, rows, columns = grads.shape
    parts = len(bases)
    share = columns // parts
    lanes = max(LANES, share)
    per = lanes // share
    steps = TEAM // per

    def column(p, t):
        place = bases[0]
        for q in range(1, parts):
            place = place + jnp.where(p >= q, bases[q] - bases[q - 1], 0)
        return place * steps + t

    grad = pl.BlockSpec((ranks // TEAM, per, rows, share), lambda p, t: (0, t, 0, p))
    wide = pl.BlockSpec((1, rows, lanes), lambda p, t: (0, 0, column(p, t)))
    flat = pl.BlockSpec((rows, lanes), lambda p, t: (0, column(p, t)))
    extra = [] if written is None else list(written)
    state = jax.ShapeDtypeStruct(first.shape, FULL)
    plain = jax.ShapeDtypeStruct(master.shape, FULL)
    return pl.pallas_call(
        functools.partial(finish_kernel, reps, share),
        grid=(parts, steps),
        out_shape=[state, state, plain, plain, plain],
        in_specs=[grad, flat, wide, wide, flat, flat, flat] + [ANYWHERE] * len(extra),
        out_specs=[wide, wide, flat, flat, flat],
        input_output_aliases={7 + i: i for i in range(len(extra))},
        compiler_params=pltpu.CompilerParams(vmem_limit_bytes=VMEM_BYTES),
        name="finish_chunk",
    )(
        grads.reshape(ranks // TEAM, TEAM, rows, columns),
        master, first, second, outer, diff, other, *extra,
    )


def adam_kernel(share, grad, master, first, second, *refs):
    first_new, second_new, diff = refs[-3:]
    for t in range(grad.shape[1]):
        at = slice(t * share, (t + 1) * share)
        gradient = grad[0, t].astype(FULL)
        for top in range(1, grad.shape[0]):
            gradient = gradient + grad[top, t].astype(FULL)
        inner, first_new[0, :, at], second_new[0, :, at] = adam_step(
            master[:, at], gradient, first[0, :, at], second[0, :, at]
        )
        diff[:, at] = (master[:, at] - inner).astype(LOW)


def chunk_specs(tops, rows, bases, share, lanes):
    per = lanes // share
    steps = TEAM // per
    parts = len(bases)

    def column(p, t):
        place = bases[0]
        for q in range(1, parts):
            place = place + jnp.where(p >= q, bases[q] - bases[q - 1], 0)
        return place * steps + t

    return (
        (parts, steps),
        pl.BlockSpec((tops, per, rows, share), lambda p, t: (0, t, 0, p)),
        pl.BlockSpec((1, rows, lanes), lambda p, t: (0, 0, column(p, t))),
        pl.BlockSpec((rows, lanes), lambda p, t: (0, column(p, t))),
        pl.BlockSpec((rows, lanes), lambda p, t: (0, p * steps + t)),
    )


def adam_chunk(grads, master, first, second, bases):
    ranks, rows, columns = grads.shape
    share = columns // len(bases)
    tops = ranks // TEAM
    grid, grad, wide, flat, packed = chunk_specs(tops, rows, bases, share, max(LANES, share))
    state = jax.ShapeDtypeStruct(first.shape, FULL)
    return pl.pallas_call(
        functools.partial(adam_kernel, share),
        grid=grid,
        out_shape=[
            state,
            state,
            jax.ShapeDtypeStruct((rows, TEAM * len(bases) * share), LOW),
        ],
        in_specs=[grad, flat, wide, wide],
        out_specs=[wide, wide, packed],
        compiler_params=pltpu.CompilerParams(vmem_limit_bytes=VMEM_BYTES),
        name="adam_chunk",
    )(grads.reshape(tops, TEAM, rows, columns), master, first, second)


def outer_kernel(reps, diff, other, master, momentum, *refs):
    mean_out, new, momentum_new = refs[-3:]
    mean = (diff[...].astype(FULL) + other[...].astype(FULL)) / reps
    mean_out[...] = mean
    new[...], momentum_new[...] = outer_step(master[...], mean, momentum[...])


def outer_chunk(reps, diff, other, master, momentum, bases):
    rows = master.shape[0]
    share = diff.shape[1] // (TEAM * len(bases))
    grid, _, _, flat, packed = chunk_specs(1, rows, bases, share, max(LANES, share))
    return pl.pallas_call(
        functools.partial(outer_kernel, reps),
        grid=grid,
        out_shape=[jax.ShapeDtypeStruct(master.shape, FULL)] * 3,
        in_specs=[packed, packed, flat, flat],
        out_specs=[flat] * 3,
        compiler_params=pltpu.CompilerParams(vmem_limit_bytes=VMEM_BYTES),
        name="outer_chunk",
    )(diff, other, master, momentum)


def on_device(
    reps,
    ranks,
    tokens,
    cotangent,
    branch,
    att_master,
    att_first,
    att_second,
    att_outer,
    mlp_master,
    mlp_first,
    mlp_second,
    mlp_outer,
):
    units, length, width = tokens.shape
    hidden_width = mlp_master.shape[1] // 3
    depth = HEAD_DIM
    count = units * length
    rows = att_master.shape[0]
    team = TEAM
    tops = ranks // team
    all_tokens = team * count
    att_share = width // team
    hid_share = hidden_width // team
    me = lax.axis_index("dp")
    rep = lax.axis_index("rep")
    top = me // team

    def hop(values, other):
        pairs = [(r * ranks + i, r * ranks + (i ^ other)) for r in range(reps) for i in range(ranks)]
        return lax.ppermute(values, ("rep", "dp"), pairs)

    def swap(values):
        pairs = [(r * ranks + i, (1 - r) * ranks + i) for r in range(reps) for i in range(ranks)]
        return lax.ppermute(values, ("rep", "dp"), pairs)

    flat_low = tokens.reshape(count, width)
    flat = flat_low.astype(FULL)
    cot = cotangent.reshape(count, width)
    seen_all = jnp.stack([branch if k == 0 else hop(branch, k) for k in range(team)])
    seen_all = seen_all.reshape(team * units, CONT)
    position, allowed = jax.vmap(lambda seen: token_layout(seen, length))(seen_all)
    cosine, sine = jax.vmap(lambda places: rotary_tables(places, depth))(position)
    bias = jnp.where(allowed, 0.0, -1e30).astype(FULL)
    wide_cosine = jnp.concatenate([cosine, cosine], axis=-1).reshape(team, count, depth)
    wide_sine = jnp.concatenate([-sine, sine], axis=-1).reshape(team, count, depth)
    att_pack = pack_shares(att_master, [0, team, 2 * team, 3 * team], att_share)
    (
        normed_one,
        grad_fed,
        att_low,
        gate_low,
        down_low,
        _,
        _,
        projected,
        mixed,
        resid,
        normed_two,
        gate_value,
        up_value,
        hidden,
    ) = forward_layer(
        ranks,
        flat_low,
        normalize(flat)[0].astype(LOW),
        cot,
        att_pack,
        mlp_master,
        wide_cosine,
        wide_sine,
        bias,
    )
    (
        grad_resid,
        one_folded,
        two_folded,
        got_att,
        got_gate,
        got_down,
        mlp_diff,
        mlp_other,
        *_,
    ) = backward_layer(
        ranks,
        (resid, cot),
        (mlp_master, mlp_first, mlp_second),
        wide_cosine,
        wide_sine,
        bias,
        grad_fed.reshape(all_tokens, width),
        hidden.reshape(all_tokens, hid_share),
        gate_value.reshape(all_tokens, hid_share),
        up_value.reshape(all_tokens, hid_share),
        normed_two.reshape(all_tokens, width),
        normed_one.reshape(all_tokens, width),
        projected,
        mixed.reshape(all_tokens, att_share),
        att_low,
        gate_low,
        down_low,
    )
    def unfold(folded):
        terms = (folded[0], hop(folded[1], 2), hop(folded[2], 4))
        return sum(term.astype(FULL) for term in terms)

    grad_normed_one, fed = unfold(one_folded), unfold(two_folded)
    grad_tokens = grad_resid + normalize_back(flat, grad_normed_one)
    out_tokens = (resid + fed).astype(LOW)
    mlp = (mlp_master, mlp_first, mlp_second, mlp_outer, mlp_diff, mlp_other)
    bases = [0, 1, 2, 3]
    *att_state, att_diff = adam_chunk(got_att, att_master, att_first, att_second, bases)
    mlp_out = finish_chunk(reps, got_down, *mlp, [2], None)
    mlp_out = finish_chunk(reps, got_gate, *mlp, [0, 1], mlp_out)
    att_new = outer_chunk(reps, att_diff, swap(att_diff), att_master, att_outer, bases)
    return (
        out_tokens.reshape(units, length, width),
        grad_tokens.reshape(units, length, width),
        *(att_new[1], *att_state, att_new[0], att_new[2]),
        *(mlp_out[3], mlp_out[0], mlp_out[1], mlp_out[2], mlp_out[4]),
    )


def solution(mesh):
    in_specs = (
        P(("rep", "dp"), None, None),
        P(("rep", "dp"), None, None),
        P(("rep", "dp"), None),
        P("dp", None),
        P("rep", "dp", None),
        P("rep", "dp", None),
        P("dp", None),
        P("dp", None),
        P("rep", "dp", None),
        P("rep", "dp", None),
        P("dp", None),
    )
    out_specs = (
        P(("rep", "dp"), None, None),
        P(("rep", "dp"), None, None),
        P("dp", None),
        P("rep", "dp", None),
        P("rep", "dp", None),
        P("dp", None),
        P("dp", None),
        P("dp", None),
        P("rep", "dp", None),
        P("rep", "dp", None),
        P("dp", None),
        P("dp", None),
    )

    def body(*args):
        return on_device(mesh.shape["rep"], mesh.shape["dp"], *args)

    return jax.shard_map(
        body, mesh=mesh, in_specs=in_specs, out_specs=out_specs, check_vma=False
    )
```

```python
import functools
import math

import jax
import jax.numpy as jnp
from jax import lax
from jax.experimental import pallas as pl
from jax.experimental.pallas import tpu as pltpu
from jax.sharding import PartitionSpec as P

HEAD_DIM = 128
PROMPT = 128
CLEN = 64
CONT = 2
STEP = 10
TEAM = 8


LN_EPS = 1e-05
BETA_ONE = 0.9
BETA_TWO = 0.95
ADAM_EPS = 1e-08
DECAY = 0.1
RATE = 0.05
OUTER_RATE = 0.7
OUTER_MOMENTUM = 0.9
CONTRACT_LAST = (((1,), (1,)), ((), ()))
CONTRACT_FIRST = (((0,), (0,)), ((), ()))
LOW = jnp.bfloat16
FULL = jnp.float32


def normalize(values):
    centre = values - jnp.mean(values, axis=-1, keepdims=True)
    factor = lax.rsqrt(jnp.mean(centre * centre, axis=-1, keepdims=True) + LN_EPS)
    return (centre * factor, factor)


def normalize_back(values, gradient):
    normed, factor = normalize(values)
    projection = jnp.mean(gradient * normed, axis=-1, keepdims=True)
    return factor * (gradient - jnp.mean(gradient, axis=-1, keepdims=True) - normed * projection)


def token_layout(seen, length):
    places = jnp.arange(length, dtype=jnp.int32)
    segment = jnp.where(places < PROMPT, -1, (places - PROMPT) // CLEN)
    within = jnp.where(places < PROMPT, places, (places - PROMPT) % CLEN)
    lookup = jnp.arange(CONT, dtype=jnp.int32)
    reach = jnp.sum(jnp.where(segment[:, None] == lookup[None, :], seen[None, :], 0), axis=1)
    position = jnp.where(segment < 0, places, reach + within)
    allowed = (segment[:, None] == segment[None, :]) & (within[None, :] <= within[:, None]) | (
        segment[None, :] < 0
    ) & (segment[:, None] >= 0) & (places[None, :] < reach[:, None])
    return (position, allowed)


def rotary_tables(position, depth):
    half_depth = depth // 2
    freqs = jnp.exp(jnp.arange(half_depth, dtype=jnp.float32) * (-2.0 * math.log(10000.0) / depth))
    angle = position.astype(jnp.float32)[:, None] * freqs[None, :]
    return (jnp.cos(angle)[:, None, :], jnp.sin(angle)[:, None, :])


def rotate(values, cosine, sine):
    half_depth = values.shape[-1] // 2
    first = values[..., :half_depth]
    second = values[..., half_depth:]
    return jnp.concatenate(
        [first * cosine - second * sine, second * cosine + first * sine], axis=-1
    )


def rotate_back(gradient, cosine, sine):
    half_depth = gradient.shape[-1] // 2
    first = gradient[..., :half_depth]
    second = gradient[..., half_depth:]
    return jnp.concatenate(
        [first * cosine + second * sine, second * cosine - first * sine], axis=-1
    )


def adam_step(master, gradient, first, second):
    first_new = BETA_ONE * first + (1.0 - BETA_ONE) * gradient
    second_new = BETA_TWO * second + (1.0 - BETA_TWO) * gradient * gradient
    ratio = (
        first_new
        / (1.0 - BETA_ONE**STEP)
        / (jnp.sqrt(second_new / (1.0 - BETA_TWO**STEP)) + ADAM_EPS)
    )
    return (master - RATE * (ratio + DECAY * master), first_new, second_new)


def outer_step(master, mean_diff, momentum):
    momentum_new = OUTER_MOMENTUM * momentum + mean_diff
    return (master - OUTER_RATE * (mean_diff + OUTER_MOMENTUM * momentum_new), momentum_new)


def dot(left, right, dims=(((1,), (0,)), ((), ()))):
    return lax.dot_general(left, right, dims, preferred_element_type=FULL)


MESH = pl.DeviceIdType.MESH
ANYWHERE = pl.BlockSpec(memory_space=pl.ANY)
BITS = (1, 2, 4)
PIECES = 4
GATE_AHEAD, GATE_MIDDLE = 7, 3
DOWN_EARLY = 15
FEED_EARLY = 6
SPLIT_TOKENS, SPLIT_ATTENDED, SPLIT_NORMED, SPLIT_COT, SPLIT_BACK = 3, 3, 2, 2, 3
STRIP = 16
GATHER_COPIES = 6 * PIECES + 1
VMEM_BYTES = 60 * 1024 * 1024


def flip(me, bit):
    return me + bit - 2 * bit * ((me // bit) % 2)


def across(me, other):
    bit = 1
    while bit <= other:
        if other & bit:
            me = flip(me, bit)
        bit *= 2
    return me


def greet(me, others, with_rep):
    barrier = pltpu.get_barrier_semaphore()
    for other in others:
        pl.semaphore_signal(
            barrier, inc=1, device_id={"dp": across(me, other)}, device_id_type=MESH
        )
    if with_rep:
        rep = lax.axis_index("rep")
        pl.semaphore_signal(barrier, inc=1, device_id={"rep": 1 - rep}, device_id_type=MESH)
    pl.semaphore_wait(barrier, len(others) + (1 if with_rep else 0))


class Sender:
    def __init__(self, sent, came):
        self.sent, self.came, self.index = sent, came, 0

    def __call__(self, source, target, where):
        copy = pltpu.make_async_remote_copy(
            src_ref=source,
            dst_ref=target,
            send_sem=self.sent.at[self.index],
            recv_sem=self.came.at[self.index],
            device_id=where,
            device_id_type=MESH,
        )
        copy.start()
        self.index += 1
        return copy


class TeamGather:
    def __init__(self, me, own, out, send, split):
        self.out, self.send, self.split = out, send, split
        self.piece = own.shape[0] // PIECES
        self.core, self.second, self.third = ({"dp": flip(me, bit)} for bit in BITS)
        self.late = list(range(split, PIECES)) + list(range(split))
        self.early = list(range(PIECES))
        self.own = own
        self.over_second, self.over_third, self.corner = {}, {}, {}
        self.rest, self.settled = [], []

    def cut(self, ref, p):
        return ref.at[pl.ds(p * self.piece, self.piece)]

    def begin(self):
        own, out, cut = self.own, self.out, self.cut
        for a, b in zip(self.late, self.early):
            self.over_second[a] = self.send(cut(own, a), cut(out.at[2], a), self.second)
            self.over_third[b] = self.send(cut(own, b), cut(out.at[4], b), self.third)
        self.rest.append(self.send(own, out.at[1], self.core))

    def turn(self):
        out, cut, send = self.out, self.cut, self.send
        for a, b in zip(self.late, self.early):
            self.over_second[a].wait_recv()
            if a >= self.split:
                self.corner[a] = send(cut(out.at[2], a), cut(out.at[6], a), self.third)
            self.rest.append(send(cut(out.at[2], a), cut(out.at[3], a), self.core))
            self.over_third[b].wait_recv()
            if b < self.split:
                self.corner[b] = send(cut(out.at[4], b), cut(out.at[6], b), self.second)
            self.rest.append(send(cut(out.at[4], b), cut(out.at[5], b), self.core))

    def settle(self):
        for copy in self.rest:
            copy.wait_recv()
        self.settled, self.rest = self.rest, []

    def finish(self):
        for p, copy in self.corner.items():
            copy.wait_recv()
            at = self.cut(self.out.at[6], p), self.cut(self.out.at[7], p)
            self.rest.append(self.send(*at, self.core))
        for group in (self.over_second, self.over_third, self.corner):
            for copy in group.values():
                copy.wait_send()
        for copy in self.settled:
            copy.wait_send()
        for copy in self.rest:
            copy.wait()


SUM_COPIES = 6


def sum_scratch(count, width):
    return [
        pltpu.VMEM((TEAM // 2, count, width), LOW),
        pltpu.VMEM((TEAM // 2, count, width), LOW),
        pltpu.VMEM((3, count, width), LOW),
    ]


def fold_steps(me, own, got, edge, first, send, split):
    count = own.shape[1]
    _, second, third = ({"dp": flip(me, bit)} for bit in BITS)
    spans = [pl.ds(0, split), pl.ds(split, count - split)]

    def add(j, span, extra=None):
        @pl.loop(0, span.size // STRIP)
        def _(step):
            at = pl.ds(span.start + step * STRIP, STRIP)
            value = own[j, at].astype(FULL)
            if extra is None:
                value = value + got[j, at].astype(FULL)
            else:
                value = value + extra[at].astype(FULL)
            own[j, at] = value.astype(LOW)

    whole = pl.ds(0, count)
    first[3].wait_recv()
    add(3, whole)
    corners = [
        send(own.at[3].at[span], edge.at[0].at[span], where)
        for span, where in zip(spans, (second, third))
    ]
    for j in (2, 1, 0):
        first[j].wait_recv()
        add(j, whole)
    yield
    for j, span, copy in zip((2, 1), spans, corners):
        copy.wait_recv()
        add(j, span, edge.at[0])
    for copy in corners + [first[j] for j in range(4)]:
        copy.wait_send()


def fold_parts(me, parts, own, got, edge, send, loads, split):
    core = {"dp": flip(me, 1)}
    loading = [pltpu.make_async_copy(parts.at[2 * j], own.at[j], loads.at[j]) for j in range(4)]
    first = {}
    for j in (3, 2, 1, 0):
        loading[j].start()
        first[j] = send(parts.at[2 * j + 1], got.at[j], core)
    for copy in loading:
        copy.wait()
    yield from fold_steps(me, own, got, edge, first, send, split)


def sum_steps(me, own, got, edge, first, send, total, split):
    count = own.shape[1]
    _, second, third = ({"dp": flip(me, bit)} for bit in BITS)
    spans = [pl.ds(0, split), pl.ds(split, count - split)]

    def add(j, h, extra=None):
        span = spans[h]

        @pl.loop(0, span.size // STRIP)
        def _(step):
            at = pl.ds(span.start + step * STRIP, STRIP)
            value = own[j, at].astype(FULL) + got[j, at].astype(FULL)
            if extra is not None:
                value = value + extra[at].astype(FULL)
            own[j, at] = value.astype(LOW)

    def go(j, h, slot, where):
        return send(own.at[j].at[spans[h]], edge.at[slot].at[spans[h]], where)

    both = split < count
    sends = []
    first[3].wait_recv()
    add(3, 0)
    corner_second = go(3, 0, 0, second)
    if both:
        add(3, 1)
        corner_third = go(3, 1, 0, third)
        sends.append(corner_third)
        first[2].wait_recv()
        add(2, 1)
        sends.append(go(2, 1, 2, third))
    first[1].wait_recv()
    add(1, 0)
    sends.append(go(1, 0, 1, second))
    yield
    if not both:
        first[2].wait_recv()
    corner_second.wait_recv()
    add(2, 0, edge.at[0])
    sends.append(go(2, 0, 2, third))
    if both:
        corner_third.wait_recv()
        add(1, 1, edge.at[0])
        sends.append(go(1, 1, 1, second))
    yield
    first[0].wait_recv()
    for copy in sends:
        if not both or copy is not corner_third:
            copy.wait_recv()

    @pl.loop(0, count // STRIP)
    def _(step):
        start = step * STRIP
        at = pl.ds(start, STRIP)
        value = own[0, at].astype(FULL) + got[0, at].astype(FULL)
        total(start, value + edge[1, at].astype(FULL) + edge[2, at].astype(FULL))

    for copy in sends + [corner_second] + [first[j] for j in range(4)]:
        copy.wait_send()


def params(collective_id):
    return pltpu.CompilerParams(
        collective_id=collective_id, has_side_effects=True, vmem_limit_bytes=VMEM_BYTES
    )


def strip_normalize(value):
    width = value.shape[1]
    centre = value - jnp.sum(value, axis=1, keepdims=True) * (1.0 / width)
    factor = lax.rsqrt(jnp.sum(centre * centre, axis=1, keepdims=True) * (1.0 / width) + LN_EPS)
    return (centre * factor, factor)


UNIT = 256


def unit_of(step):
    return 2 * (TEAM // 2 - 1 - step % (TEAM // 2)) + jnp.where(step < TEAM // 2, 1, 0)


def stream(steps, loads, body, arrive=None):
    if arrive is not None:
        arrive(0)
    for copy in loads(0, 0):
        copy.start()

    @pl.loop(0, steps)
    def _(step):
        slot = step % 2

        @pl.when(step + 1 < steps)
        def _():
            if arrive is not None:
                arrive(step + 1)
            for copy in loads(step + 1, 1 - slot):
                copy.start()

        for copy in loads(step, slot):
            copy.wait()
        body(step, slot)


def stream_out(steps, loads, stores, body):
    def whole(step, slot):
        @pl.when(step >= 2)
        def _():
            for copy in stores(step - 2, slot):
                copy.wait()

        body(step, slot)
        for copy in stores(step, slot):
            copy.start()

    stream(steps, loads, whole)
    for step in (steps - 2, steps - 1):
        for copy in stores(step, step % 2):
            copy.wait()


def rows_at(step, size):
    return pl.ds(pl.multiple_of(step * size, size), size)


class RowGather:
    def __init__(self, ranks, me, rep, weights, send, send_x, local):
        self.me, self.rep, self.weights, self.local = me, rep, weights, local
        self.send, self.send_x = send, send_x
        self.rows = weights.shape[0] // ranks
        self.half = self.rows // 2
        self.order = list(range(1, ranks))
        self.ways, self.swaps = {}, []

    def place(self, device):
        return self.weights.at[pl.ds(device * self.rows + self.rep * self.half, self.half)]

    def begin(self, pack, number=None):
        me, rep = self.me, self.rep
        if not self.ways:
            at = self.weights.at[pl.ds(me * self.rows, self.rows)]
            self.own = pltpu.make_async_copy(pack.at[me % TEAM], at, self.local)
            self.own.start()
        started = len(self.ways)
        number = len(self.order) - started if number is None else number
        for other in self.order[started : started + number]:
            where = across(me, other)
            source = pack.at[where % TEAM, pl.ds(rep * self.half, self.half)]
            self.ways[other] = self.send(source, self.place(me), {"dp": where})

    def forward(self, number=None):
        done = len(self.swaps)
        number = len(self.order) - done if number is None else number
        for other in self.order[done : done + number]:
            self.ways[other].wait_recv()
            at = self.place(across(self.me, other))
            self.swaps.append(self.send_x(at, at, {"rep": 1 - self.rep}))

    def finish(self):
        for copy in self.ways.values():
            copy.wait_send()
        for copy in self.swaps + [self.own]:
            copy.wait()


def attend_unit(values, cosine, sine, bias, share):
    depth = HEAD_DIM
    parts = []
    for p in range(2):
        turned = []
        for at in range(p * share, (p + 1) * share, depth):
            head = values[:, at : at + depth]
            turned.append((head * cosine + pltpu.roll(head, depth // 2, 1) * sine).astype(LOW))
        parts.append(turned)
    query, keys = parts
    value = [
        values[:, at : at + depth].astype(LOW) for at in range(2 * share, 3 * share, depth)
    ]
    mixed = []
    for one, two, three in zip(query, keys, value):
        scores = dot(one, two, CONTRACT_LAST) * depth ** (-0.5) + bias
        powers = jnp.exp(scores - jnp.max(scores, axis=1, keepdims=True))
        prob = powers / jnp.sum(powers, axis=1, keepdims=True)
        mixed.append(dot(prob.astype(LOW), three).astype(LOW))
    return jnp.concatenate(query + keys + value, axis=1), jnp.concatenate(mixed, axis=1)


def forward_kernel(
    ranks,
    flat,
    normed_own,
    cot,
    att_pack,
    mlp_master,
    cosine,
    sine,
    bias,
    normed_all,
    cot_all,
    att_weights,
    gate_weights,
    down_weights,
    gate_pack,
    down_pack,
    projected_all,
    mixed_all,
    resid,
    normed_two_all,
    gate_all,
    up_all,
    hidden_all,
    att,
    gate,
    block,
    odd,
    own,
    got,
    edge,
    normed,
    *sems,
):
    sent_team, came_team, sent_rows, came_rows, sent_x, came_x, first_sent, first_came, local = sems
    me = lax.axis_index("dp")
    rep = lax.axis_index("rep")
    rows, share = att_pack.shape[1], att_pack.shape[2] // 4
    hid = gate_pack.shape[2] // 2
    core = {"dp": flip(me, 1)}
    greet(me, range(1, ranks), True)
    send = Sender(sent_team, came_team)
    send_rows = Sender(sent_rows, came_rows)
    send_x = Sender(sent_x, came_x)
    tokens = TeamGather(me, normed_own, normed_all, send, SPLIT_TOKENS)
    tokens.begin()
    gathers = [
        RowGather(ranks, me, rep, weights, send_rows, send_x, local.at[i])
        for i, weights in enumerate((att_weights, gate_weights, down_weights))
    ]
    gathers[0].begin(att_pack)
    keep = [pltpu.make_async_copy(normed_own, normed_all.at[0], local.at[3])]
    keep.append(pltpu.make_async_copy(cot, cot_all.at[0], local.at[4]))
    for copy in keep:
        copy.start()

    def pack(wide, low):
        def loads(t, slot):
            return [
                pltpu.make_async_copy(
                    mlp_master.at[:, rows_at(p * TEAM + t, hid)],
                    wide.at[slot, p],
                    local.at[5 + 3 * slot + p],
                )
                for p in range(3)
            ]

        def stores(t, slot):
            near = low.at[slot]
            return [
                pltpu.make_async_copy(
                    near.at[:, pl.ds(0, 2 * hid)], gate_pack.at[t], local.at[11 + slot]
                ),
                pltpu.make_async_copy(
                    near.at[:, pl.ds(2 * hid, hid)], down_pack.at[t], local.at[13 + slot]
                ),
            ]

        def body(t, slot):
            for p in range(3):
                low[slot, :, p * hid : (p + 1) * hid] = wide[slot, p].astype(LOW)

        stream_out(TEAM, loads, stores, body)

    pl.run_scoped(
        pack, pltpu.VMEM((2, 3, rows, hid), FULL), pltpu.VMEM((2, rows, 3 * hid), LOW)
    )
    tokens.turn()
    gathers[1].begin(gate_pack)
    gathers[0].forward()
    tokens.finish()
    gathers[0].finish()
    for copy in keep:
        copy.wait()
    load = pltpu.make_async_copy(att_weights, att, local.at[0])
    load.start()
    load.wait()

    gathers[1].forward(GATE_AHEAD)

    def fetch(step, slot):
        return pltpu.make_async_copy(
            normed_all.at[unit_of(step)], block.at[slot], local.at[5 + slot]
        )

    fetch(0, 0).start()

    @pl.loop(0, TEAM)
    def _(step):
        slot = step % 2
        unit = unit_of(step)

        @pl.when(step + 1 < TEAM)
        def _():
            fetch(step + 1, 1 - slot).start()

        fetch(step, slot).wait()
        values = dot(block[slot], att[:, : 3 * share])
        projected, mixed = attend_unit(values, cosine[unit], sine[unit], bias[unit], share)
        projected_all[unit] = projected
        mixed_all[unit] = mixed
        term = dot(mixed, att[:, 3 * share :], CONTRACT_LAST).astype(LOW)
        j = unit // 2

        @pl.when(step < TEAM // 2)
        def _():
            odd[j] = term
            pltpu.make_async_remote_copy(
                src_ref=odd.at[j],
                dst_ref=got.at[j],
                send_sem=first_sent.at[j],
                recv_sem=first_came.at[j],
                device_id=core,
                device_id_type=MESH,
            ).start()

        @pl.when(step >= TEAM // 2)
        def _():
            own[j] = term

    first = [
        pltpu.make_async_remote_copy(
            src_ref=odd.at[j],
            dst_ref=got.at[j],
            send_sem=first_sent.at[j],
            recv_sem=first_came.at[j],
            device_id=core,
            device_id_type=MESH,
        )
        for j in range(TEAM // 2)
    ]

    def total(start, value):
        at = pl.ds(start, STRIP)
        value = value + flat[at].astype(FULL)
        resid[at] = value
        normed[at] = strip_normalize(value)[0].astype(LOW)

    steps = sum_steps(me, own, got, edge, first, send, total, SPLIT_ATTENDED * UNIT // PIECES)
    next(steps)
    early = DOWN_EARLY * (ranks - 1) // 15
    gathers[2].begin(down_pack, early)
    gathers[1].forward(GATE_MIDDLE * (ranks - TEAM) // TEAM)
    next(steps)
    for _ in steps:
        pass
    tokens = TeamGather(me, normed, normed_two_all, send, SPLIT_NORMED)
    tokens.begin()
    gathers[2].begin(down_pack)
    cots = TeamGather(me, cot, cot_all, send, SPLIT_COT)
    cots.begin()
    keep = pltpu.make_async_copy(normed, normed_two_all.at[0], local.at[3])
    keep.start()
    gathers[1].forward()
    gathers[2].forward(early)
    tokens.turn()
    keep.wait()
    gathers[1].finish()
    tokens.settle()
    load = pltpu.make_async_copy(gate_weights, gate, local.at[1])
    load.start()
    load.wait()

    def feed(base, low):
        def loads(step, slot):
            source = normed_two_all.at[base + step]
            return [pltpu.make_async_copy(source, block.at[slot], local.at[5 + slot])]

        def stores(step, slot):
            return [
                pltpu.make_async_copy(
                    low.at[slot, i], out.at[base + step], local.at[7 + 3 * slot + i]
                )
                for i, out in enumerate((gate_all, up_all, hidden_all))
            ]

        def body(step, slot):
            @pl.loop(0, hid // UNIT)
            def _(column):
                at = rows_at(column, UNIT)
                later = pl.ds(pl.multiple_of(hid + column * UNIT, UNIT), UNIT)
                gate_value = dot(block[slot], gate[:, at])
                up_value = dot(block[slot], gate[:, later])
                low[slot, 0, :, at] = gate_value.astype(LOW)
                low[slot, 1, :, at] = up_value.astype(LOW)
                hidden = gate_value * jax.nn.sigmoid(gate_value) * up_value
                low[slot, 2, :, at] = hidden.astype(LOW)

        stream_out(FEED_EARLY if base == 0 else TEAM - FEED_EARLY, loads, stores, body)

    fed = pltpu.VMEM((2, 3, normed.shape[0], hid), LOW)
    pl.run_scoped(functools.partial(feed, 0), fed)
    tokens.finish()
    cots.turn()
    gathers[2].forward()
    pl.run_scoped(functools.partial(feed, FEED_EARLY), fed)
    cots.finish()
    gathers[2].finish()


def forward_layer(ranks, flat, normed, cot, att_pack, mlp_master, cosine, sine, bias):
    count, width = normed.shape
    rows, share = att_pack.shape[1], att_pack.shape[2] // 4
    hid = mlp_master.shape[1] // (3 * TEAM)
    gathered = jax.ShapeDtypeStruct((TEAM, count, width), LOW)
    hidden = jax.ShapeDtypeStruct((TEAM, count, hid), LOW)
    vmem = pl.BlockSpec(memory_space=pltpu.VMEM)

    def weights(columns):
        return jax.ShapeDtypeStruct((ranks * rows, columns), LOW)

    def packs(columns):
        return jax.ShapeDtypeStruct((TEAM, rows, columns), LOW)

    out = [
        (gathered, ANYWHERE),
        (gathered, ANYWHERE),
        (weights(4 * share), ANYWHERE),
        (weights(2 * hid), ANYWHERE),
        (weights(hid), ANYWHERE),
        (packs(2 * hid), ANYWHERE),
        (packs(hid), ANYWHERE),
        (jax.ShapeDtypeStruct((TEAM, count, 3 * share), LOW), vmem),
        (jax.ShapeDtypeStruct((TEAM, count, share), LOW), vmem),
        (jax.ShapeDtypeStruct((count, width), FULL), vmem),
        (gathered, ANYWHERE),
        (hidden, ANYWHERE),
        (hidden, ANYWHERE),
        (hidden, ANYWHERE),
    ]
    team_copies = 3 * GATHER_COPIES + SUM_COPIES
    pairs = [team_copies] * 2 + [3 * (ranks - 1)] * 4 + [TEAM // 2] * 2 + [15]
    return pl.pallas_call(
        functools.partial(forward_kernel, ranks),
        out_shape=[shape for shape, _ in out],
        in_specs=[vmem] + [ANYWHERE] * 4 + [vmem] * 3,
        out_specs=[spec for _, spec in out],
        scratch_shapes=[
            pltpu.VMEM((ranks * rows, 4 * share), LOW),
            pltpu.VMEM((ranks * rows, 2 * hid), LOW),
            pltpu.VMEM((2, count, width), LOW),
            pltpu.VMEM((TEAM // 2, count, width), LOW),
            pltpu.VMEM((TEAM // 2, count, width), LOW),
            pltpu.VMEM((TEAM // 2, count, width), LOW),
            pltpu.VMEM((3, count, width), LOW),
            pltpu.VMEM((count, width), LOW),
        ]
        + [pltpu.SemaphoreType.DMA((number,)) for number in pairs],
        compiler_params=params(0),
        name="forward_layer",
    )(flat, normed, cot, att_pack, mlp_master, cosine, sine, bias)


def attend_unit_back(values, given, cosine, sine, bias, share):
    depth = HEAD_DIM
    scale = depth ** (-0.5)
    grads = ([], [], [])
    for at in range(0, share, depth):
        query, keys, value = (values[:, p * share + at : p * share + at + depth] for p in range(3))
        grad = given[:, at : at + depth]
        scores = dot(query, keys, CONTRACT_LAST) * scale + bias
        powers = jnp.exp(scores - jnp.max(scores, axis=1, keepdims=True))
        prob = powers / jnp.sum(powers, axis=1, keepdims=True)
        grad_prob = dot(grad, value, CONTRACT_LAST)
        grad_value = dot(prob.astype(LOW), grad, CONTRACT_FIRST)
        along = jnp.sum(grad_prob * prob, axis=1, keepdims=True)
        grad_scores = (prob * (grad_prob - along)).astype(LOW)
        turned = (
            dot(grad_scores, keys) * scale,
            dot(grad_scores, query, CONTRACT_FIRST) * scale,
        )
        for p in range(2):
            back = turned[p] * cosine - pltpu.roll(turned[p], depth // 2, 1) * sine
            grads[p].append(back.astype(LOW))
        grads[2].append(grad_value.astype(LOW))
    return jnp.concatenate(grads[0] + grads[1] + grads[2], axis=1)


class Terms:
    def __init__(self, me, odd, own, got, sent, came):
        self.odd, self.own, self.got, self.sent, self.came = odd, own, got, sent, came
        self.core = {"dp": flip(me, 1)}

    def copy(self, j):
        return pltpu.make_async_remote_copy(
            src_ref=self.odd.at[j],
            dst_ref=self.got.at[j],
            send_sem=self.sent.at[j],
            recv_sem=self.came.at[j],
            device_id=self.core,
            device_id_type=MESH,
        )

    def put(self, step, term):
        j = unit_of(step) // 2

        @pl.when(step < TEAM // 2)
        def _():
            self.odd[j] = term
            self.copy(j).start()

        @pl.when(step >= TEAM // 2)
        def _():
            self.own[j] = term

    def first(self):
        return [self.copy(j) for j in range(TEAM // 2)]


LOWS = (0, 4, 2, 6, 1, 5, 3, 7)


def backward_kernel(
    ranks,
    resid,
    cot,
    cosine,
    sine,
    bias,
    cot_all,
    hidden_all,
    gate_all,
    up_all,
    normed_two_all,
    normed_one_all,
    projected_all,
    mixed_all,
    att_weights,
    gate_weights,
    down_weights,
    mlp_master,
    mlp_first,
    mlp_second,
    grad_resid,
    one_folded,
    two_folded,
    got_att,
    got_gate,
    got_down,
    mlp_diff,
    mlp_other,
    grad_all,
    att_grad,
    gate_grad,
    down_grad,
    fed_all,
    own,
    got,
    edge,
    odd,
    own_two,
    got_two,
    edge_two,
    grad_low,
    stage,
    wide,
    sent,
    came,
    sent_rows,
    came_rows,
    sent_first,
    came_first,
    sent_x,
    came_x,
    kept,
    local,
):
    me = lax.axis_index("dp")
    rep = lax.axis_index("rep")
    tops = ranks // TEAM
    rows = got_att.shape[1]
    share = mixed_all.shape[1]
    hid = hidden_all.shape[1]
    count, width = resid.shape
    tokens = TEAM * count
    tiles = width // UNIT
    greet(me, range(1, ranks), True)
    send = Sender(sent, came)
    order = []
    for low_bits in LOWS:
        order += [top * TEAM + low_bits for top in range(1, tops)]
        order += [low_bits] if low_bits else []

    chunks = ((down_grad, got_down), (gate_grad, got_gate), (att_grad, got_att))

    def block_copy(chunk, other):
        grad, target = chunks[chunk]
        index = chunk * (ranks - 1) + other - 1
        where = across(me, other)
        return pltpu.make_async_remote_copy(
            src_ref=grad.at[pl.ds(where * rows, rows)],
            dst_ref=target.at[me],
            send_sem=sent_rows.at[index],
            recv_sem=came_rows.at[index],
            device_id={"dp": where},
            device_id_type=MESH,
        )

    def keep_own(grad, target, index):
        copy = pltpu.make_async_copy(
            grad.at[pl.ds(me * rows, rows)], target.at[me], kept.at[index]
        )
        copy.start()
        return copy

    def down_phase(hidden, tile, low):
        whole = pltpu.make_async_copy(hidden_all, hidden, local.at[0])
        whole.start()

        def loads(step, slot):
            at = rows_at(step, UNIT)
            return [pltpu.make_async_copy(cot_all.at[:, at], tile.at[slot], local.at[2 + slot])]

        def stores(step, slot):
            at = rows_at(step, UNIT)
            return [pltpu.make_async_copy(low.at[slot], down_grad.at[at], local.at[4 + slot])]

        def body(step, slot):
            low[slot] = dot(tile[slot], hidden[...], CONTRACT_FIRST).astype(LOW)

        whole.wait()
        stream_out(tiles, loads, stores, body)

    pl.run_scoped(
        down_phase,
        pltpu.VMEM((tokens, hid), LOW),
        pltpu.VMEM((2, tokens, UNIT), LOW),
        pltpu.VMEM((2, UNIT, hid), LOW),
    )
    for other in order:
        block_copy(0, other).start()
    own_copies = [keep_own(down_grad, got_down, 0)]

    gate_order = list(order)

    def more(number):
        for _ in range(min(number, len(gate_order))):
            block_copy(1, gate_order.pop(0)).start()

    terms = Terms(me, odd, own, got, sent_first.at[0], came_first.at[0])

    grad_gate = wide.at[pl.ds(0, tokens), pl.ds(0, 2 * hid)]

    def hidden_phase(down, block, gate, up):
        whole = pltpu.make_async_copy(down_weights, down, local.at[1])
        whole.start()

        def loads(step, slot):
            at = rows_at(step, count)
            return [
                pltpu.make_async_copy(cot_all.at[at], block.at[slot], local.at[2 + slot]),
                pltpu.make_async_copy(gate_all.at[at], gate.at[slot], local.at[4 + slot]),
                pltpu.make_async_copy(up_all.at[at], up.at[slot], local.at[6 + slot]),
            ]

        def body(step, slot):
            at = rows_at(step, count)

            @pl.loop(0, hid // UNIT)
            def _(column):
                place = rows_at(column, UNIT)
                later = pl.ds(pl.multiple_of(hid + column * UNIT, UNIT), UNIT)
                grad = dot(block[slot], down[:, place])
                value = gate[slot, :, place].astype(FULL)
                sigmoid = jax.nn.sigmoid(value)
                slope = sigmoid * (1.0 + value * (1.0 - sigmoid))
                up_value = up[slot, :, place].astype(FULL)
                grad_gate[at, place] = (grad * up_value * slope).astype(LOW)
                grad_gate[at, later] = (grad * value * sigmoid).astype(LOW)

        whole.wait()
        stream(TEAM, loads, body)

    pl.run_scoped(
        hidden_phase,
        pltpu.VMEM((width, hid), LOW),
        pltpu.VMEM((2, count, width), LOW),
        pltpu.VMEM((2, count, hid), LOW),
        pltpu.VMEM((2, count, hid), LOW),
    )

    def back_phase(gate):
        whole = pltpu.make_async_copy(gate_weights, gate, local.at[0])
        whole.start()
        whole.wait()

        @pl.loop(0, TEAM)
        def _(step):
            at = rows_at(unit_of(step), count)
            terms.put(step, dot(grad_gate[at, :], gate[...], CONTRACT_LAST).astype(LOW))

    pl.run_scoped(back_phase, pltpu.VMEM((width, 2 * hid), LOW))

    def weight_phase(tile, low):
        def loads(step, slot):
            at = rows_at(step, UNIT)
            return [
                pltpu.make_async_copy(
                    normed_two_all.at[:, at], tile.at[slot], local.at[2 + slot]
                )
            ]

        def stores(step, slot):
            at = rows_at(step, UNIT)
            return [pltpu.make_async_copy(low.at[slot], gate_grad.at[at], local.at[4 + slot])]

        def body(step, slot):
            low[slot] = dot(tile[slot], grad_gate[...], CONTRACT_FIRST).astype(LOW)

        stream_out(tiles, loads, stores, body)


    def resid_total(start, value):
        at = pl.ds(start, STRIP)
        normed, factor = strip_normalize(resid[at])
        along = jnp.sum(value * normed, axis=1, keepdims=True) * (1.0 / width)
        middle = jnp.sum(value, axis=1, keepdims=True) * (1.0 / width)
        value = cot[at].astype(FULL) + factor * (value - middle - normed * along)
        grad_resid[at] = value
        grad_low[at] = value.astype(LOW)

    split = SPLIT_BACK * UNIT // PIECES
    steps = sum_steps(me, own, got, edge, terms.first(), send, resid_total, split)
    next(steps)
    pl.run_scoped(
        weight_phase, pltpu.VMEM((2, tokens, UNIT), LOW), pltpu.VMEM((2, UNIT, 2 * hid), LOW)
    )
    own_copies.append(keep_own(gate_grad, got_gate, 1))
    more(GATE_FIRST)
    next(steps)
    more(GATE_LATE)
    for _ in steps:
        pass
    gather = TeamGather(me, grad_low, grad_all, send, SPLIT_BACK)
    gather.begin()
    more(GATE_GATHER)
    keep = pltpu.make_async_copy(grad_low, grad_all.at[0], local.at[8])
    keep.start()
    def fed_phase(hidden, down, term):
        whole = [
            pltpu.make_async_copy(hidden_all, hidden, local.at[0]),
            pltpu.make_async_copy(down_weights, down, local.at[1]),
        ]
        for copy in whole:
            copy.start()
        for copy in whole:
            copy.wait()

        def fed_stores(step, slot):
            return [pltpu.make_async_copy(term.at[slot], fed_all.at[step], local.at[6 + slot])]

        def fed_body(step, slot):
            term[slot] = dot(hidden[rows_at(step, count)], down[...], CONTRACT_LAST).astype(LOW)

        stream_out(TEAM, lambda step, slot: [], fed_stores, fed_body)

    pl.run_scoped(
        fed_phase,
        pltpu.VMEM((tokens, hid), LOW),
        pltpu.VMEM((width, hid), LOW),
        pltpu.VMEM((2, count, width), LOW),
    )
    gather.turn()
    more(len(gate_order))
    gather.finish()
    keep.wait()

    terms = Terms(me, odd, own, got, sent_first.at[1], came_first.at[1])

    def att_phase():
        att = wide.at[pl.ds(0, width), pl.ds(0, 4 * share)]
        grad_projected = wide.at[pl.ds(0, tokens), pl.ds(4 * share, 3 * share)]

        def unit_phase(block, projected, tables, mask):
            def loads(step, slot):
                unit = unit_of(step)
                return [
                    pltpu.make_async_copy(grad_all.at[unit], block.at[slot], local.at[slot]),
                    pltpu.make_async_copy(
                        projected_all.at[unit], projected.at[slot], local.at[2 + slot]
                    ),
                    pltpu.make_async_copy(cosine.at[unit], tables.at[slot, 0], local.at[4 + slot]),
                    pltpu.make_async_copy(sine.at[unit], tables.at[slot, 1], local.at[6 + slot]),
                    pltpu.make_async_copy(bias.at[unit], mask.at[slot], local.at[8 + slot]),
                ]

            def body(step, slot):
                given = dot(block[slot], att[:, 3 * share :]).astype(LOW)
                grads = attend_unit_back(
                    projected[slot], given, tables[slot, 0], tables[slot, 1], mask[slot], share
                )
                grad_projected[rows_at(unit_of(step), count), :] = grads
                terms.put(step, dot(grads, att[:, : 3 * share], CONTRACT_LAST).astype(LOW))

            whole = pltpu.make_async_copy(att_weights, att, local.at[10])
            whole.start()
            whole.wait()
            stream(TEAM, loads, body)

        pl.run_scoped(
            unit_phase,
            pltpu.VMEM((2, count, width), LOW),
            pltpu.VMEM((2, count, 3 * share), LOW),
            pltpu.VMEM((2, 2, count, HEAD_DIM), FULL),
            pltpu.VMEM((2, count, count), FULL),
        )

        def weight_phase(normed, grad, mixed, low):
            def loads(step, slot):
                at = rows_at(step, UNIT)
                return [
                    pltpu.make_async_copy(
                        normed_one_all.at[:, at], normed.at[slot], local.at[slot]
                    ),
                    pltpu.make_async_copy(
                        grad_all.at[:, :, at], grad.at[slot], local.at[2 + slot]
                    ),
                ]

            def stores(step, slot):
                at = rows_at(step, UNIT)
                return [pltpu.make_async_copy(low.at[slot], att_grad.at[at], local.at[4 + slot])]

            def body(step, slot):
                left = normed[slot]
                low[slot, :, : 3 * share] = dot(left, grad_projected[...], CONTRACT_FIRST).astype(LOW)
                left = grad[slot].reshape(tokens, UNIT)
                low[slot, :, 3 * share :] = dot(left, mixed[...], CONTRACT_FIRST).astype(LOW)

            whole = pltpu.make_async_copy(mixed_all, mixed, local.at[10])
            whole.start()
            whole.wait()
            stream_out(tiles, loads, stores, body)

        pl.run_scoped(
            weight_phase,
            pltpu.VMEM((2, tokens, UNIT), LOW),
            pltpu.VMEM((2, TEAM, count, UNIT), LOW),
            pltpu.VMEM((tokens, share), LOW),
            pltpu.VMEM((2, UNIT, 4 * share), LOW),
        )

    att_phase()
    for other in order:
        block_copy(2, other).start()
    own_copies.append(keep_own(att_grad, got_att, 2))

    def mate_at(low):
        mate = 0
        for bit in BITS:
            mine, its = (me // bit) % 2, (low // bit) % 2
            mate = mate + bit * (mine + its - 2 * mine * its)
        return mate

    def differ(chunk, parts, first_part, base):
        source = chunks[chunk][1]

        def low_at(step):
            turn = step // parts
            return 4 * (turn % 2) + 2 * ((turn // 2) % 2) + turn // 4

        def column(step):
            return rows_at((first_part + step % parts) * TEAM + mate_at(low_at(step)), hid)

        def near(step):
            at = column(step)
            return pltpu.make_async_copy(
                stage.at[step % 2], mlp_diff.at[:, at], kept.at[3 + step % 2]
            )

        def far(step):
            at = column(step)
            return pltpu.make_async_remote_copy(
                src_ref=mlp_diff.at[:, at],
                dst_ref=mlp_other.at[:, at],
                send_sem=sent_x.at[base + step],
                recv_sem=came_x.at[base + step],
                device_id={"rep": 1 - rep},
                device_id_type=MESH,
            )

        def arrive(step):
            low = low_at(step)

            @pl.when(step % parts == 0)
            def _():
                for top in range(tops):
                    index = chunk * (ranks - 1) + top * TEAM + low - 1

                    def wait():
                        pltpu.make_async_remote_copy(
                            src_ref=source.at[me],
                            dst_ref=source.at[me],
                            send_sem=sent_rows.at[index],
                            recv_sem=came_rows.at[index],
                            device_id={"dp": flip(me, 1)},
                            device_id_type=MESH,
                        ).wait_recv()

                    if top:
                        wait()
                    else:
                        pl.when(low > 0)(wait)
                        pl.when(low == 0)(own_copies[chunk].wait)

        def run(big, low):
            def loads(step, slot):
                at = column(step)
                mate = mate_at(low_at(step))
                part = rows_at(step % parts, hid)
                return [
                    pltpu.make_async_copy(mlp_master.at[:, at], big.at[slot, 0], local.at[slot]),
                    pltpu.make_async_copy(mlp_first.at[0, :, at], big.at[slot, 1], local.at[2 + slot]),
                    pltpu.make_async_copy(mlp_second.at[0, :, at], big.at[slot, 2], local.at[4 + slot]),
                ] + [
                    pltpu.make_async_copy(
                        source.at[top * TEAM + mate, :, part],
                        low.at[slot, top],
                        local.at[6 + slot + 2 * top],
                    )
                    for top in range(tops)
                ]

            def body(step, slot):
                @pl.loop(0, rows // STRIP)
                def _(strip):
                    at = pl.ds(strip * STRIP, STRIP)
                    grad = low[slot, 0, at].astype(FULL)
                    for top in range(1, tops):
                        grad = grad + low[slot, top, at].astype(FULL)
                    value = big[slot, 0, at]
                    inner, _, _ = adam_step(value, grad, big[slot, 1, at], big[slot, 2, at])
                    stage[slot, at] = (value - inner).astype(LOW)

                near(step).start()

                @pl.when(step > 0)
                def _():
                    near(step - 1).wait()
                    far(step - 1).start()

            steps = parts * TEAM
            stream(steps, loads, body, arrive)
            near(steps - 1).wait()
            far(steps - 1).start()

        pl.run_scoped(
            run, pltpu.VMEM((2, 3, rows, hid), FULL), pltpu.VMEM((2, tops, rows, hid), LOW)
        )

        def finish():
            @pl.loop(0, parts * TEAM)
            def _(step):
                far(step).wait()

        return finish

    waits = [differ(0, 1, 2, 0)]
    folds = [
        fold_steps(me, own, got, edge, terms.first(), send, split),
        fold_parts(me, fed_all, own_two, got_two, edge_two, send, local, split),
    ]
    for steps in folds:
        next(steps)
    waits.append(differ(1, 2, 0, TEAM))
    outs = []
    for steps, terms_now, folded in zip(folds, (own, own_two), (one_folded, two_folded)):
        for _ in steps:
            pass
        outs.append(
            pltpu.make_async_copy(
                terms_now.at[pl.ds(0, 3)], folded, local.at[len(outs)]
            )
        )
        outs[-1].start()
    for copy in outs:
        copy.wait()
    own_copies[2].wait()
    for other in order:
        block_copy(2, other).wait_recv()
    for chunk in range(3):
        for other in order:
            block_copy(chunk, other).wait_send()
    for wait in waits:
        wait()


GATE_FIRST, GATE_LATE, GATE_GATHER = 0, 1, 2


def backward_layer(ranks, tokens, mlp, *rest):
    resid, cot = tokens
    hidden_all, projected_all, gate_weights = rest[4], rest[9], rest[12]
    count, width = resid.shape
    all_tokens, hid = hidden_all.shape
    share = projected_all.shape[2] // 3
    rows = width // ranks
    vmem = pl.BlockSpec(memory_space=pltpu.VMEM)
    low = functools.partial(jax.ShapeDtypeStruct, dtype=LOW)
    out = [
        (jax.ShapeDtypeStruct((count, width), FULL), vmem),
        (low((3, count, width)), ANYWHERE),
        (low((3, count, width)), ANYWHERE),
        (low((ranks, rows, 4 * share)), ANYWHERE),
        (low((ranks, rows, 2 * hid)), ANYWHERE),
        (low((ranks, rows, hid)), ANYWHERE),
        (low(mlp[0].shape), ANYWHERE),
        (low(mlp[0].shape), ANYWHERE),
        (low((TEAM, count, width)), ANYWHERE),
        (low((width, 4 * share)), ANYWHERE),
        (low((width, 2 * hid)), ANYWHERE),
        (low((width, hid)), ANYWHERE),
        (low((TEAM, count, width)), ANYWHERE),
    ]
    team_copies = GATHER_COPIES + 2 * SUM_COPIES + SUM_COPIES + TEAM // 2
    locals_needed = 6 + 2 * (ranks // TEAM) * (hid // share) + 2
    sems = [team_copies] * 2 + [3 * (ranks - 1)] * 2
    return pl.pallas_call(
        functools.partial(backward_kernel, ranks),
        out_shape=[shape for shape, _ in out],
        in_specs=[vmem] * 2 + [ANYWHERE] * (len(rest) + 3),
        out_specs=[spec for _, spec in out],
        scratch_shapes=sum_scratch(count, width)
        + [pltpu.VMEM((TEAM // 2, count, width), LOW)]
        + sum_scratch(count, width)
        + [
            pltpu.VMEM((count, width), LOW),
            pltpu.VMEM((2, rows, hid), LOW),
            pltpu.VMEM((max(width, all_tokens), max(2 * hid, 7 * share)), LOW),
        ]
        + [pltpu.SemaphoreType.DMA((number,)) for number in sems]
        + [pltpu.SemaphoreType.DMA((2, TEAM // 2))] * 2
        + [pltpu.SemaphoreType.DMA((3 * TEAM,))] * 2
        + [
            pltpu.SemaphoreType.DMA((3 + TEAM,)),
            pltpu.SemaphoreType.DMA((max(locals_needed, 12),)),
        ],
        compiler_params=params(2),
        name="backward_layer",
    )(resid, cot, *rest, *mlp)


def pack_kernel(*refs):
    share = refs[0].shape[1]
    for p, ref in enumerate(refs[:-1]):
        refs[-1][0, :, p * share : (p + 1) * share] = ref[...].astype(LOW)


def pack_shares(master, bases, share):
    rows = master.shape[0]
    return pl.pallas_call(
        pack_kernel,
        grid=(TEAM,),
        out_shape=jax.ShapeDtypeStruct((TEAM, rows, len(bases) * share), LOW),
        in_specs=[
            pl.BlockSpec((rows, share), lambda i, base=base: (0, base + i)) for base in bases
        ],
        out_specs=pl.BlockSpec((1, rows, len(bases) * share), lambda i: (i, 0, 0)),
        name="pack_shares",
    )(*[master] * len(bases))


LANES = 1024


def finish_kernel(reps, share, grads, master, first, second, outer, diff, other, *refs):
    first_new, second_new, mean_out, new, outer_new = refs[-5:]
    for t in range(grads.shape[1]):
        at = slice(t * share, (t + 1) * share)
        grad = grads[0, t].astype(FULL)
        for top in range(1, grads.shape[0]):
            grad = grad + grads[top, t].astype(FULL)
        first_new[0, :, at] = BETA_ONE * first[0, :, at] + (1.0 - BETA_ONE) * grad
        second_new[0, :, at] = BETA_TWO * second[0, :, at] + (1.0 - BETA_TWO) * grad * grad
    mean = (diff[...].astype(FULL) + other[...].astype(FULL)) / reps
    mean_out[...] = mean
    new[...], outer_new[...] = outer_step(master[...], mean, outer[...])


def finish_chunk(reps, grads, master, first, second, outer, diff, other, bases, written):
    ranks, rows, columns = grads.shape
    parts = len(bases)
    share = columns // parts
    lanes = max(LANES, share)
    per = lanes // share
    steps = TEAM // per

    def column(p, t):
        place = bases[0]
        for q in range(1, parts):
            place = place + jnp.where(p >= q, bases[q] - bases[q - 1], 0)
        return place * steps + t

    grad = pl.BlockSpec((ranks // TEAM, per, rows, share), lambda p, t: (0, t, 0, p))
    wide = pl.BlockSpec((1, rows, lanes), lambda p, t: (0, 0, column(p, t)))
    flat = pl.BlockSpec((rows, lanes), lambda p, t: (0, column(p, t)))
    extra = [] if written is None else list(written)
    state = jax.ShapeDtypeStruct(first.shape, FULL)
    plain = jax.ShapeDtypeStruct(master.shape, FULL)
    return pl.pallas_call(
        functools.partial(finish_kernel, reps, share),
        grid=(parts, steps),
        out_shape=[state, state, plain, plain, plain],
        in_specs=[grad, flat, wide, wide, flat, flat, flat] + [ANYWHERE] * len(extra),
        out_specs=[wide, wide, flat, flat, flat],
        input_output_aliases={7 + i: i for i in range(len(extra))},
        compiler_params=pltpu.CompilerParams(vmem_limit_bytes=VMEM_BYTES),
        name="finish_chunk",
    )(
        grads.reshape(ranks // TEAM, TEAM, rows, columns),
        master, first, second, outer, diff, other, *extra,
    )


def adam_kernel(share, grad, master, first, second, *refs):
    first_new, second_new, diff = refs[-3:]
    for t in range(grad.shape[1]):
        at = slice(t * share, (t + 1) * share)
        gradient = grad[0, t].astype(FULL)
        for top in range(1, grad.shape[0]):
            gradient = gradient + grad[top, t].astype(FULL)
        inner, first_new[0, :, at], second_new[0, :, at] = adam_step(
            master[:, at], gradient, first[0, :, at], second[0, :, at]
        )
        diff[:, at] = (master[:, at] - inner).astype(LOW)


def chunk_specs(tops, rows, bases, share, lanes):
    per = lanes // share
    steps = TEAM // per
    parts = len(bases)

    def column(p, t):
        place = bases[0]
        for q in range(1, parts):
            place = place + jnp.where(p >= q, bases[q] - bases[q - 1], 0)
        return place * steps + t

    return (
        (parts, steps),
        pl.BlockSpec((tops, per, rows, share), lambda p, t: (0, t, 0, p)),
        pl.BlockSpec((1, rows, lanes), lambda p, t: (0, 0, column(p, t))),
        pl.BlockSpec((rows, lanes), lambda p, t: (0, column(p, t))),
        pl.BlockSpec((rows, lanes), lambda p, t: (0, p * steps + t)),
    )


def adam_chunk(grads, master, first, second, bases):
    ranks, rows, columns = grads.shape
    share = columns // len(bases)
    tops = ranks // TEAM
    grid, grad, wide, flat, packed = chunk_specs(tops, rows, bases, share, max(LANES, share))
    state = jax.ShapeDtypeStruct(first.shape, FULL)
    return pl.pallas_call(
        functools.partial(adam_kernel, share),
        grid=grid,
        out_shape=[
            state,
            state,
            jax.ShapeDtypeStruct((rows, TEAM * len(bases) * share), LOW),
        ],
        in_specs=[grad, flat, wide, wide],
        out_specs=[wide, wide, packed],
        compiler_params=pltpu.CompilerParams(vmem_limit_bytes=VMEM_BYTES),
        name="adam_chunk",
    )(grads.reshape(tops, TEAM, rows, columns), master, first, second)


def outer_kernel(reps, diff, other, master, momentum, *refs):
    mean_out, new, momentum_new = refs[-3:]
    mean = (diff[...].astype(FULL) + other[...].astype(FULL)) / reps
    mean_out[...] = mean
    new[...], momentum_new[...] = outer_step(master[...], mean, momentum[...])


def outer_chunk(reps, diff, other, master, momentum, bases):
    rows = master.shape[0]
    share = diff.shape[1] // (TEAM * len(bases))
    grid, _, _, flat, packed = chunk_specs(1, rows, bases, share, max(LANES, share))
    return pl.pallas_call(
        functools.partial(outer_kernel, reps),
        grid=grid,
        out_shape=[jax.ShapeDtypeStruct(master.shape, FULL)] * 3,
        in_specs=[packed, packed, flat, flat],
        out_specs=[flat] * 3,
        compiler_params=pltpu.CompilerParams(vmem_limit_bytes=VMEM_BYTES),
        name="outer_chunk",
    )(diff, other, master, momentum)


def on_device(
    reps,
    ranks,
    tokens,
    cotangent,
    branch,
    att_master,
    att_first,
    att_second,
    att_outer,
    mlp_master,
    mlp_first,
    mlp_second,
    mlp_outer,
):
    units, length, width = tokens.shape
    hidden_width = mlp_master.shape[1] // 3
    depth = HEAD_DIM
    count = units * length
    rows = att_master.shape[0]
    team = TEAM
    tops = ranks // team
    all_tokens = team * count
    att_share = width // team
    hid_share = hidden_width // team
    me = lax.axis_index("dp")
    rep = lax.axis_index("rep")
    top = me // team

    def hop(values, other):
        pairs = [(r * ranks + i, r * ranks + (i ^ other)) for r in range(reps) for i in range(ranks)]
        return lax.ppermute(values, ("rep", "dp"), pairs)

    def swap(values):
        pairs = [(r * ranks + i, (1 - r) * ranks + i) for r in range(reps) for i in range(ranks)]
        return lax.ppermute(values, ("rep", "dp"), pairs)

    flat_low = tokens.reshape(count, width)
    flat = flat_low.astype(FULL)
    cot = cotangent.reshape(count, width)
    seen_all = jnp.stack([branch if k == 0 else hop(branch, k) for k in range(team)])
    seen_all = seen_all.reshape(team * units, CONT)
    position, allowed = jax.vmap(lambda seen: token_layout(seen, length))(seen_all)
    cosine, sine = jax.vmap(lambda places: rotary_tables(places, depth))(position)
    bias = jnp.where(allowed, 0.0, -1e30).astype(FULL)
    wide_cosine = jnp.concatenate([cosine, cosine], axis=-1).reshape(team, count, depth)
    wide_sine = jnp.concatenate([-sine, sine], axis=-1).reshape(team, count, depth)
    att_pack = pack_shares(att_master, [0, team, 2 * team, 3 * team], att_share)
    (
        normed_one,
        grad_fed,
        att_low,
        gate_low,
        down_low,
        _,
        _,
        projected,
        mixed,
        resid,
        normed_two,
        gate_value,
        up_value,
        hidden,
    ) = forward_layer(
        ranks,
        flat_low,
        normalize(flat)[0].astype(LOW),
        cot,
        att_pack,
        mlp_master,
        wide_cosine,
        wide_sine,
        bias,
    )
    (
        grad_resid,
        one_folded,
        two_folded,
        got_att,
        got_gate,
        got_down,
        mlp_diff,
        mlp_other,
        *_,
    ) = backward_layer(
        ranks,
        (resid, cot),
        (mlp_master, mlp_first, mlp_second),
        wide_cosine,
        wide_sine,
        bias,
        grad_fed.reshape(all_tokens, width),
        hidden.reshape(all_tokens, hid_share),
        gate_value.reshape(all_tokens, hid_share),
        up_value.reshape(all_tokens, hid_share),
        normed_two.reshape(all_tokens, width),
        normed_one.reshape(all_tokens, width),
        projected,
        mixed.reshape(all_tokens, att_share),
        att_low,
        gate_low,
        down_low,
    )
    def unfold(folded):
        terms = (folded[0], hop(folded[1], 2), hop(folded[2], 4))
        return sum(term.astype(FULL) for term in terms)

    grad_normed_one, fed = unfold(one_folded), unfold(two_folded)
    grad_tokens = grad_resid + normalize_back(flat, grad_normed_one)
    out_tokens = (resid + fed).astype(LOW)
    mlp = (mlp_master, mlp_first, mlp_second, mlp_outer, mlp_diff, mlp_other)
    bases = [0, 1, 2, 3]
    *att_state, att_diff = adam_chunk(got_att, att_master, att_first, att_second, bases)
    mlp_out = finish_chunk(reps, got_down, *mlp, [2], None)
    mlp_out = finish_chunk(reps, got_gate, *mlp, [0, 1], mlp_out)
    att_new = outer_chunk(reps, att_diff, swap(att_diff), att_master, att_outer, bases)
    return (
        out_tokens.reshape(units, length, width),
        grad_tokens.reshape(units, length, width),
        *(att_new[1], *att_state, att_new[0], att_new[2]),
        *(mlp_out[3], mlp_out[0], mlp_out[1], mlp_out[2], mlp_out[4]),
    )


def solution(mesh):
    in_specs = (
        P(("rep", "dp"), None, None),
        P(("rep", "dp"), None, None),
        P(("rep", "dp"), None),
        P("dp", None),
        P("rep", "dp", None),
        P("rep", "dp", None),
        P("dp", None),
        P("dp", None),
        P("rep", "dp", None),
        P("rep", "dp", None),
        P("dp", None),
    )
    out_specs = (
        P(("rep", "dp"), None, None),
        P(("rep", "dp"), None, None),
        P("dp", None),
        P("rep", "dp", None),
        P("rep", "dp", None),
        P("dp", None),
        P("dp", None),
        P("dp", None),
        P("rep", "dp", None),
        P("rep", "dp", None),
        P("dp", None),
        P("dp", None),
    )

    def body(*args):
        return on_device(mesh.shape["rep"], mesh.shape["dp"], *args)

    return jax.shard_map(
        body, mesh=mesh, in_specs=in_specs, out_specs=out_specs, check_vma=False
    )
```
